32 devices in a mesh: dp: 16 (over z, y, x), group: 2 (over core).
Axes of the slice: x: 2, y: 2, z: 4, core: 2. Of those that a mesh axis runs over, the one named last changes fastest.
Arguments:
- samples: bfloat16 [32, 2048, 512], P(('dp', 'group')), may hold values from -6 to 6
- mel: bfloat16 [32, 11, 80], P(('dp', 'group')), may hold values from -6 to 6
- lengths: int32 [32], P(('dp', 'group')), may hold values from 1024 to 2048, as said below
- hops: int32 [32], P(('dp', 'group')), may hold values from 200 to 300, as said below
- conv_weight: bfloat16 [2, 1024, 1024], P(None, None, ('dp', 'group')), may hold values from -0.1875 to 0.1875
- cond_weight: bfloat16 [2, 80, 1024], P(None, None, ('dp', 'group')), may hold values from -0.625 to 0.625
- conv_bias: bfloat16 [2, 1024], P(None, ('dp', 'group')), may hold values from -3 to 3
- out_weight: bfloat16 [2, 512, 1024], P(None, None, ('dp', 'group')), may hold values from -0.75 to 0.75
- out_bias: bfloat16 [2, 1024], P(None, ('dp', 'group')), may hold values from -3 to 3
- grad_out: bfloat16 [32, 2048, 512], P(('dp', 'group')), may hold values from -6 to 6
- grad_skip: bfloat16 [32, 2048, 512], P(('dp', 'group')), may hold values from -6 to 6
Outputs:
- residual_out: bfloat16 [32, 2048, 512], P(('dp', 'group'))
- skip_output_sum: bfloat16 [32, 2048, 512], P(('dp', 'group'))
- samples_grad: float32 [32, 2048, 512], P(('dp', 'group'))
- mel_grad: float32 [32, 11, 80], P(('dp', 'group'))
- conv_weight_grad: float32 [2, 1024, 1024], P(None, None, ('dp', 'group'))
- cond_weight_grad: float32 [2, 80, 1024], P(None, None, ('dp', 'group'))
- conv_bias_grad: float32 [2, 1024], P(None, ('dp', 'group'))
- out_weight_grad: float32 [2, 512, 1024], P(None, None, ('dp', 'group'))
- out_bias_grad: float32 [2, 1024], P(None, ('dp', 'group'))
The draws below stay inside these ranges and needn't reach their ends.
Inputs may be any that keep to these rules, and one draw needn't show every extreme that they name: `lengths`: every clip uses at least 1024 samples, and some clip uses all 2048. `hops`: each clip's value is 200 or 300, both occur.
All inputs are finite; a program needn't handle non-finite values.
Results may differ from the reference program's by a relative error of at most 0.0074.
Values may be sent and summed in bfloat16 or wider, within the bound.
No kernel may reach another device: no remote copies, remote signals or barrier semaphores. Data moves between devices by JAX's collectives and lax.ppermute only.
A program may use at most 192 MiB of HBM per device.

```python
import jax
import jax.numpy as jnp
from jax import lax

R = 512
MEL = 80
L = 2048
LAYERS = 2
FIRST_DILATION = 512
HOP_A = 200
HOP_B = 300
CLIPS = 32
MELF = 11


def draw_lengths(key, part):
    key = jax.random.fold_in(key, 11)
    first_key, second_random_key = jax.random.split(key)
    values = jax.random.randint(first_key, (CLIPS,), L // 2, L + 1)
    chosen = jax.random.randint(second_random_key, (), 0, CLIPS)
    return jnp.where(jnp.arange(CLIPS) == chosen, L, values).astype(jnp.int32)


def draw_hops(key, part):
    key = jax.random.fold_in(key, 23)
    first_key, second_random_key = jax.random.split(key)
    picks = jax.random.randint(first_key, (CLIPS,), 0, 2)
    chosen = jax.random.randint(second_random_key, (), 0, CLIPS)
    places = jnp.arange(CLIPS)
    picks = jnp.where(places == chosen, 0, picks)
    picks = jnp.where(places == (chosen + 1) % CLIPS, 1, picks)
    return jnp.where(picks == 0, HOP_A, HOP_B).astype(jnp.int32)


def steps_of(stream_key, shape, cuts, smallest, top_value):
    gain = 1.0
    for position, blocks in cuts:
        heights = jax.random.uniform(jax.random.fold_in(jax.random.fold_in(stream_key, 6), position), (blocks,), jnp.float32, smallest / len(cuts), top_value / len(cuts))
        gain = gain * jnp.repeat(jnp.exp(heights), shape[position] // blocks).reshape((-1,) + (1,) * (len(shape) - 1 - position))
    return gain


def gaussian(own_key, extent, spread, limit, cuts=(), held_as=jnp.bfloat16):
    values = spread * jax.random.normal(own_key, extent, jnp.float32)
    if cuts:
        values = values * steps_of(own_key, extent, cuts, -0.22, 0.18)
    return jnp.clip(values, -limit, limit).astype(held_as)


def setup_inputs(seed: int = 0) -> dict:
    splits = jax.random.split(jax.random.key(seed), 12)
    samples = gaussian(splits[0], (CLIPS, L, R), 1.0, 6.0, ((0, 32),))
    mel = gaussian(splits[1], (CLIPS, MELF, MEL), 1.0, 6.0, ((0, 32),))
    lengths = draw_lengths(jax.random.fold_in(splits[11], 71), 0)
    hops = draw_hops(jax.random.fold_in(splits[11], 71), 0)
    conv_weight = gaussian(splits[4], (LAYERS, 2 * R, 2 * R), (2 * R) ** -0.5, 0.1875, ((2, 32),))
    cond_weight = gaussian(splits[5], (LAYERS, MEL, 2 * R), MEL ** -0.5, 0.625, ((2, 32),))
    conv_bias = gaussian(splits[6], (LAYERS, 2 * R), 0.5, 3.0, ((1, 32),))
    out_weight = gaussian(splits[7], (LAYERS, R, 2 * R), (R // 8) ** -0.5, 0.75, ((2, 32),))
    out_bias = gaussian(splits[8], (LAYERS, 2 * R), 0.5, 3.0, ((1, 32),))
    grad_out = gaussian(splits[9], (CLIPS, L, R), 1.0, 6.0, ((0, 32),))
    grad_skip = gaussian(splits[10], (CLIPS, L, R), 1.0, 6.0, ((0, 32),))
    return {"samples": samples, "mel": mel, "lengths": lengths, "hops": hops, "conv_weight": conv_weight, "cond_weight": cond_weight, "conv_bias": conv_bias, "out_weight": out_weight, "out_bias": out_bias, "grad_out": grad_out, "grad_skip": grad_skip}


@jax.custom_vjp
def low(v):
    return lax.optimization_barrier(v.astype(jnp.bfloat16)).astype(jnp.float32)

@jax.custom_vjp
def low_back(v):
    return v

def low_keep(v):
    return (low(v), None)

def low_pass(kept, grad):
    return (grad,)

def back_keep(v):
    return (v, None)

def back_low(kept, grad):
    return (low(grad),)
low.defvjp(low_keep, low_pass)
low_back.defvjp(back_keep, back_low)

def product(left, right):
    return jnp.dot(left, right, precision=lax.Precision.HIGHEST, preferred_element_type=jnp.float32)

def clip_forward(parameters, samples_clip, mel_clip, length, hop):
    conv_w, cond_w, conv_b, out_w, out_b = parameters
    positions = jnp.arange(L, dtype=jnp.int32)
    pad_mask = (positions < length).astype(jnp.float32)[:, None]
    frame_table = ((positions // hop)[:, None] == jnp.arange(MELF, dtype=jnp.int32)[None, :]).astype(jnp.float32)
    conditioning = product(frame_table, mel_clip)
    hidden = samples_clip * pad_mask
    skip_total = jnp.zeros((L, R), jnp.float32)
    for layer_position in range(LAYERS):
        dilation_factor = FIRST_DILATION if layer_position == 0 else 1
        hidden_low = low(hidden)
        shifted = jnp.pad(hidden_low[:L - dilation_factor], ((dilation_factor, 0), (0, 0)))
        preact = product(shifted, conv_w[layer_position][:R]) + product(hidden_low, conv_w[layer_position][R:])
        preact = preact + product(conditioning, cond_w[layer_position]) + conv_b[layer_position]
        preact = low_back(preact)
        gated = low(jnp.tanh(preact[:, :R]) * jax.nn.sigmoid(preact[:, R:]))
        projected = low_back(product(gated, out_w[layer_position]) + out_b[layer_position])
        hidden = (hidden + projected[:, :R]) * pad_mask
        skip_total = skip_total + projected[:, R:] * pad_mask
    return (hidden, skip_total)

def add_up(total, extra):
    return total + extra

def reference(samples, mel, lengths, hops, conv_weight, cond_weight, conv_bias, out_weight, out_bias, grad_out, grad_skip):
    parameters = tuple((item.astype(jnp.float32) for item in (conv_weight, cond_weight, conv_bias, out_weight, out_bias)))

    def one_clip(grad_totals, clip_items):
        samples_clip, mel_clip, length, hop, out_cot, skip_cot = clip_items

        def forward_fn(param_tuple, samples_in, mel_in):
            return clip_forward(param_tuple, samples_in, mel_in, length, hop)
        results, pullback = jax.vjp(forward_fn, parameters, samples_clip.astype(jnp.float32), mel_clip.astype(jnp.float32))
        grad_params, grad_samples, grad_mel = pullback((out_cot.astype(jnp.float32), skip_cot.astype(jnp.float32)))
        grad_totals = jax.tree.map(add_up, grad_totals, grad_params)
        return (grad_totals, (results[0].astype(jnp.bfloat16), results[1].astype(jnp.bfloat16), grad_samples, grad_mel))
    start_totals = jax.tree.map(jnp.zeros_like, parameters)
    grad_totals, stacked = lax.scan(one_clip, start_totals, (samples, mel, lengths, hops, grad_out, grad_skip))
    residual_out, skip_output_sum, samples_grad, mel_grad = stacked
    return (residual_out, skip_output_sum, samples_grad, mel_grad, grad_totals[0], grad_totals[1], grad_totals[2], grad_totals[3], grad_totals[4])
```

```python
import jax
import jax.numpy as jnp
from jax import lax
from jax.sharding import PartitionSpec as P

FIRST_DILATION = 512
AXES = ("dp", "group")
LANES = 128


def contract_rows(left, right):
    return lax.dot_general(
        left, right, (((0,), (0,)), ((), ())), preferred_element_type=jnp.float32
    )


def contract_cols(left, right):
    return lax.dot_general(
        left, right, (((1,), (1,)), ((), ())), preferred_element_type=jnp.float32
    )


class Wires:
    def __init__(self, dp, cores):
        assert dp % 4 == 0 and cores == 2
        self.rest = dp // 4
        self.devices = dp * 2
        me = lax.axis_index(AXES)
        self.core = me % 2
        self.a = (me // 2) % 2
        self.b = (me // 4) % 2
        self.alone = jnp.where(self.core == 0, self.a, self.b)
        self.core_pairs = [(i, i ^ 1) for i in range(self.devices)]
        self.alone_pairs = [(i, i ^ (2 if i % 2 == 0 else 4)) for i in range(self.devices)]
        groups = []
        for core in range(2):
            for fixed in range(2):
                members = []
                for rest in range(self.rest):
                    for varied in range(2):
                        b, a = (varied, fixed) if core == 0 else (fixed, varied)
                        members.append(((rest * 2 + b) * 2 + a) * 2 + core)
                groups.append(members)
        self.groups = groups

    def spread(self, blocks):
        return lax.all_to_all(blocks, AXES, 0, 0, tiled=True, axis_index_groups=self.groups)

    def gather(self, block):
        rows, depth = block.shape
        count = self.rest * 2
        mine = self.spread(jnp.broadcast_to(block[None], (count, rows, depth)))
        other = lax.ppermute(mine, AXES, self.alone_pairs)
        low = jnp.where(self.alone == 0, mine, other)
        high = jnp.where(self.alone == 0, other, mine)
        half = jnp.stack([low, high]).reshape(2, self.rest, 2, rows, depth)
        passed = lax.ppermute(half, AXES, self.core_pairs)
        first = jnp.where(self.core == 0, half, passed)
        second = jnp.where(self.core == 0, passed, half)
        whole = jnp.stack(
            [first.transpose(1, 2, 0, 3, 4), second.transpose(1, 0, 2, 3, 4)], axis=3
        )
        return whole.reshape(self.devices * rows, depth)

    def scatter_sum(self, full):
        depth = full.shape[1]
        rows = full.shape[0] // self.devices
        blocks = full.reshape(self.rest, 4, 2, rows, depth)
        away = lax.dynamic_index_in_dim(blocks, 1 - self.core, 2, keepdims=False)
        here = lax.dynamic_index_in_dim(blocks, self.core, 2, keepdims=False)
        came = lax.ppermute(away.astype(jnp.bfloat16), AXES, self.core_pairs)
        chip = here + came.astype(jnp.float32)

        def pick(side):
            places = [
                jnp.where(self.core == 0, step * 2 + side, side * 2 + step) for step in range(2)
            ]
            return jnp.stack(
                [lax.dynamic_index_in_dim(chip, place, 1, keepdims=False) for place in places],
                axis=1,
            )

        came = lax.ppermute(pick(1 - self.alone).astype(jnp.bfloat16), AXES, self.alone_pairs)
        pair = pick(self.alone) + came.astype(jnp.float32)
        parts = self.spread(pair.astype(jnp.bfloat16).reshape(self.rest * 2, rows, depth))
        return jnp.sum(parts.astype(jnp.float32), axis=0)


def layer_forward(hidden, conditioning, pad_mask, weights, dilation_factor):
    conv_t, cond_t, conv_b, out_t, out_b = weights
    channels = hidden.shape[1]
    sample_count = hidden.shape[0]
    hidden_low = hidden.astype(jnp.bfloat16)
    shifted = jnp.pad(hidden_low[: sample_count - dilation_factor], ((dilation_factor, 0), (0, 0)))
    taps = jnp.concatenate([shifted, hidden_low, conditioning], axis=1)
    preact = contract_cols(taps, jnp.concatenate([conv_t, cond_t], axis=1)) + conv_b
    tangent = jnp.tanh(preact[:, :channels])
    sig_gate = jax.nn.sigmoid(preact[:, channels:])
    gated_out = (tangent * sig_gate).astype(jnp.bfloat16)
    projected = contract_cols(gated_out, out_t) + out_b
    hidden_next = (hidden + projected[:, :channels]) * pad_mask
    skip_part = projected[:, channels:] * pad_mask
    return (hidden_next, skip_part, (hidden_low, shifted, tangent, sig_gate, gated_out))


def per_device(
    dp,
    cores,
    samples,
    mel,
    lengths,
    hops,
    conv_weight,
    cond_weight,
    conv_bias,
    out_weight,
    out_bias,
    grad_out,
    grad_skip,
):
    wires = Wires(dp, cores)
    sample_count, channels = samples.shape[1:]
    frame_count, mel_count = mel.shape[1:]
    number_of_layers = conv_weight.shape[0]
    conv_depth = conv_weight.shape[1]
    out_depth = out_weight.shape[1]
    positions = jnp.arange(sample_count, dtype=jnp.int32)
    pad_mask = (positions < lengths[0]).astype(jnp.float32)[:, None]
    frame_table = (
        (positions // hops[0])[:, None] == jnp.arange(frame_count, dtype=jnp.int32)[None, :]
    ).astype(jnp.bfloat16)
    conditioning = jnp.dot(
        frame_table, mel[0], preferred_element_type=jnp.float32
    ).astype(jnp.bfloat16)

    loaded = []
    for layer in range(number_of_layers):
        fill = -(mel_count + 2) % LANES
        conv_pack = jnp.concatenate(
            [
                conv_weight[layer],
                cond_weight[layer],
                conv_bias[layer][None],
                out_bias[layer][None],
                jnp.zeros((fill, conv_weight.shape[2]), jnp.bfloat16),
            ],
            axis=0,
        ).T
        conv_full = wires.gather(conv_pack)
        out_t = wires.gather(out_weight[layer].T)
        at = conv_depth + mel_count
        loaded.append(
            (
                conv_full[:, :conv_depth],
                conv_full[:, conv_depth:at],
                conv_full[:, at].astype(jnp.float32),
                out_t,
                conv_full[:, at + 1].astype(jnp.float32),
            )
        )

    hidden = samples[0].astype(jnp.float32) * pad_mask
    skip_total = jnp.zeros(hidden.shape, jnp.float32)
    saved = []
    for layer in range(number_of_layers):
        dilation = FIRST_DILATION if layer == 0 else 1
        hidden, skip_part, kept = layer_forward(
            hidden, conditioning, pad_mask, loaded[layer], dilation
        )
        skip_total = skip_total + skip_part
        saved.append(kept)
    residual_out = hidden.astype(jnp.bfloat16)[None]
    skip_output_sum = skip_total.astype(jnp.bfloat16)[None]

    grad_hidden = grad_out[0].astype(jnp.float32)
    skip_cot = grad_skip[0].astype(jnp.float32) * pad_mask
    mel_grad = jnp.zeros((frame_count, mel_count), jnp.float32)
    owned = [None] * number_of_layers
    exact = dict(precision=lax.Precision.HIGHEST, preferred_element_type=jnp.float32)
    for layer in reversed(range(number_of_layers)):
        dilation = FIRST_DILATION if layer == 0 else 1
        conv_t, cond_t, conv_b, out_t, out_b = loaded[layer]
        hidden_low, shifted, tangent, sig_gate, gated_out = saved[layer]
        masked = grad_hidden * pad_mask
        grad_proj = jnp.concatenate([masked, skip_cot], axis=1).astype(jnp.bfloat16)
        out_grad = contract_rows(grad_proj, gated_out)
        out_b_grad = jnp.sum(grad_proj, axis=0, dtype=jnp.float32)
        out_own = wires.scatter_sum(out_grad)
        grad_gated = jnp.dot(grad_proj, out_t, preferred_element_type=jnp.float32)
        grad_pre = jnp.concatenate(
            [
                grad_gated * sig_gate * (1.0 - tangent * tangent),
                grad_gated * tangent * sig_gate * (1.0 - sig_gate),
            ],
            axis=1,
        ).astype(jnp.bfloat16)
        conv_grad = contract_rows(grad_pre, jnp.concatenate([shifted, hidden_low], axis=1))
        frame_sums = contract_rows(grad_pre, frame_table)
        cond_grad = lax.dot_general(
            frame_sums, mel[0].astype(jnp.float32), (((1,), (0,)), ((), ())), **exact
        )
        mel_grad = mel_grad + lax.dot_general(
            frame_sums, cond_t.astype(jnp.float32), (((0,), (0,)), ((), ())), **exact
        )
        fill = jnp.zeros((conv_grad.shape[0], -(mel_count + 2) % LANES), jnp.float32)
        conv_own = wires.scatter_sum(
            jnp.concatenate(
                [
                    conv_grad,
                    cond_grad,
                    jnp.sum(frame_sums, axis=1, keepdims=True),
                    out_b_grad[:, None],
                    fill,
                ],
                axis=1,
            )
        )
        grad_stack = jnp.dot(grad_pre, conv_t, preferred_element_type=jnp.float32)
        moved = jnp.pad(grad_stack[dilation:, :channels], ((0, dilation), (0, 0)))
        grad_hidden = masked + grad_stack[:, channels:] + moved
        at = conv_depth + mel_count
        owned[layer] = (
            conv_own[:, :conv_depth].T,
            conv_own[:, conv_depth:at].T,
            conv_own[:, at],
            out_own.T,
            conv_own[:, at + 1],
        )
    samples_grad = (grad_hidden * pad_mask)[None]
    owned = [jnp.stack([part[member] for part in owned], axis=0) for member in range(5)]
    return (residual_out, skip_output_sum, samples_grad, mel_grad[None], *owned)


def solution(mesh):
    dp, cores = mesh.shape["dp"], mesh.shape["group"]

    def whole(*arrays):
        return per_device(dp, cores, *arrays)

    clips = P(AXES, None, None)
    columns = P(None, None, AXES)
    biases = P(None, AXES)
    return jax.shard_map(
        whole,
        mesh=mesh,
        in_specs=(
            clips, clips, P(AXES), P(AXES), columns, columns, biases, columns, biases, clips, clips,
        ),
        out_specs=(clips, clips, clips, clips, columns, columns, biases, columns, biases),
        check_vma=False,
    )
```

```python
import functools

import jax
import jax.numpy as jnp
from jax import lax
from jax.experimental import pallas as pl
from jax.experimental.pallas import tpu as pltpu
from jax.sharding import PartitionSpec as P

FIRST_DILATION = 512
AXES = ("dp", "group")
LANES = 128
TILE = 512
VMEM = 56 * 1024 * 1024
LOW = jnp.bfloat16
FULL = jnp.float32


def dot(left, right):
    return jnp.dot(left, right, preferred_element_type=FULL)


def dot_cols(left, right, **more):
    return lax.dot_general(
        left, right, (((1,), (1,)), ((), ())), preferred_element_type=FULL, **more
    )


def dot_rows(left, right, **more):
    return lax.dot_general(
        left, right, (((0,), (0,)), ((), ())), preferred_element_type=FULL, **more
    )


class Sizes:
    def __init__(self, channels, mel_count):
        self.channels = channels
        self.mel = mel_count
        self.taps = 2 * channels
        self.extra = -(-(mel_count + 2) // LANES) * LANES
        self.conv = self.taps + self.extra
        self.pack = self.conv + channels


def mask_of(info_ref, start, rows):
    places = start + lax.broadcasted_iota(jnp.int32, (rows, 1), 0)
    return (places < info_ref[0]).astype(FULL)


def frames_of(info_ref, start, rows):
    places = start + lax.broadcasted_iota(jnp.int32, (rows, LANES), 0)
    first = lax.broadcasted_iota(jnp.int32, (rows, LANES), 1) * info_ref[1]
    return ((places >= first) & (places < first + info_ref[1])).astype(FULL).astype(LOW)


def out_bias_row(size, w_ref, rows):
    column = lax.broadcasted_iota(jnp.int32, (8, size.extra), 1)
    pick = (column == size.mel + 1).astype(FULL).astype(LOW)
    return dot_cols(pick, w_ref[rows, size.taps : size.conv])[0:1]


def gates(taps, w_ref, size, side):
    channels = size.channels
    width = channels // 2
    low = slice(side * width, (side + 1) * width)
    high = slice(channels + side * width, channels + (side + 1) * width)
    tangent = jnp.tanh(dot_cols(taps, w_ref[low, : size.conv]))
    sig_gate = 0.5 * jnp.tanh(0.5 * dot_cols(taps, w_ref[high, : size.conv])) + 0.5
    gated = tangent * sig_gate
    return low, high, gated, sig_gate * (1.0 - tangent * tangent), gated * (1.0 - sig_gate)


def forward_0(size, info_ref, prev_ref, x_ref, w_ref, mel_ref, low0_ref, h1_ref, low1_ref, gated_ref, slope_ref):
    step = pl.program_id(0)
    rows, channels = x_ref.shape
    mask = mask_of(info_ref, step * rows, rows)
    hidden = x_ref[...].astype(FULL) * mask
    low = hidden.astype(LOW)
    low0_ref[...] = low
    prev_mask = mask_of(info_ref, (step - 1) * rows, rows) * (step > 0).astype(FULL)
    prev = (prev_ref[...].astype(FULL) * prev_mask).astype(LOW)
    cond = dot(frames_of(info_ref, step * rows, rows), mel_ref[...]).astype(LOW)
    taps = jnp.concatenate([prev, low, cond], axis=1)
    for side in range(2):
        first, second, gated, slope_a, slope_b = gates(taps, w_ref, size, side)
        gated_ref[:, first] = gated.astype(LOW)
        slope_ref[:, first] = slope_a.astype(LOW)
        slope_ref[:, second] = slope_b.astype(LOW)
    moved = dot_cols(gated_ref[...], w_ref[:channels, size.conv :])
    moved = moved + out_bias_row(size, w_ref, slice(0, channels))
    hidden = (hidden + moved) * mask
    h1_ref[...] = hidden
    low1_ref[...] = hidden.astype(LOW)


def forward_1(size, info_ref, low1_ref, w_ref, mel_ref, go_ref, gs_ref, prev_ref, gated_ref, pre_ref, proj_ref, carry_ref):
    step = pl.program_id(0)
    rows, channels = low1_ref.shape
    mask = mask_of(info_ref, step * rows, rows)
    low = low1_ref[...]
    wide = low.astype(FULL)

    @pl.when(step == 0)
    def _():
        carry_ref[...] = jnp.zeros_like(carry_ref)

    place = lax.broadcasted_iota(jnp.int32, (rows, 1), 0)
    prev = jnp.where(place == 0, carry_ref[7:8], pltpu.roll(wide, 1, 0)).astype(LOW)
    carry_ref[...] = wide[rows - 8 :]
    prev_ref[...] = prev
    cond = dot(frames_of(info_ref, step * rows, rows), mel_ref[...]).astype(LOW)
    taps = jnp.concatenate([prev, low, cond], axis=1)
    proj_ref[:, :channels] = (go_ref[...].astype(FULL) * mask).astype(LOW)
    proj_ref[:, channels:] = (gs_ref[...].astype(FULL) * mask).astype(LOW)
    grad_gated = dot(proj_ref[...], w_ref[:, size.conv :])
    for side in range(2):
        first, second, gated, slope_a, slope_b = gates(taps, w_ref, size, side)
        gated_ref[:, first] = gated.astype(LOW)
        pre_ref[:, first] = (grad_gated[:, first] * slope_a).astype(LOW)
        pre_ref[:, second] = (grad_gated[:, first] * slope_b).astype(LOW)


def weight_grads(size, shift, info_ref, pre_ref, proj_ref, low_ref, prev_ref, gated_ref, mel_ref, wc_ref, out_ref, melg_ref, frames_ref):
    step = pl.program_id(0)
    samples = low_ref.shape[0]

    @pl.when(step == 0)
    def _():
        frames_ref[...] = frames_of(info_ref, 0, samples)
        melg_ref[...] = jnp.zeros_like(melg_ref)

    pre = pre_ref[...]
    if shift % TILE == 0:
        early = dot_rows(pre[shift:], low_ref[: samples - shift])
    else:
        early = dot_rows(pre, prev_ref[...])
    out_ref[:, : size.channels] = early.astype(LOW)
    out_ref[:, size.channels : size.taps] = dot_rows(pre, low_ref[...]).astype(LOW)
    sums = dot_rows(pre, frames_ref[...])
    exact = dict(precision=lax.Precision.HIGHEST)
    extra = jnp.dot(sums, mel_ref[...].astype(FULL), preferred_element_type=FULL, **exact)
    melg_ref[...] += dot_rows(sums, wc_ref[...].astype(FULL), **exact)
    proj = proj_ref[...]
    bias = jnp.sum(dot_rows(proj, frames_ref[...]), axis=1, keepdims=True)
    column = lax.broadcasted_iota(jnp.int32, extra.shape, 1)
    extra = jnp.where(column == size.mel + 1, bias, extra)
    out_ref[:, size.taps : size.conv] = extra.astype(LOW)
    out_ref[:, size.conv :] = dot_rows(proj, gated_ref[...]).astype(LOW)


def backward_0(size, info_ref, pre1_ref, w1_ref, w0_ref, go_ref, gs_ref, slope_ref, gh_ref, proj_ref, pre0_ref, carry_ref):
    step = pl.program_id(0)
    rows, channels = go_ref.shape
    tile = pl.num_programs(0) - 1 - step
    mask = mask_of(info_ref, tile * rows, rows)

    @pl.when(step == 0)
    def _():
        carry_ref[...] = jnp.zeros_like(carry_ref)

    pre1 = pre1_ref[...]
    early = dot(pre1, w1_ref[:, :channels])
    place = lax.broadcasted_iota(jnp.int32, (rows, 1), 0)
    later = jnp.where(place == rows - 1, carry_ref[0:1], pltpu.roll(early, rows - 1, 0))
    carry_ref[...] = early[:8]
    now = dot(pre1, w1_ref[:, channels : size.taps])
    grad = (go_ref[...].astype(FULL) * mask + now + later) * mask
    gh_ref[...] = grad
    proj_ref[:, :channels] = grad.astype(LOW)
    proj_ref[:, channels:] = (gs_ref[...].astype(FULL) * mask).astype(LOW)
    grad_gated = dot(proj_ref[...], w0_ref[:, size.conv :])
    pre0_ref[:, :channels] = (grad_gated * slope_ref[:, :channels].astype(FULL)).astype(LOW)
    pre0_ref[:, channels:] = (grad_gated * slope_ref[:, channels:].astype(FULL)).astype(LOW)


def outputs(size, info_ref, gh_ref, pre_ref, next_ref, w0_ref, w1_ref, h1_ref, gated0_ref, gated1_ref, res_ref, skip_ref, sg_ref):
    step = pl.program_id(0)
    rows, channels = gh_ref.shape
    mask = mask_of(info_ref, step * rows, rows)
    grad = gh_ref[...] + dot(pre_ref[...], w0_ref[:, channels : size.taps])
    later = dot(next_ref[...], w0_ref[:, :channels])
    grad = grad + jnp.where(step < pl.num_programs(0) - 1, later, 0.0)
    sg_ref[...] = grad * mask
    gated1 = gated1_ref[...]
    res = dot_cols(gated1, w1_ref[:channels, size.conv :])
    res = res + out_bias_row(size, w1_ref, slice(0, channels))
    res_ref[...] = ((h1_ref[...] + res) * mask).astype(LOW)
    late = slice(channels, 2 * channels)
    skip = dot_cols(gated0_ref[...], w0_ref[late, size.conv :])
    skip = skip + dot_cols(gated1, w1_ref[late, size.conv :])
    skip = skip + out_bias_row(size, w0_ref, late) + out_bias_row(size, w1_ref, late)
    skip_ref[...] = (skip * mask).astype(LOW)


def call(kernel, grid, info, operands, specs, outs, out_specs, scratch, flops):
    moved = sum(x.size * x.dtype.itemsize for x in operands)
    moved += sum(x.size * x.dtype.itemsize for x in outs)
    return pl.pallas_call(
        kernel,
        grid_spec=pltpu.PrefetchScalarGridSpec(
            num_scalar_prefetch=1,
            grid=(grid,),
            in_specs=specs,
            out_specs=out_specs,
            scratch_shapes=scratch,
        ),
        out_shape=outs,
        compiler_params=pltpu.CompilerParams(
            vmem_limit_bytes=VMEM, dimension_semantics=("arbitrary",)
        ),
        cost_estimate=pl.CostEstimate(flops=flops, bytes_accessed=moved, transcendentals=0),
    )(info, *operands)


def shape_of(*shape, dtype=LOW):
    return jax.ShapeDtypeStruct(shape, dtype)


def tiled(width, place=lambda i: i):
    return pl.BlockSpec((TILE, width), lambda i, info: (place(i), 0))


def fixed(*shape):
    return pl.BlockSpec(shape, lambda i, info: (0,) * len(shape))


def put_together(rows, core_ref, *refs):
    pieces, out_ref, sems = refs[:4], refs[4], refs[5]
    core, a, b = core_ref[0], core_ref[1], core_ref[2]
    copies = []
    for index, piece in enumerate(pieces):
        source = core if index < 2 else 1 - core
        alone = jnp.where(source == 0, a, b)
        alone = alone if index % 2 == 0 else 1 - alone
        for block in range(piece.shape[0]):
            rest, varied = block // 2, block % 2
            at_b = jnp.where(source == 0, varied, alone)
            at_a = jnp.where(source == 0, alone, varied)
            place = ((rest * 2 + at_b) * 2 + at_a) * 2 + source
            copies.append(
                pltpu.make_async_copy(
                    piece.at[block],
                    out_ref.at[pl.ds(pl.multiple_of(place * rows, rows), rows)],
                    sems.at[index, block],
                )
            )
    for copy in copies:
        copy.start()
    for copy in copies:
        copy.wait()


class Wires:
    def __init__(self, dp, cores):
        assert dp % 4 == 0 and cores == 2
        self.rest = dp // 4
        self.devices = dp * 2
        me = lax.axis_index(AXES)
        self.core = me % 2
        self.a = (me // 2) % 2
        self.b = (me // 4) % 2
        self.alone = jnp.where(self.core == 0, self.a, self.b)
        self.core_pairs = [(i, i ^ 1) for i in range(self.devices)]
        self.alone_pairs = [(i, i ^ (2 if i % 2 == 0 else 4)) for i in range(self.devices)]
        groups = []
        for core in range(2):
            for still in range(2):
                members = []
                for rest in range(self.rest):
                    for varied in range(2):
                        b, a = (varied, still) if core == 0 else (still, varied)
                        members.append(((rest * 2 + b) * 2 + a) * 2 + core)
                groups.append(members)
        self.groups = groups

    def spread(self, blocks):
        return lax.all_to_all(blocks, AXES, 0, 0, tiled=True, axis_index_groups=self.groups)

    def gather(self, block):
        rows, depth = block.shape
        count = self.rest * 2
        mine = self.spread(jnp.broadcast_to(block[None], (count, rows, depth)))
        other = lax.ppermute(mine, AXES, self.alone_pairs)
        passed = lax.ppermute(mine, AXES, self.core_pairs)
        passed_other = lax.ppermute(other, AXES, self.core_pairs)
        pieces = (mine, other, passed, passed_other)
        if rows % 16:
            return self.put_in_order(pieces)
        return pl.pallas_call(
            functools.partial(put_together, rows),
            in_specs=[pl.BlockSpec(memory_space=pltpu.SMEM)]
            + [pl.BlockSpec(memory_space=pl.ANY)] * 4,
            out_specs=pl.BlockSpec(memory_space=pl.ANY),
            out_shape=shape_of(self.devices * rows, depth),
            scratch_shapes=[pltpu.SemaphoreType.DMA((4, count))],
        )(jnp.stack([self.core, self.a, self.b]).astype(jnp.int32), *pieces)

    def put_in_order(self, pieces):
        mine, other, passed, passed_other = pieces
        count, rows, depth = mine.shape
        sibling = jnp.where(self.core == 0, self.b, self.a)

        def ordered(own, away, alone):
            low = jnp.where(alone == 0, own, away)
            high = jnp.where(alone == 0, away, own)
            return jnp.stack([low, high]).reshape(2, self.rest, 2, rows, depth)

        half = ordered(mine, other, self.alone)
        half_passed = ordered(passed, passed_other, sibling)
        first = jnp.where(self.core == 0, half, half_passed)
        second = jnp.where(self.core == 0, half_passed, half)
        whole = jnp.stack(
            [first.transpose(1, 2, 0, 3, 4), second.transpose(1, 0, 2, 3, 4)], axis=3
        )
        return whole.reshape(self.devices * rows, depth)

    def scatter_sum(self, full):
        depth = full.shape[1]
        rows = full.shape[0] // self.devices
        blocks = full.reshape(self.rest, 4, 2, rows, depth)
        away = lax.dynamic_index_in_dim(blocks, 1 - self.core, 2, keepdims=False)
        here = lax.dynamic_index_in_dim(blocks, self.core, 2, keepdims=False)
        came = lax.ppermute(away, AXES, self.core_pairs)
        chip = (here.astype(FULL) + came.astype(FULL)).astype(LOW)

        def pick(side):
            places = [
                jnp.where(self.core == 0, step * 2 + side, side * 2 + step) for step in range(2)
            ]
            return jnp.stack(
                [lax.dynamic_index_in_dim(chip, place, 1, keepdims=False) for place in places],
                axis=1,
            )

        came = lax.ppermute(pick(1 - self.alone), AXES, self.alone_pairs)
        pair = pick(self.alone).astype(FULL) + came.astype(FULL)
        parts = self.spread(pair.astype(LOW).reshape(self.rest * 2, rows, depth))
        return jnp.sum(parts.astype(FULL), axis=0)


def per_device(
    dp,
    cores,
    samples,
    mel,
    lengths,
    hops,
    conv_weight,
    cond_weight,
    conv_bias,
    out_weight,
    out_bias,
    grad_out,
    grad_skip,
):
    wires = Wires(dp, cores)
    sample_count, channels = samples.shape[1:]
    frame_count, mel_count = mel.shape[1:]
    layers = conv_weight.shape[0]
    size = Sizes(channels, mel_count)
    gate = 2 * channels
    assert layers == 2 and sample_count % TILE == 0 and TILE == FIRST_DILATION
    steps = sample_count // TILE
    info = jnp.concatenate([lengths, hops])
    x, go, gs = samples[0], grad_out[0], grad_skip[0]
    mel_table = jnp.zeros((LANES, size.extra), LOW)
    mel_table = mel_table.at[:frame_count, :mel_count].set(mel[0])
    mel_table = mel_table.at[:frame_count, mel_count].set(1.0)

    packs = []
    for layer in range(layers):
        fill = jnp.zeros((size.extra - mel_count - 2, conv_weight.shape[2]), LOW)
        pack = jnp.concatenate(
            [
                conv_weight[layer],
                cond_weight[layer],
                conv_bias[layer][None],
                out_bias[layer][None],
                fill,
                out_weight[layer],
            ],
            axis=0,
        ).T
        packs.append(wires.gather(pack))
    w0, w1 = packs

    weights = fixed(gate, size.pack)
    table = fixed(LANES, size.extra)
    macs = sample_count * channels * channels

    low0, h1, low1, gated0, slope0 = call(
        functools.partial(forward_0, size),
        steps,
        info,
        (x, x, w0, mel_table),
        [tiled(channels, lambda i: jnp.maximum(i - 1, 0)), tiled(channels), weights, table],
        (
            shape_of(sample_count, channels),
            shape_of(sample_count, channels, dtype=FULL),
            shape_of(sample_count, channels),
            shape_of(sample_count, channels),
            shape_of(sample_count, gate),
        ),
        [tiled(channels), tiled(channels), tiled(channels), tiled(channels), tiled(gate)],
        [],
        10 * macs,
    )
    prev1, gated1, pre1, proj1 = call(
        functools.partial(forward_1, size),
        steps,
        info,
        (low1, w1, mel_table, go, gs),
        [tiled(channels), weights, table, tiled(channels), tiled(channels)],
        (
            shape_of(sample_count, channels),
            shape_of(sample_count, channels),
            shape_of(sample_count, gate),
            shape_of(sample_count, gate),
        ),
        [tiled(channels), tiled(channels), tiled(gate), tiled(gate)],
        [pltpu.VMEM((8, channels), FULL)],
        12 * macs,
    )

    part = gate // 4
    columns = pl.BlockSpec((sample_count, part), lambda i, info: (0, i))
    whole = fixed(sample_count, channels)

    def weight_part(shift, pre, proj, low, prev, gated, w):
        cond_columns = pl.BlockSpec(
            (part, size.extra), lambda i, info: (i, size.taps // size.extra)
        )
        return call(
            functools.partial(weight_grads, size, shift),
            4,
            info,
            (pre, proj, low, prev, gated, mel_table, w),
            [columns, columns, whole, whole, whole, table, cond_columns],
            (shape_of(gate, size.pack), shape_of(LANES, size.extra, dtype=FULL)),
            [
                pl.BlockSpec((part, size.pack), lambda i, info: (i, 0)),
                fixed(LANES, size.extra),
            ],
            [pltpu.VMEM((sample_count, LANES), LOW)],
            12 * macs,
        )

    grads1, melg1 = weight_part(1, pre1, proj1, low1, prev1, gated1, w1)
    own1 = wires.scatter_sum(grads1)

    backwards = lambda i: steps - 1 - i
    gh1, proj0, pre0 = call(
        functools.partial(backward_0, size),
        steps,
        info,
        (pre1, w1, w0, go, gs, slope0),
        [
            tiled(gate, backwards),
            weights,
            weights,
            tiled(channels, backwards),
            tiled(channels, backwards),
            tiled(gate, backwards),
        ],
        (
            shape_of(sample_count, channels, dtype=FULL),
            shape_of(sample_count, gate),
            shape_of(sample_count, gate),
        ),
        [tiled(channels, backwards), tiled(gate, backwards), tiled(gate, backwards)],
        [pltpu.VMEM((8, channels), FULL)],
        12 * macs,
    )
    grads0, melg0 = weight_part(FIRST_DILATION, pre0, proj0, low0, low0, gated0, w0)
    own0 = wires.scatter_sum(grads0)

    residual_out, skip_output_sum, samples_grad = call(
        functools.partial(outputs, size),
        steps,
        info,
        (gh1, pre0, pre0, w0, w1, h1, gated0, gated1),
        [
            tiled(channels),
            tiled(gate),
            tiled(gate, lambda i: jnp.minimum(i + 1, steps - 1)),
            weights,
            weights,
            tiled(channels),
            tiled(channels),
            tiled(channels),
        ],
        (
            shape_of(sample_count, channels),
            shape_of(sample_count, channels),
            shape_of(sample_count, channels, dtype=FULL),
        ),
        [tiled(channels), tiled(channels), tiled(channels)],
        [],
        14 * macs,
    )
    mel_grad = (melg0 + melg1)[:frame_count, :mel_count]
    own = jnp.stack([own0, own1]).transpose(0, 2, 1)
    at = size.taps + mel_count
    return (
        residual_out[None],
        skip_output_sum[None],
        samples_grad[None],
        mel_grad[None],
        own[:, : size.taps],
        own[:, size.taps : at],
        own[:, at],
        own[:, size.conv :],
        own[:, at + 1],
    )


def solution(mesh):
    dp, cores = mesh.shape["dp"], mesh.shape["group"]

    def everything(*arrays):
        return per_device(dp, cores, *arrays)

    clips = P(AXES, None, None)
    columns = P(None, None, AXES)
    biases = P(None, AXES)
    return jax.shard_map(
        everything,
        mesh=mesh,
        in_specs=(
            clips, clips, P(AXES), P(AXES), columns, columns, biases, columns, biases, clips, clips,
        ),
        out_specs=(clips, clips, clips, clips, columns, columns, biases, columns, biases),
        check_vma=False,
    )
```

```python
import functools

import jax
import jax.numpy as jnp
from jax import lax
from jax.experimental import pallas as pl
from jax.experimental.pallas import tpu as pltpu
from jax.sharding import PartitionSpec as P

FIRST_DILATION = 512
AXES = ("dp", "group")
LANES = 128
TILE = 512
VMEM = 56 * 1024 * 1024
LOW = jnp.bfloat16
FULL = jnp.float32


def dot(left, right):
    return jnp.dot(left, right, preferred_element_type=FULL)


def dot_cols(left, right, **more):
    return lax.dot_general(
        left, right, (((1,), (1,)), ((), ())), preferred_element_type=FULL, **more
    )


def dot_rows(left, right, **more):
    return lax.dot_general(
        left, right, (((0,), (0,)), ((), ())), preferred_element_type=FULL, **more
    )


class Sizes:
    def __init__(self, channels, mel_count):
        self.channels = channels
        self.gate = 2 * channels
        self.mel = mel_count
        self.early = channels
        self.now = 2 * channels
        self.extra = 3 * channels
        self.extra_width = -(-(mel_count + 2) // LANES) * LANES
        self.pack = self.extra + self.extra_width


def mask_of(info_ref, start, rows):
    places = start + lax.broadcasted_iota(jnp.int32, (rows, 1), 0)
    return (places < info_ref[0]).astype(FULL)


def frames_of(info_ref, start, rows):
    places = start + lax.broadcasted_iota(jnp.int32, (rows, LANES), 0)
    first = lax.broadcasted_iota(jnp.int32, (rows, LANES), 1) * info_ref[1]
    return ((places >= first) & (places < first + info_ref[1])).astype(FULL).astype(LOW)


def masked(ref, mask):
    return (ref[...].astype(FULL) * mask).astype(LOW)


def out_bias_row(size, extra):
    column = lax.broadcasted_iota(jnp.int32, (8, size.extra_width), 1)
    pick = (column == size.mel + 1).astype(FULL).astype(LOW)
    return dot_cols(pick, extra)[0:1]


def gates(taps, w_ref, size, side):
    channels = size.channels
    width = channels // 2
    low = slice(side * width, (side + 1) * width)
    high = slice(channels + side * width, channels + (side + 1) * width)
    tangent = jnp.tanh(dot_cols(taps, w_ref[low, size.early :]))
    sig_gate = 0.5 * jnp.tanh(0.5 * dot_cols(taps, w_ref[high, size.early :])) + 0.5
    gated = tangent * sig_gate
    return low, high, gated, sig_gate * (1.0 - tangent * tangent), gated * (1.0 - sig_gate)


def forward_0(size, wires, info_ref, x_ref, mel_ref, *refs):
    pieces, refs = refs[: wires.pieces], refs[wires.pieces :]
    low1_ref, gated_ref, slope_ref, whole_ref, w_ref, prev_ref, sems, out_sem = refs
    step = pl.program_id(0)
    rows, channels = x_ref.shape

    @pl.when(step == 0)
    def _():
        wires.put_together(info_ref, pieces, w_ref, sems)
        pltpu.make_async_copy(w_ref, whole_ref, out_sem).start()
        prev_ref[...] = jnp.zeros_like(prev_ref)

    mask = mask_of(info_ref, step * rows, rows)
    hidden = x_ref[...].astype(FULL) * mask
    low = hidden.astype(LOW)
    cond = dot(frames_of(info_ref, step * rows, rows), mel_ref[...]).astype(LOW)
    taps = jnp.concatenate([prev_ref[...], low, cond], axis=1)
    for side in range(2):
        first, second, gated, slope_a, slope_b = gates(taps, w_ref, size, side)
        gated_ref[:, first] = gated.astype(LOW)
        slope_ref[:, first] = slope_a.astype(LOW)
        slope_ref[:, second] = slope_b.astype(LOW)
    prev_ref[...] = low
    moved = dot_cols(gated_ref[...], w_ref[:channels, :channels])
    moved = moved + out_bias_row(size, w_ref[:channels, size.extra :])
    low1_ref[...] = ((hidden + moved) * mask).astype(LOW)

    @pl.when(step == pl.num_programs(0) - 1)
    def _():
        pltpu.make_async_copy(w_ref, whole_ref, out_sem).wait()


def layer_1(size, wires, steps, info_ref, low1_ref, mel_ref, go_ref, gs_ref, *refs):
    pieces, refs = refs[: wires.pieces], refs[wires.pieces :]
    gated_ref, pre_ref, here_ref, away_ref, melg_ref, whole_ref, *scratch = refs
    w_ref, prev_s, low_s, gated_s, pre_s, proj_s, frames_s, part_s, carry_ref, sems, out_sem = scratch
    step = pl.program_id(0)
    rows, channels = low1_ref.shape

    @pl.when(step == 0)
    def _():
        wires.put_together(info_ref, pieces, w_ref, sems)
        pltpu.make_async_copy(w_ref, whole_ref, out_sem).start()
        carry_ref[...] = jnp.zeros_like(carry_ref)
        melg_ref[...] = jnp.zeros_like(melg_ref)

    @pl.when(step < steps)
    def _():
        tile = pl.ds(pl.multiple_of(step * rows, rows), rows)
        mask = mask_of(info_ref, step * rows, rows)
        low = low1_ref[...]
        wide = low.astype(FULL)
        place = lax.broadcasted_iota(jnp.int32, (rows, 1), 0)
        prev = jnp.where(place == 0, carry_ref[7:8], pltpu.roll(wide, 1, 0)).astype(LOW)
        carry_ref[...] = wide[rows - 8 :]
        frames = frames_of(info_ref, step * rows, rows)
        cond = dot(frames, mel_ref[...]).astype(LOW)
        taps = jnp.concatenate([prev, low, cond], axis=1)
        proj = jnp.concatenate([masked(go_ref, mask), masked(gs_ref, mask)], axis=1)
        prev_s[tile] = prev
        low_s[tile] = low
        frames_s[tile] = frames
        proj_s[tile] = proj
        grad_gated = dot(proj, w_ref[:, :channels])
        for side in range(2):
            first, second, gated, slope_a, slope_b = gates(taps, w_ref, size, side)
            gated_ref[:, first] = gated.astype(LOW)
            pre_ref[:, first] = (grad_gated[:, first] * slope_a).astype(LOW)
            pre_ref[:, second] = (grad_gated[:, first] * slope_b).astype(LOW)
        gated_s[tile] = gated_ref[...]
        pre_s[tile] = pre_ref[...]

    @pl.when(step >= steps)
    def _():
        width = part_s.shape[0]
        part = pl.ds(pl.multiple_of((step - steps) * width, width), width)
        pre = pre_s[:, part]
        part_s[:, size.early : size.now] = dot_rows(pre, prev_s[...]).astype(LOW)
        part_s[:, size.now : size.extra] = dot_rows(pre, low_s[...]).astype(LOW)
        finish_part(size, pre, proj_s[:, part], frames_s, gated_s, mel_ref, w_ref[part, size.extra :], melg_ref, part_s)
        wires.put_apart(info_ref, part_s, here_ref, away_ref)

    @pl.when(step == pl.num_programs(0) - 1)
    def _():
        pltpu.make_async_copy(w_ref, whole_ref, out_sem).wait()


def finish_part(size, pre, proj, frames_ref, gated_ref, mel_ref, cond_weight, melg_ref, part_ref):
    exact = dict(precision=lax.Precision.HIGHEST)
    sums = dot_rows(pre, frames_ref[...])
    extra = jnp.dot(sums, mel_ref[...].astype(FULL), preferred_element_type=FULL, **exact)
    melg_ref[...] += dot_rows(sums, cond_weight.astype(FULL), **exact)
    total = jnp.sum(proj.astype(FULL), axis=0, keepdims=True)
    bias = jnp.broadcast_to(total, (LANES, total.shape[1])).T[:, 0:1]
    column = lax.broadcasted_iota(jnp.int32, extra.shape, 1)
    part_ref[:, size.extra :] = jnp.where(column == size.mel + 1, bias, extra).astype(LOW)
    part_ref[:, : size.channels] = dot_rows(proj, gated_ref[...]).astype(LOW)


def backward_0(size, info_ref, pre1_ref, early1_ref, now1_ref, out0_ref, go_ref, gs_ref, slope_ref, res_ref, pre0_ref, carry_ref):
    step = pl.program_id(0)
    rows, channels = go_ref.shape
    tile = pl.num_programs(0) - 1 - step
    mask = mask_of(info_ref, tile * rows, rows)

    @pl.when(step == 0)
    def _():
        carry_ref[...] = jnp.zeros_like(carry_ref)

    pre1 = pre1_ref[...]
    early = dot(pre1, early1_ref[...])
    place = lax.broadcasted_iota(jnp.int32, (rows, 1), 0)
    later = jnp.where(place == rows - 1, carry_ref[0:1], pltpu.roll(early, rows - 1, 0))
    carry_ref[...] = early[:8]
    now = dot(pre1, now1_ref[...])
    res = ((go_ref[...].astype(FULL) * mask + now + later) * mask).astype(LOW)
    res_ref[...] = res
    proj = jnp.concatenate([res, masked(gs_ref, mask)], axis=1)
    grad_gated = dot(proj, out0_ref[...])
    pre0_ref[:, :channels] = (grad_gated * slope_ref[:, :channels].astype(FULL)).astype(LOW)
    pre0_ref[:, channels:] = (grad_gated * slope_ref[:, channels:].astype(FULL)).astype(LOW)


def weights_0(size, wires, info_ref, pre_ref, res_ref, gs_ref, x_ref, gated_ref, mel_ref, wc_ref, here_ref, away_ref, melg_ref, frames_s, proj_s, part_s):
    step = pl.program_id(0)
    samples = x_ref.shape[0]

    @pl.when(step == 0)
    def _():
        frames_s[...] = frames_of(info_ref, 0, samples)
        melg_ref[...] = jnp.zeros_like(melg_ref)

    half = pl.num_programs(0) // 2

    @pl.when(step < half)
    def _():
        proj_s[...] = res_ref[...]

    @pl.when(step >= half)
    def _():
        proj_s[...] = masked(gs_ref, mask_of(info_ref, 0, samples))

    pre = pre_ref[...]
    shift = FIRST_DILATION
    early = dot_rows(pre[shift:], x_ref[: samples - shift])
    part_s[:, size.early : size.now] = early.astype(LOW)
    part_s[:, size.now : size.extra] = dot_rows(pre, x_ref[...]).astype(LOW)
    finish_part(size, pre, proj_s[...], frames_s, gated_ref, mel_ref, wc_ref[...], melg_ref, part_s)
    wires.put_apart(info_ref, part_s, here_ref, away_ref)


def outputs(size, info_ref, x_ref, res_ref, pre_ref, next_ref, gated0_ref, gated1_ref, w0_ref, out1_ref, extra1_ref, out_ref, skip_ref, sg_ref):
    step = pl.program_id(0)
    rows, channels = x_ref.shape
    mask = mask_of(info_ref, step * rows, rows)
    grad = res_ref[...].astype(FULL) + dot(pre_ref[...], w0_ref[:, size.now : size.extra])
    later = dot(next_ref[...], w0_ref[:, size.early : size.now])
    grad = grad + jnp.where(step < pl.num_programs(0) - 1, later, 0.0)
    sg_ref[...] = grad * mask
    gated0, gated1 = gated0_ref[...], gated1_ref[...]
    gated = jnp.concatenate([gated0, gated1], axis=1)

    def projected(rows):
        both = jnp.concatenate([w0_ref[rows, :channels], out1_ref[rows]], axis=1)
        bias = out_bias_row(size, w0_ref[rows, size.extra :]) + out_bias_row(size, extra1_ref[rows])
        return dot_cols(gated, both) + bias

    res = projected(slice(0, channels))
    out_ref[...] = ((x_ref[...].astype(FULL) + res) * mask).astype(LOW)
    skip_ref[...] = (projected(slice(channels, 2 * channels)) * mask).astype(LOW)


def call(kernel, grid, info, operands, specs, outs, out_specs, scratch, flops):
    moved = sum(x.size * x.dtype.itemsize for x in operands)
    moved += sum(x.size * x.dtype.itemsize for x in outs)
    return pl.pallas_call(
        kernel,
        grid_spec=pltpu.PrefetchScalarGridSpec(
            num_scalar_prefetch=1,
            grid=(grid,),
            in_specs=specs,
            out_specs=out_specs,
            scratch_shapes=scratch,
        ),
        out_shape=outs,
        compiler_params=pltpu.CompilerParams(
            vmem_limit_bytes=VMEM, dimension_semantics=("arbitrary",)
        ),
        cost_estimate=pl.CostEstimate(flops=flops, bytes_accessed=moved, transcendentals=0),
    )(info, *operands)


def shape_of(*shape, dtype=LOW):
    return jax.ShapeDtypeStruct(shape, dtype)


def tiled(width, place=lambda i: i):
    return pl.BlockSpec((TILE, width), lambda i, info: (place(i), 0))


def fixed(*shape, at=(0, 0)):
    return pl.BlockSpec(shape, lambda i, info: at)


ANYWHERE = pl.BlockSpec(memory_space=pl.ANY)


class Wires:
    def __init__(self, dp, cores, channels):
        assert dp % 4 == 0 and cores == 2
        self.rest = dp // 4
        self.devices = dp * 2
        self.rows = channels // self.devices
        self.direct = self.rows % 16 == 0
        self.pieces = 8 if self.direct else 1
        me = lax.axis_index(AXES)
        self.core = me % 2
        self.a = (me // 2) % 2
        self.b = (me // 4) % 2
        every = range(self.devices)
        self.sibling = [(i, i ^ 1) for i in every]
        self.first = [(i, i ^ (4 if i % 2 else 2)) for i in every]
        self.second = [(i, i ^ (2 if i % 2 else 4)) for i in every]
        self.columns = [[rest * 8 + low for rest in range(self.rest)] for low in range(8)]

    def place(self):
        return jnp.stack([self.core, self.a, self.b]).astype(jnp.int32)

    def hop(self, value, pairs):
        return lax.ppermute(value, AXES, pairs)

    def swap_rest(self, blocks):
        return lax.all_to_all(blocks, AXES, 0, 0, tiled=True, axis_index_groups=self.columns)

    def gather(self, block):
        mine = self.swap_rest(jnp.broadcast_to(block[None], (self.rest,) + block.shape))
        one = self.hop(mine, self.first)
        two = self.hop(mine, self.second)
        far = self.hop(one, self.second)
        pieces = [mine, one, two, far]
        pieces += [self.hop(piece, self.sibling) for piece in pieces]
        return pieces if self.direct else [self.put_in_order(pieces)]

    def put_in_order(self, pieces):
        whole = jnp.zeros((self.rest, 2, 2, 2) + pieces[0].shape[1:], LOW)
        for index, piece in enumerate(pieces):
            source = self.core if index < 4 else 1 - self.core
            first, second = index % 2, (index // 2) % 2
            at_a = self.a ^ jnp.where(source == 0, first, second)
            at_b = self.b ^ jnp.where(source == 0, second, first)
            whole = lax.dynamic_update_slice(
                whole, piece[:, None, None, None], (0, at_b, at_a, source, 0, 0)
            )
        return whole.reshape(-1, pieces[0].shape[2])

    def put_together(self, info_ref, pieces, w_ref, sems):
        if not self.direct:
            copy = pltpu.make_async_copy(pieces[0], w_ref, sems.at[0, 0])
            copy.start()
            copy.wait()
            return
        core, a, b = info_ref[2], info_ref[3], info_ref[4]
        copies = []
        for index, piece in enumerate(pieces):
            source = core if index < 4 else 1 - core
            first, second = index % 2, (index // 2) % 2
            at_a = a ^ jnp.where(source == 0, first, second)
            at_b = b ^ jnp.where(source == 0, second, first)
            for rest in range(self.rest):
                place = ((rest * 2 + at_b) * 2 + at_a) * 2 + source
                rows = pl.ds(pl.multiple_of(place * self.rows, self.rows), self.rows)
                copies.append(
                    pltpu.make_async_copy(piece.at[rest], w_ref.at[rows], sems.at[index, rest])
                )
        for copy in copies:
            copy.start()
        for copy in copies:
            copy.wait()

    def put_apart(self, info_ref, part_ref, here_ref, away_ref):
        if not self.direct:
            here_ref[...] = part_ref[...]
            return
        core, a, b = info_ref[2], info_ref[3], info_ref[4]
        for block in range(part_ref.shape[0] // self.rows):
            at_b, at_a, owner = (block // 4) % 2, (block // 2) % 2, block % 2
            value = part_ref[block * self.rows : (block + 1) * self.rows]
            first, second = at_a ^ a, at_b ^ b
            if owner:
                first, second = second, first

            @pl.when(core == owner)
            def _():
                here_ref[first, second, block // 8] = value

            @pl.when(core != owner)
            def _():
                away_ref[first, second, block // 8] = value

    def apart_specs(self, parts, width, pack, step):
        if not self.direct:
            spec = pl.BlockSpec((width, pack), lambda i, info: (step(i), 0))
            none = pl.BlockSpec((8, LANES), lambda i, info: (0, 0))
            return (shape_of(parts * width, pack), shape_of(8, LANES)), [spec, none]
        shape = shape_of(2, 2, self.rest, self.rows, pack)
        spec = pl.BlockSpec(
            (2, 2, self.rest // parts, self.rows, pack), lambda i, info: (0, 0, step(i), 0, 0)
        )
        return (shape, shape), [spec, spec]

    def by_distance(self, full):
        rows = full.shape[0] // self.devices
        blocks = full.reshape(self.rest, 2, 2, 2, rows, full.shape[1])
        parts = []
        for away in range(2):
            source = self.core ^ away
            for first in range(2):
                for second in range(2):
                    at_a = self.a ^ jnp.where(source == 0, first, second)
                    at_b = self.b ^ jnp.where(source == 0, second, first)
                    parts.append(
                        lax.dynamic_slice(
                            blocks,
                            (0, at_b, at_a, source, 0, 0),
                            (self.rest, 1, 1, 1, rows, full.shape[1]),
                        )[:, 0, 0, 0]
                    )
        return jnp.stack(parts).reshape(2, 2, 2, self.rest, rows, full.shape[1])

    def chip_sum(self, here, away):
        return add_low(here, self.hop(away, self.sibling))

    def pair_sum(self, chip):
        return add_low(chip[0], self.hop(chip[1], self.first))

    def four_sum(self, pair):
        return add_low(pair[0], self.hop(pair[1], self.second))

    def rest_sum(self, four):
        return jnp.sum(self.swap_rest(four).astype(FULL), axis=0)


def add_low(left, right):
    return (left.astype(FULL) + right.astype(FULL)).astype(LOW)


def per_device(
    dp,
    cores,
    samples,
    mel,
    lengths,
    hops,
    conv_weight,
    cond_weight,
    conv_bias,
    out_weight,
    out_bias,
    grad_out,
    grad_skip,
):
    sample_count, channels = samples.shape[1:]
    frame_count, mel_count = mel.shape[1:]
    layers = conv_weight.shape[0]
    size = Sizes(channels, mel_count)
    gate = size.gate
    wires = Wires(dp, cores, gate)
    assert layers == 2 and sample_count % TILE == 0 and TILE == FIRST_DILATION
    steps = sample_count // TILE
    info = jnp.concatenate([lengths, hops, wires.place()])
    x, go, gs = samples[0], grad_out[0], grad_skip[0]
    mel_table = jnp.concatenate([mel[0], jnp.ones((frame_count, 1), LOW)], axis=1)
    mel_table = jnp.pad(
        mel_table, ((0, LANES - frame_count), (0, size.extra_width - mel_count - 1))
    )

    packs = []
    for layer in range(layers):
        fill = jnp.zeros((size.extra_width - mel_count - 2, conv_weight.shape[2]), LOW)
        pack = jnp.concatenate(
            [
                out_weight[layer],
                conv_weight[layer],
                cond_weight[layer],
                conv_bias[layer][None],
                out_bias[layer][None],
                fill,
            ],
            axis=0,
        ).T
        packs.append(wires.gather(pack))

    table = fixed(LANES, size.extra_width)
    macs = sample_count * channels * channels
    whole_w = shape_of(gate, size.pack)
    weights = pltpu.VMEM((gate, size.pack), LOW)
    sems = pltpu.SemaphoreType.DMA((8, wires.rest))
    one_sem = pltpu.SemaphoreType.DMA

    low1, gated0, slope0, w0 = call(
        functools.partial(forward_0, size, wires),
        steps,
        info,
        (x, mel_table, *packs[0]),
        [tiled(channels), table] + [ANYWHERE] * wires.pieces,
        (
            shape_of(sample_count, channels),
            shape_of(sample_count, channels),
            shape_of(sample_count, gate),
            whole_w,
        ),
        [tiled(channels), tiled(channels), tiled(gate), ANYWHERE],
        [weights, pltpu.VMEM((TILE, channels), LOW), sems, one_sem],
        10 * macs,
    )

    parts = 4
    width = gate // parts
    late = lambda i: jnp.minimum(i, steps - 1)
    apart, apart_specs = wires.apart_specs(
        parts, width, size.pack, lambda i: jnp.maximum(i - steps, 0)
    )
    melg = shape_of(LANES, size.extra_width, dtype=FULL)
    gated1, pre1, here1, away1, melg1, w1 = call(
        functools.partial(layer_1, size, wires, steps),
        steps + parts,
        info,
        (low1, mel_table, go, gs, *packs[1]),
        [tiled(channels, late), table, tiled(channels, late), tiled(channels, late)]
        + [ANYWHERE] * wires.pieces,
        (shape_of(sample_count, channels), shape_of(sample_count, gate), *apart, melg, whole_w),
        [tiled(channels, late), tiled(gate, late), *apart_specs, table, ANYWHERE],
        [
            weights,
            pltpu.VMEM((sample_count, channels), LOW),
            pltpu.VMEM((sample_count, channels), LOW),
            pltpu.VMEM((sample_count, channels), LOW),
            pltpu.VMEM((sample_count, gate), LOW),
            pltpu.VMEM((sample_count, gate), LOW),
            pltpu.VMEM((sample_count, LANES), LOW),
            pltpu.VMEM((width, size.pack), LOW),
            pltpu.VMEM((8, channels), FULL),
            sems,
            one_sem,
        ],
        24 * macs,
    )
    if not wires.direct:
        here1, away1 = wires.by_distance(here1)

    backwards = lambda i: steps - 1 - i
    tap = lambda at: fixed(gate, channels, at=(0, at))
    res0, pre0 = call(
        functools.partial(backward_0, size),
        steps,
        info,
        (pre1, w1, w1, w0, go, gs, slope0),
        [
            tiled(gate, backwards),
            tap(1),
            tap(2),
            tap(0),
            tiled(channels, backwards),
            tiled(channels, backwards),
            tiled(gate, backwards),
        ],
        (shape_of(sample_count, channels), shape_of(sample_count, gate)),
        [tiled(channels, backwards), tiled(gate, backwards)],
        [pltpu.VMEM((8, channels), FULL)],
        12 * macs,
    )
    chip1 = wires.chip_sum(here1, away1)
    pre0, chip1 = lax.optimization_barrier((pre0, chip1))

    half = parts // 2
    apart, apart_specs = wires.apart_specs(parts, width, size.pack, lambda i: i)
    columns = lambda place: pl.BlockSpec((sample_count, width), lambda i, info: (0, place(i)))
    here0, away0, melg0 = call(
        functools.partial(weights_0, size, wires),
        parts,
        info,
        (pre0, res0, gs, x, gated0, mel_table, w0),
        [
            columns(lambda i: i),
            columns(lambda i: jnp.minimum(i, half - 1)),
            columns(lambda i: jnp.maximum(i - half, 0)),
            fixed(sample_count, channels),
            fixed(sample_count, channels),
            table,
            pl.BlockSpec(
                (width, size.extra_width), lambda i, info: (i, size.extra // size.extra_width)
            ),
        ],
        (*apart, melg),
        [*apart_specs, table],
        [
            pltpu.VMEM((sample_count, LANES), LOW),
            pltpu.VMEM((sample_count, width), LOW),
            pltpu.VMEM((width, size.pack), LOW),
        ],
        12 * macs,
    )
    if not wires.direct:
        here0, away0 = wires.by_distance(here0)
    pair1 = wires.pair_sum(chip1)
    chip0 = wires.chip_sum(here0, away0)
    four1 = wires.four_sum(pair1)
    pair0 = wires.pair_sum(chip0)
    own1 = wires.rest_sum(four1)
    four0 = wires.four_sum(pair0)
    own0 = wires.rest_sum(four0)

    residual_out, skip_output_sum, samples_grad = call(
        functools.partial(outputs, size),
        steps,
        info,
        (x, res0, pre0, pre0, gated0, gated1, w0, w1, w1),
        [
            tiled(channels),
            tiled(channels),
            tiled(gate),
            tiled(gate, lambda i: jnp.minimum(i + 1, steps - 1)),
            tiled(channels),
            tiled(channels),
            fixed(gate, size.pack),
            tap(0),
            fixed(gate, size.extra_width, at=(0, size.extra // size.extra_width)),
        ],
        (
            shape_of(sample_count, channels),
            shape_of(sample_count, channels),
            shape_of(sample_count, channels, dtype=FULL),
        ),
        [tiled(channels), tiled(channels), tiled(channels)],
        [],
        16 * macs,
    )
    mel_grad = (melg0 + melg1)[:frame_count, :mel_count]
    own = jnp.stack([own0, own1]).transpose(0, 2, 1)
    at = size.extra + mel_count
    return (
        residual_out[None],
        skip_output_sum[None],
        samples_grad[None],
        mel_grad[None],
        own[:, size.early : size.extra],
        own[:, size.extra : at],
        own[:, at],
        own[:, : size.channels],
        own[:, at + 1],
    )


def solution(mesh):
    dp, cores = mesh.shape["dp"], mesh.shape["group"]

    def everything(*arrays):
        return per_device(dp, cores, *arrays)

    clips = P(AXES, None, None)
    columns = P(None, None, AXES)
    biases = P(None, AXES)
    return jax.shard_map(
        everything,
        mesh=mesh,
        in_specs=(
            clips, clips, P(AXES), P(AXES), columns, columns, biases, columns, biases, clips, clips,
        ),
        out_specs=(clips, clips, clips, clips, columns, columns, biases, columns, biases),
        check_vma=False,
    )
```

```python
import functools

import jax
import jax.numpy as jnp
from jax import lax
from jax.experimental import pallas as pl
from jax.experimental.pallas import tpu as pltpu
from jax.sharding import PartitionSpec as P

FIRST_DILATION = 512
AXES = ("dp", "group")
LANES = 128
TILE = 512
MIB = 1024 * 1024
ROOM_0, ROOM_1, ROOM_2, ROOM_3, ROOM_4, ROOM_5, ROOM_SMALL = 8, 13, 6, 8, 8, 8, 12
LOW = jnp.bfloat16
FULL = jnp.float32


def dot(left, right):
    return jnp.dot(left, right, preferred_element_type=FULL)


def dot_cols(left, right, **more):
    return lax.dot_general(
        left, right, (((1,), (1,)), ((), ())), preferred_element_type=FULL, **more
    )


def dot_rows(left, right, **more):
    return lax.dot_general(
        left, right, (((0,), (0,)), ((), ())), preferred_element_type=FULL, **more
    )


class Sizes:
    def __init__(self, channels, mel_count):
        self.channels = channels
        self.gate = 2 * channels
        self.mel = mel_count
        self.early = channels
        self.now = 2 * channels
        self.extra = 3 * channels
        self.extra_width = -(-(mel_count + 2) // LANES) * LANES
        self.pack = self.extra + self.extra_width


def mask_of(info_ref, start, rows):
    places = start + lax.broadcasted_iota(jnp.int32, (rows, 1), 0)
    return (places < info_ref[0]).astype(FULL)


def frames_of(info_ref, start, rows):
    places = start + lax.broadcasted_iota(jnp.int32, (rows, LANES), 0)
    first = lax.broadcasted_iota(jnp.int32, (rows, LANES), 1) * info_ref[1]
    return ((places >= first) & (places < first + info_ref[1])).astype(FULL).astype(LOW)


def masked(value, mask):
    return (value.astype(FULL) * mask).astype(LOW)


def out_bias_row(size, extra):
    column = lax.broadcasted_iota(jnp.int32, (8, size.extra_width), 1)
    pick = (column == size.mel + 1).astype(FULL).astype(LOW)
    return dot_cols(pick, extra)[0:1]


def gates(taps, w_ref, size, side):
    channels = size.channels
    width = channels // 2
    low = slice(side * width, (side + 1) * width)
    high = slice(channels + side * width, channels + (side + 1) * width)
    tangent = jnp.tanh(dot_cols(taps, w_ref[low, size.early :]))
    sig_gate = 0.5 * jnp.tanh(0.5 * dot_cols(taps, w_ref[high, size.early :])) + 0.5
    gated = tangent * sig_gate
    return low, high, gated, sig_gate * (1.0 - tangent * tangent), gated * (1.0 - sig_gate)


def rows_of(step, rows):
    return pl.ds(pl.multiple_of(step * rows, rows), rows)


def forward_0(size, wires, info_ref, x_ref, mel_ref, *refs):
    pieces, refs = refs[: wires.pieces], refs[wires.pieces :]
    low1_ref, gated_ref, slope_ref, w_ref = refs
    step = pl.program_id(0)
    channels = size.channels

    @pl.when(step == 0)
    def _():
        wires.put_together(info_ref, pieces, w_ref)

    tile = rows_of(step, TILE)
    mask = mask_of(info_ref, step * TILE, TILE)
    hidden = x_ref[tile].astype(FULL) * mask
    low = hidden.astype(LOW)
    prev_mask = mask_of(info_ref, (step - 1) * TILE, TILE) * (step > 0).astype(FULL)
    prev = x_ref[rows_of(jnp.maximum(step - 1, 0), TILE)].astype(FULL) * prev_mask
    cond = dot(frames_of(info_ref, step * TILE, TILE), mel_ref[...]).astype(LOW)
    taps = jnp.concatenate([prev.astype(LOW), low, cond], axis=1)
    for side in range(2):
        first, second, gated, slope_a, slope_b = gates(taps, w_ref, size, side)
        gated_ref[tile, first] = gated.astype(LOW)
        slope_ref[tile, first] = slope_a.astype(LOW)
        slope_ref[tile, second] = slope_b.astype(LOW)
    moved = dot_cols(gated_ref[tile], w_ref[:channels, :channels])
    moved = moved + out_bias_row(size, w_ref[:channels, size.extra :])
    low1_ref[tile] = ((hidden + moved) * mask).astype(LOW)


def layer_1(size, wires, steps, info_ref, low1_ref, mel_ref, go_ref, gs_ref, *refs):
    pieces, refs = refs[: wires.pieces], refs[wires.pieces :]
    gated_ref, pre_ref, w_ref, here_ref, away_ref, melg_ref, *scratch = refs
    prev_s, proj_s, frames_s, part_s = scratch
    step = pl.program_id(0)
    channels = size.channels

    @pl.when(step == 0)
    def _():
        wires.put_together(info_ref, pieces, w_ref)
        melg_ref[...] = jnp.zeros_like(melg_ref)

    @pl.when(step < steps)
    def _():
        tile = rows_of(step, TILE)
        mask = mask_of(info_ref, step * TILE, TILE)
        low = low1_ref[tile]
        before = pl.ds(pl.multiple_of(jnp.maximum(step * TILE - 16, 0), 16), 16)
        last = low1_ref[before].astype(FULL)[15:16] * (step > 0).astype(FULL)
        place = lax.broadcasted_iota(jnp.int32, (TILE, 1), 0)
        prev = jnp.where(place == 0, last, pltpu.roll(low.astype(FULL), 1, 0)).astype(LOW)
        frames = frames_of(info_ref, step * TILE, TILE)
        cond = dot(frames, mel_ref[...]).astype(LOW)
        taps = jnp.concatenate([prev, low, cond], axis=1)
        proj = jnp.concatenate([masked(go_ref[tile], mask), masked(gs_ref[tile], mask)], axis=1)
        prev_s[tile] = prev
        frames_s[tile] = frames
        grad_gated = dot(proj, w_ref[:, :channels])
        for side in range(2):
            first, second, gated, slope_a, slope_b = gates(taps, w_ref, size, side)
            gated_ref[tile, first] = gated.astype(LOW)
            pre_ref[tile, first] = (grad_gated[:, first] * slope_a).astype(LOW)
            pre_ref[tile, second] = (grad_gated[:, first] * slope_b).astype(LOW)

    @pl.when(step >= steps)
    def _():
        width = part_s.shape[0]
        part = rows_of(step - steps, width)
        half = channels // width
        mask = mask_of(info_ref, 0, low1_ref.shape[0])

        @pl.when(step < steps + half)
        def _():
            columns = rows_of(jnp.clip(step - steps, 0, half - 1), width)
            proj_s[...] = masked(go_ref[:, columns], mask)

        @pl.when(step >= steps + half)
        def _():
            columns = rows_of(jnp.maximum(step - steps - half, 0), width)
            proj_s[...] = masked(gs_ref[:, columns], mask)

        pre = pre_ref[:, part]
        part_s[:, size.early : size.now] = dot_rows(pre, prev_s[...]).astype(LOW)
        part_s[:, size.now : size.extra] = dot_rows(pre, low1_ref[...]).astype(LOW)
        finish_part(size, pre, proj_s[...], frames_s, gated_ref, mel_ref, w_ref[part, size.extra :], melg_ref, part_s)
        wires.put_apart(info_ref, step - steps, part_s, here_ref, away_ref)

def in_two(value):
    high = value.astype(LOW)
    return high, (value - high.astype(FULL)).astype(LOW)


def finish_part(size, pre, proj, frames_ref, gated_ref, mel_ref, cond_weight, melg_ref, part_ref):
    sums = in_two(dot_rows(frames_ref[...], pre))
    extra = sum(dot_rows(half, mel_ref[...]) for half in sums)
    melg_ref[...] += sum(dot(half, cond_weight) for half in sums)
    total = jnp.sum(proj.astype(FULL), axis=0, keepdims=True)
    bias = jnp.broadcast_to(total, (LANES, total.shape[1])).T[:, 0:1]
    column = lax.broadcasted_iota(jnp.int32, extra.shape, 1)
    part_ref[:, size.extra :] = jnp.where(column == size.mel + 1, bias, extra).astype(LOW)
    part_ref[:, : size.channels] = dot_rows(proj, gated_ref[...]).astype(LOW)


def backward_0(size, info_ref, pre1_ref, w1_ref, w0_ref, go_ref, gs_ref, slope_ref, res_ref, pre0_ref, carry_ref):
    step = pl.program_id(0)
    channels = size.channels
    index = pl.num_programs(0) - 1 - step
    tile = rows_of(index, TILE)
    mask = mask_of(info_ref, index * TILE, TILE)

    @pl.when(step == 0)
    def _():
        carry_ref[...] = jnp.zeros_like(carry_ref)

    pre1 = pre1_ref[tile]
    early = dot(pre1, w1_ref[:, size.early : size.now])
    place = lax.broadcasted_iota(jnp.int32, (TILE, 1), 0)
    later = jnp.where(place == TILE - 1, carry_ref[0:1], pltpu.roll(early, TILE - 1, 0))
    carry_ref[...] = early[:8]
    now = dot(pre1, w1_ref[:, size.now : size.extra])
    res = ((go_ref[tile].astype(FULL) * mask + now + later) * mask).astype(LOW)
    res_ref[tile] = res
    proj = jnp.concatenate([res, masked(gs_ref[tile], mask)], axis=1)
    grad_gated = dot(proj, w0_ref[:, :channels])
    for half in (slice(0, channels), slice(channels, 2 * channels)):
        pre0_ref[tile, half] = (grad_gated * slope_ref[tile, half].astype(FULL)).astype(LOW)


def weights_0(size, wires, info_ref, pre_ref, res_ref, gs_ref, x_ref, gated_ref, mel_ref, w_ref, here_ref, away_ref, melg_ref, frames_s, proj_s, part_s):
    step = pl.program_id(0)
    samples = x_ref.shape[0]

    @pl.when(step == 0)
    def _():
        frames_s[...] = frames_of(info_ref, 0, samples)
        melg_ref[...] = jnp.zeros_like(melg_ref)

    width = part_s.shape[0]
    half = pl.num_programs(0) // 2
    part = rows_of(step, width)

    @pl.when(step < half)
    def _():
        proj_s[...] = res_ref[:, rows_of(jnp.minimum(step, half - 1), width)]

    @pl.when(step >= half)
    def _():
        proj_s[...] = masked(
            gs_ref[:, rows_of(jnp.maximum(step - half, 0), width)], mask_of(info_ref, 0, samples)
        )

    pre = pre_ref[:, part]
    shift = FIRST_DILATION
    early = dot_rows(pre[shift:], x_ref[: samples - shift])
    part_s[:, size.early : size.now] = early.astype(LOW)
    part_s[:, size.now : size.extra] = dot_rows(pre, x_ref[...]).astype(LOW)
    finish_part(size, pre, proj_s[...], frames_s, gated_ref, mel_ref, w_ref[part, size.extra :], melg_ref, part_s)
    wires.put_apart(info_ref, step, part_s, here_ref, away_ref)


def samples_gradient(size, info_ref, res_ref, pre_ref, w0_ref, sg_ref):
    step = pl.program_id(0)
    tile = rows_of(step, TILE)
    grad = res_ref[tile].astype(FULL) + dot(pre_ref[tile], w0_ref[:, size.now : size.extra])
    after = rows_of(jnp.minimum(step + 1, pl.num_programs(0) - 1), TILE)
    later = dot(pre_ref[after], w0_ref[:, size.early : size.now])
    grad = grad + jnp.where(step < pl.num_programs(0) - 1, later, 0.0)
    sg_ref[...] = grad * mask_of(info_ref, step * TILE, TILE)


def forward_outputs(size, info_ref, x_ref, gated0_ref, gated1_ref, w0_ref, w1_ref, res_ref, skip_ref):
    step = pl.program_id(0)
    tile = rows_of(step, TILE)
    mask = mask_of(info_ref, step * TILE, TILE)
    channels = size.channels
    gated = jnp.concatenate([gated0_ref[tile], gated1_ref[tile]], axis=1)

    def projected(rows):
        both = jnp.concatenate([w0_ref[rows, :channels], w1_ref[rows, :channels]], axis=1)
        bias = out_bias_row(size, w0_ref[rows, size.extra :])
        return dot_cols(gated, both) + bias + out_bias_row(size, w1_ref[rows, size.extra :])

    res = projected(slice(0, channels))
    res_ref[...] = ((x_ref[tile].astype(FULL) + res) * mask).astype(LOW)
    skip_ref[...] = (projected(slice(channels, 2 * channels)) * mask).astype(LOW)


def add_and_part(left_ref, right_ref, stay_ref, go_ref):
    stay_ref[...] = add_low(left_ref[0], right_ref[0])
    go_ref[...] = add_low(left_ref[1], right_ref[1])


def pack_layers(layers, copies, conv_ref, cond_ref, conv_b_ref, out_ref, out_b_ref, *refs):
    rows = conv_ref.shape[1]
    same = lax.broadcasted_iota(jnp.int32, (rows, rows), 0)
    same = (same == lax.broadcasted_iota(jnp.int32, (rows, rows), 1)).astype(FULL).astype(LOW)
    for layer in range(layers):
        to_ref = refs[layer]
        early, extra = out_ref.shape[2], out_ref.shape[2] + conv_ref.shape[2]
        mel = cond_ref.shape[2]
        width = to_ref.shape[2] - extra
        biases = dot_cols(same, jnp.concatenate([conv_b_ref[...], out_b_ref[...]], axis=0))
        place = lax.broadcasted_iota(jnp.int32, (rows, width), 1)
        cond = jnp.concatenate(
            [cond_ref[layer].astype(FULL), jnp.zeros((rows, width - mel), FULL)], axis=1
        )
        cond = jnp.where(place == mel, biases[:, layer : layer + 1], cond)
        cond = jnp.where(place == mel + 1, biases[:, layers + layer : layers + layer + 1], cond)
        cond = cond.astype(LOW)
        for copy in range(copies):
            to_ref[copy, :, :early] = out_ref[layer]
            to_ref[copy, :, early:extra] = conv_ref[layer]
            to_ref[copy, :, extra:] = cond


def unpack_layers(layers, mel, *refs):
    conv_ref, cond_ref, conv_b_ref, out_ref, out_b_ref = refs[layers:]
    rows = conv_ref.shape[1]
    same = lax.broadcasted_iota(jnp.int32, (rows, rows), 0)
    same = (same == lax.broadcasted_iota(jnp.int32, (rows, rows), 1)).astype(FULL)
    early, extra = out_ref.shape[2], out_ref.shape[2] + conv_ref.shape[2]
    for layer in range(layers):
        total = jnp.sum(refs[layer][...].astype(FULL), axis=0)
        out_ref[layer] = total[:, :early]
        conv_ref[layer] = total[:, early:extra]
        cond_ref[layer] = total[:, extra : extra + mel]
        biases = dot_rows(total[:, extra:], same, precision=lax.Precision.HIGHEST)
        conv_b_ref[layer : layer + 1] = biases[mel : mel + 1]
        out_b_ref[layer : layer + 1] = biases[mel + 1 : mel + 2]


def plain(kernel, operands, outs):
    return pl.pallas_call(
        kernel,
        out_shape=outs,
        compiler_params=pltpu.CompilerParams(vmem_limit_bytes=ROOM_SMALL * MIB),
    )(*operands)


def call(kernel, grid, info, operands, outs, scratch, flops, room):
    arrays = [x if spec else pltpu.with_memory_space_constraint(x, pltpu.VMEM) for x, spec in operands]
    shapes = [x if spec else pltpu.VMEM(x.shape, x.dtype) for x, spec in outs]
    moved = sum(x.size * x.dtype.itemsize for x, spec in (*operands, *outs) if spec)
    return pl.pallas_call(
        kernel,
        grid_spec=pltpu.PrefetchScalarGridSpec(
            num_scalar_prefetch=1,
            grid=(grid,),
            in_specs=[spec or KEPT for _, spec in operands],
            out_specs=[spec or KEPT for _, spec in outs],
            scratch_shapes=scratch,
        ),
        out_shape=shapes,
        compiler_params=pltpu.CompilerParams(
            vmem_limit_bytes=room * MIB, dimension_semantics=("arbitrary",)
        ),
        cost_estimate=pl.CostEstimate(flops=flops, bytes_accessed=moved, transcendentals=0),
    )(info, *arrays)


def shape_of(*shape, dtype=LOW):
    return jax.ShapeDtypeStruct(shape, dtype)


def tiled(width, place=lambda i: i):
    return pl.BlockSpec((TILE, width), lambda i, info: (place(i), 0))


def fixed(*shape, at=(0, 0)):
    return pl.BlockSpec(shape, lambda i, info: at)


KEPT = pl.BlockSpec(memory_space=pltpu.VMEM)


class Wires:
    def __init__(self, dp, cores, channels):
        assert dp % 4 == 0 and cores == 2
        self.rest = dp // 4
        self.devices = dp * 2
        self.rows = channels // self.devices
        self.direct = self.rows % 16 == 0
        self.pieces = 8 if self.direct else 1
        me = lax.axis_index(AXES)
        self.core = me % 2
        self.a = (me // 2) % 2
        self.b = (me // 4) % 2
        every = range(self.devices)
        self.sibling = [(i, i ^ 1) for i in every]
        self.first = [(i, i ^ (4 if i % 2 else 2)) for i in every]
        self.second = [(i, i ^ (2 if i % 2 else 4)) for i in every]
        self.columns = [[rest * 8 + low for rest in range(self.rest)] for low in range(8)]

    def place(self):
        return jnp.stack([self.core, self.a, self.b]).astype(jnp.int32)

    def hop(self, value, pairs):
        return lax.ppermute(value, AXES, pairs)

    def swap_rest(self, blocks):
        return lax.all_to_all(blocks, AXES, 0, 0, tiled=True, axis_index_groups=self.columns)

    def far_hops(self, mine, one, two):
        pieces = [mine, one, two, self.hop(one, self.second)]
        pieces += [self.hop(piece, self.sibling) for piece in pieces]
        return pieces if self.direct else [self.put_in_order(pieces)]

    def put_in_order(self, pieces):
        whole = jnp.zeros((self.rest, 2, 2, 2) + pieces[0].shape[1:], LOW)
        for index, piece in enumerate(pieces):
            source = self.core if index < 4 else 1 - self.core
            first, second = index % 2, (index // 2) % 2
            at_a = self.a ^ jnp.where(source == 0, first, second)
            at_b = self.b ^ jnp.where(source == 0, second, first)
            whole = lax.dynamic_update_slice(
                whole, piece[:, None, None, None], (0, at_b, at_a, source, 0, 0)
            )
        return whole.reshape(-1, pieces[0].shape[2])

    def put_together(self, info_ref, pieces, w_ref):
        if not self.direct:
            w_ref[...] = pieces[0][...]
            return
        core, a, b = info_ref[2], info_ref[3], info_ref[4]
        for index, piece in enumerate(pieces):
            source = core if index < 4 else 1 - core
            first, second = index % 2, (index // 2) % 2
            at_a = a ^ jnp.where(source == 0, first, second)
            at_b = b ^ jnp.where(source == 0, second, first)
            for rest in range(self.rest):
                place = ((rest * 2 + at_b) * 2 + at_a) * 2 + source
                w_ref[rows_of(place, self.rows)] = piece[rest]

    def put_apart(self, info_ref, step, part_ref, here_ref, away_ref):
        if not self.direct:
            here_ref[rows_of(step, part_ref.shape[0])] = part_ref[...]
            return
        core, a, b = info_ref[2], info_ref[3], info_ref[4]
        blocks = part_ref.shape[0] // self.rows
        for block in range(blocks):
            at_b, at_a, owner = (block // 4) % 2, (block // 2) % 2, block % 2
            value = part_ref[block * self.rows : (block + 1) * self.rows]
            first, second = at_a ^ a, at_b ^ b
            if owner:
                first, second = second, first
            rest = step * (blocks // 8) + block // 8

            @pl.when(core == owner)
            def _():
                here_ref[first, second, rest] = value

            @pl.when(core != owner)
            def _():
                away_ref[first, second, rest] = value

    def apart(self, depth):
        if not self.direct:
            return [(shape_of(self.devices * self.rows, depth), None), (shape_of(16, LANES), None)]
        return [(shape_of(2, 2, self.rest, self.rows, depth), None)] * 2

    def by_distance(self, full):
        rows = full.shape[0] // self.devices
        blocks = full.reshape(self.rest, 2, 2, 2, rows, full.shape[1])
        parts = []
        for away in range(2):
            source = self.core ^ away
            for first in range(2):
                for second in range(2):
                    at_a = self.a ^ jnp.where(source == 0, first, second)
                    at_b = self.b ^ jnp.where(source == 0, second, first)
                    parts.append(
                        lax.dynamic_slice(
                            blocks,
                            (0, at_b, at_a, source, 0, 0),
                            (self.rest, 1, 1, 1, rows, full.shape[1]),
                        )[:, 0, 0, 0]
                    )
        return jnp.stack(parts).reshape(2, 2, 2, self.rest, rows, full.shape[1])


def add_low(left, right):
    return (left.astype(FULL) + right.astype(FULL)).astype(LOW)


def per_device(
    dp,
    cores,
    samples,
    mel,
    lengths,
    hops,
    conv_weight,
    cond_weight,
    conv_bias,
    out_weight,
    out_bias,
    grad_out,
    grad_skip,
):
    sample_count, channels = samples.shape[1:]
    frame_count, mel_count = mel.shape[1:]
    layers = conv_weight.shape[0]
    size = Sizes(channels, mel_count)
    gate = size.gate
    wires = Wires(dp, cores, gate)
    assert layers == 2 and sample_count % TILE == 0 and TILE == FIRST_DILATION
    steps = sample_count // TILE
    info = jnp.concatenate([lengths, hops, wires.place()])
    x, go, gs = samples[0], grad_out[0], grad_skip[0]
    mel_table = jnp.concatenate([mel[0], jnp.ones((frame_count, 1), LOW)], axis=1)
    mel_table = jnp.pad(
        mel_table, ((0, LANES - frame_count), (0, size.extra_width - mel_count - 1))
    )

    conv_t, cond_t, out_t = (
        w.swapaxes(1, 2) for w in (conv_weight, cond_weight, out_weight)
    )
    rows = conv_t.shape[1]
    own = plain(
        functools.partial(pack_layers, layers, wires.rest),
        (conv_t, cond_t, conv_bias, out_t, out_bias),
        [shape_of(wires.rest, rows, size.pack)] * layers,
    )
    mine0 = wires.swap_rest(own[0])
    one0, two0 = wires.hop(mine0, wires.first), wires.hop(mine0, wires.second)
    pieces0 = wires.far_hops(mine0, one0, two0)
    mine1 = wires.swap_rest(own[1])
    mine1, *pieces0 = lax.optimization_barrier((mine1, *pieces0))
    one1, two1 = wires.hop(mine1, wires.first), wires.hop(mine1, wires.second)

    table = fixed(LANES, size.extra_width)
    macs = sample_count * channels * channels
    kept = lambda *columns: [(shape_of(sample_count, c), None) for c in columns]
    whole_w = (shape_of(gate, size.pack), None)
    parts = 4
    width = gate // parts
    melg = (shape_of(LANES, size.extra_width, dtype=FULL), table)
    scratch = lambda *shape: pltpu.VMEM(shape, LOW)

    blocked = (shape_of(sample_count, channels), tiled(channels))
    keep = lambda *values: [(value, None) for value in values]

    low1, gated0, slope0, w0 = call(
        functools.partial(forward_0, size, wires),
        steps,
        info,
        [(x, None), (mel_table, table), *keep(*pieces0)],
        [*kept(channels, channels, gate), whole_w],
        [],
        10 * macs,
        ROOM_0,
    )
    one1, two1, low1 = lax.optimization_barrier((one1, two1, low1))
    gated1, pre1, w1, here1, away1, melg1 = call(
        functools.partial(layer_1, size, wires, steps),
        steps + parts,
        info,
        [(low1, None), (mel_table, table), (go, None), (gs, None)]
        + keep(*wires.far_hops(mine1, one1, two1)),
        [
            *kept(channels, gate),
            whole_w,
            *wires.apart(size.pack),
            melg,
        ],
        [
            scratch(sample_count, channels),
            scratch(sample_count, width),
            scratch(sample_count, LANES),
            scratch(width, size.pack),
        ],
        24 * macs,
        ROOM_1,
    )
    if not wires.direct:
        here1, away1 = wires.by_distance(here1)
    came1 = wires.hop(away1, wires.sibling)

    res0, pre0 = call(
        functools.partial(backward_0, size),
        steps,
        info,
        keep(pre1, w1, w0, go, gs, slope0),
        kept(channels, gate),
        [pltpu.VMEM((8, channels), FULL)],
        12 * macs,
        ROOM_2,
    )
    half_shape = shape_of(2, wires.rest, rows, size.pack)
    last_shape = shape_of(wires.rest, rows, size.pack)
    stay1, leave1 = plain(add_and_part, (here1, came1), [half_shape] * 2)
    pre0, stay1, leave1 = lax.optimization_barrier((pre0, stay1, leave1))
    came1 = wires.hop(leave1, wires.first)

    here0, away0, melg0 = call(
        functools.partial(weights_0, size, wires),
        parts,
        info,
        [*keep(pre0, res0, gs, x, gated0), (mel_table, table), (w0, None)],
        [*wires.apart(size.pack), melg],
        [
            scratch(sample_count, LANES),
            scratch(sample_count, width),
            scratch(width, size.pack),
        ],
        12 * macs,
        ROOM_3,
    )
    if not wires.direct:
        here0, away0 = wires.by_distance(here0)
    away0, came1 = lax.optimization_barrier((away0, came1))
    came0 = wires.hop(away0, wires.sibling)
    stay1, leave1 = plain(add_and_part, (stay1, came1), [last_shape] * 2)
    came1 = wires.hop(leave1, wires.second)
    came0, leave1 = lax.optimization_barrier((came0, leave1))
    stay0, leave0 = plain(add_and_part, (here0, came0), [half_shape] * 2)
    pre0, stay0, leave0 = lax.optimization_barrier((pre0, stay0, leave0))
    came0 = wires.hop(leave0, wires.first)

    (samples_grad,) = call(
        functools.partial(samples_gradient, size),
        steps,
        info,
        keep(res0, pre0, w0),
        [(shape_of(sample_count, channels, dtype=FULL), tiled(channels))],
        [],
        8 * macs,
        ROOM_4,
    )
    came1, samples_grad = lax.optimization_barrier((came1, samples_grad))
    parts1 = wires.swap_rest(add_low(stay1, came1))
    stay0, leave0 = plain(add_and_part, (stay0, came0), [last_shape] * 2)
    x, stay0, leave0 = lax.optimization_barrier((x, stay0, leave0))
    came0 = wires.hop(leave0, wires.second)
    residual_out, skip_output_sum = call(
        functools.partial(forward_outputs, size),
        steps,
        info,
        keep(x, gated0, gated1, w0, w1),
        [blocked, blocked],
        [],
        8 * macs,
        ROOM_5,
    )
    came0, residual_out = lax.optimization_barrier((came0, residual_out))
    parts0 = wires.swap_rest(add_low(stay0, came0))
    grads = plain(
        functools.partial(unpack_layers, layers, mel_count),
        (parts0, parts1),
        [
            shape_of(layers, rows, 2 * channels, dtype=FULL),
            shape_of(layers, rows, mel_count, dtype=FULL),
            shape_of(layers, rows, dtype=FULL),
            shape_of(layers, rows, channels, dtype=FULL),
            shape_of(layers, rows, dtype=FULL),
        ],
    )
    mel_grad = (melg0 + melg1)[:frame_count, :mel_count]
    conv_grad, cond_grad, conv_b_grad, out_grad, out_b_grad = grads
    return (
        residual_out[None],
        skip_output_sum[None],
        samples_grad[None],
        mel_grad[None],
        conv_grad.swapaxes(1, 2),
        cond_grad.swapaxes(1, 2),
        conv_b_grad,
        out_grad.swapaxes(1, 2),
        out_b_grad,
    )


def solution(mesh):
    dp, cores = mesh.shape["dp"], mesh.shape["group"]

    def everything(*arrays):
        return per_device(dp, cores, *arrays)

    clips = P(AXES, None, None)
    columns = P(None, None, AXES)
    biases = P(None, AXES)
    return jax.shard_map(
        everything,
        mesh=mesh,
        in_specs=(
            clips, clips, P(AXES), P(AXES), columns, columns, biases, columns, biases, clips, clips,
        ),
        out_specs=(clips, clips, clips, clips, columns, columns, biases, columns, biases),
        check_vma=False,
    )
```

```python
import functools

import jax
import jax.numpy as jnp
from jax import lax
from jax.experimental import pallas as pl
from jax.experimental.pallas import tpu as pltpu
from jax.sharding import PartitionSpec as P

FIRST_DILATION = 512
AXES = ("dp", "group")
LANES = 128
TILE = 512
MIB = 1024 * 1024
HINT = 4
ROOM_0, ROOM_1, ROOM_2, ROOM_3, ROOM_4, ROOM_5, ROOM_SMALL = 8, 13, 6, 8, 8, 8, 12
LOW = jnp.bfloat16
FULL = jnp.float32


def dot(left, right):
    return jnp.dot(left, right, preferred_element_type=FULL)


def dot_cols(left, right, **more):
    return lax.dot_general(
        left, right, (((1,), (1,)), ((), ())), preferred_element_type=FULL, **more
    )


def dot_rows(left, right, **more):
    return lax.dot_general(
        left, right, (((0,), (0,)), ((), ())), preferred_element_type=FULL, **more
    )


class Sizes:
    def __init__(self, channels, mel_count):
        self.channels = channels
        self.gate = 2 * channels
        self.mel = mel_count
        self.early = channels
        self.now = 2 * channels
        self.extra = 3 * channels
        self.extra_width = -(-(mel_count + 2) // LANES) * LANES
        self.pack = self.extra + self.extra_width


def mask_of(info_ref, start, rows):
    places = start + lax.broadcasted_iota(jnp.int32, (rows, 1), 0)
    return (places < info_ref[0]).astype(FULL)


def frames_of(info_ref, start, rows):
    places = start + lax.broadcasted_iota(jnp.int32, (rows, LANES), 0)
    first = lax.broadcasted_iota(jnp.int32, (rows, LANES), 1) * info_ref[1]
    return ((places >= first) & (places < first + info_ref[1])).astype(FULL).astype(LOW)


def masked(value, mask):
    return (value.astype(FULL) * mask).astype(LOW)


def out_bias_row(size, extra):
    column = lax.broadcasted_iota(jnp.int32, (8, size.extra_width), 1)
    pick = (column == size.mel + 1).astype(FULL).astype(LOW)
    return dot_cols(pick, extra)[0:1]


def gates(taps, w_ref, size, side):
    channels = size.channels
    width = channels // 2
    low = slice(side * width, (side + 1) * width)
    high = slice(channels + side * width, channels + (side + 1) * width)
    tangent = jnp.tanh(dot_cols(taps, w_ref[low, size.early :]))
    sig_gate = 0.5 * jnp.tanh(0.5 * dot_cols(taps, w_ref[high, size.early :])) + 0.5
    gated = tangent * sig_gate
    return low, high, gated, sig_gate * (1.0 - tangent * tangent), gated * (1.0 - sig_gate)


def rows_of(step, rows):
    return pl.ds(pl.multiple_of(step * rows, rows), rows)


def forward_0(size, wires, info_ref, x_ref, mel_ref, *refs):
    count = 8 if wires.direct else 1
    pieces, refs = refs[:count], refs[count:]
    low1_ref, gated_ref, slope_ref, w_ref = refs
    step = pl.program_id(0)
    channels = size.channels

    @pl.when(step == 0)
    def _():
        wires.put_together(info_ref, pieces, w_ref)

    tile = rows_of(step, TILE)
    mask = mask_of(info_ref, step * TILE, TILE)
    hidden = x_ref[tile].astype(FULL) * mask
    low = hidden.astype(LOW)
    prev_mask = mask_of(info_ref, (step - 1) * TILE, TILE) * (step > 0).astype(FULL)
    prev = x_ref[rows_of(jnp.maximum(step - 1, 0), TILE)].astype(FULL) * prev_mask
    cond = dot(frames_of(info_ref, step * TILE, TILE), mel_ref[...]).astype(LOW)
    taps = jnp.concatenate([prev.astype(LOW), low, cond], axis=1)
    for side in range(2):
        first, second, gated, slope_a, slope_b = gates(taps, w_ref, size, side)
        gated_ref[tile, first] = gated.astype(LOW)
        slope_ref[tile, first] = slope_a.astype(LOW)
        slope_ref[tile, second] = slope_b.astype(LOW)
    moved = dot_cols(gated_ref[tile], w_ref[:channels, :channels])
    moved = moved + out_bias_row(size, w_ref[:channels, size.extra :])
    low1_ref[tile] = ((hidden + moved) * mask).astype(LOW)


def layer_1(size, wires, steps, info_ref, low1_ref, mel_ref, go_ref, gs_ref, *refs):
    count = 8 if wires.direct else 1
    pieces, refs = refs[:count], refs[count:]
    gated_ref, pre_ref, w_ref, here_ref, away_ref, melg_ref, *scratch = refs
    prev_s, proj_s, frames_s, part_s = scratch
    step = pl.program_id(0)
    channels = size.channels

    @pl.when(step == 0)
    def _():
        wires.put_together(info_ref, pieces, w_ref)
        melg_ref[...] = jnp.zeros_like(melg_ref)

    @pl.when(step < steps)
    def _():
        tile = rows_of(step, TILE)
        mask = mask_of(info_ref, step * TILE, TILE)
        low = low1_ref[tile]
        before = pl.ds(pl.multiple_of(jnp.maximum(step * TILE - 16, 0), 16), 16)
        last = low1_ref[before].astype(FULL)[15:16] * (step > 0).astype(FULL)
        place = lax.broadcasted_iota(jnp.int32, (TILE, 1), 0)
        prev = jnp.where(place == 0, last, pltpu.roll(low.astype(FULL), 1, 0)).astype(LOW)
        frames = frames_of(info_ref, step * TILE, TILE)
        cond = dot(frames, mel_ref[...]).astype(LOW)
        taps = jnp.concatenate([prev, low, cond], axis=1)
        proj = jnp.concatenate([masked(go_ref[tile], mask), masked(gs_ref[tile], mask)], axis=1)
        prev_s[tile] = prev
        frames_s[tile] = frames
        grad_gated = dot(proj, w_ref[:, :channels])
        for side in range(2):
            first, second, gated, slope_a, slope_b = gates(taps, w_ref, size, side)
            gated_ref[tile, first] = gated.astype(LOW)
            pre_ref[tile, first] = (grad_gated[:, first] * slope_a).astype(LOW)
            pre_ref[tile, second] = (grad_gated[:, first] * slope_b).astype(LOW)

    @pl.when(step >= steps)
    def _():
        width = part_s.shape[0]
        part = rows_of(step - steps, width)
        half = channels // width
        mask = mask_of(info_ref, 0, low1_ref.shape[0])

        @pl.when(step < steps + half)
        def _():
            columns = rows_of(jnp.clip(step - steps, 0, half - 1), width)
            proj_s[...] = masked(go_ref[:, columns], mask)

        @pl.when(step >= steps + half)
        def _():
            columns = rows_of(jnp.maximum(step - steps - half, 0), width)
            proj_s[...] = masked(gs_ref[:, columns], mask)

        pre = pre_ref[:, part]
        part_s[:, size.early : size.now] = dot_rows(pre, prev_s[...]).astype(LOW)
        part_s[:, size.now : size.extra] = dot_rows(pre, low1_ref[...]).astype(LOW)
        finish_part(size, pre, proj_s[...], frames_s, gated_ref, mel_ref, w_ref[part, size.extra :], melg_ref, part_s)
        wires.put_apart(info_ref, step - steps, part_s, here_ref, away_ref)

def in_two(value):
    high = value.astype(LOW)
    return high, (value - high.astype(FULL)).astype(LOW)


def finish_part(size, pre, proj, frames_ref, gated_ref, mel_ref, cond_weight, melg_ref, part_ref):
    sums = in_two(dot_rows(frames_ref[...], pre))
    extra = sum(dot_rows(half, mel_ref[...]) for half in sums)
    melg_ref[...] += sum(dot(half, cond_weight) for half in sums)
    total = jnp.sum(proj.astype(FULL), axis=0, keepdims=True)
    bias = jnp.broadcast_to(total, (LANES, total.shape[1])).T[:, 0:1]
    column = lax.broadcasted_iota(jnp.int32, extra.shape, 1)
    part_ref[:, size.extra :] = jnp.where(column == size.mel + 1, bias, extra).astype(LOW)
    part_ref[:, : size.channels] = dot_rows(proj, gated_ref[...]).astype(LOW)


def backward_0(size, info_ref, pre1_ref, w1_ref, w0_ref, go_ref, gs_ref, slope_ref, res_ref, pre0_ref, carry_ref):
    step = pl.program_id(0)
    channels = size.channels
    index = pl.num_programs(0) - 1 - step
    tile = rows_of(index, TILE)
    mask = mask_of(info_ref, index * TILE, TILE)

    @pl.when(step == 0)
    def _():
        carry_ref[...] = jnp.zeros_like(carry_ref)

    pre1 = pre1_ref[tile]
    early = dot(pre1, w1_ref[:, size.early : size.now])
    place = lax.broadcasted_iota(jnp.int32, (TILE, 1), 0)
    later = jnp.where(place == TILE - 1, carry_ref[0:1], pltpu.roll(early, TILE - 1, 0))
    carry_ref[...] = early[:8]
    now = dot(pre1, w1_ref[:, size.now : size.extra])
    res = ((go_ref[tile].astype(FULL) * mask + now + later) * mask).astype(LOW)
    res_ref[tile] = res
    proj = jnp.concatenate([res, masked(gs_ref[tile], mask)], axis=1)
    grad_gated = dot(proj, w0_ref[:, :channels])
    for half in (slice(0, channels), slice(channels, 2 * channels)):
        pre0_ref[tile, half] = (grad_gated * slope_ref[tile, half].astype(FULL)).astype(LOW)


def weights_0(size, wires, info_ref, pre_ref, res_ref, gs_ref, x_ref, gated_ref, mel_ref, w_ref, here_ref, away_ref, melg_ref, frames_s, proj_s, part_s):
    step = pl.program_id(0)
    samples = x_ref.shape[0]

    @pl.when(step == 0)
    def _():
        frames_s[...] = frames_of(info_ref, 0, samples)
        melg_ref[...] = jnp.zeros_like(melg_ref)

    width = part_s.shape[0]
    half = pl.num_programs(0) // 2
    part = rows_of(step, width)

    @pl.when(step < half)
    def _():
        proj_s[...] = res_ref[:, rows_of(jnp.minimum(step, half - 1), width)]

    @pl.when(step >= half)
    def _():
        proj_s[...] = masked(
            gs_ref[:, rows_of(jnp.maximum(step - half, 0), width)], mask_of(info_ref, 0, samples)
        )

    pre = pre_ref[:, part]
    shift = FIRST_DILATION
    early = dot_rows(pre[shift:], x_ref[: samples - shift])
    part_s[:, size.early : size.now] = early.astype(LOW)
    part_s[:, size.now : size.extra] = dot_rows(pre, x_ref[...]).astype(LOW)
    finish_part(size, pre, proj_s[...], frames_s, gated_ref, mel_ref, w_ref[part, size.extra :], melg_ref, part_s)
    wires.put_apart(info_ref, step, part_s, here_ref, away_ref)


def samples_gradient(size, info_ref, res_ref, pre_ref, w0_ref, sg_ref):
    step = pl.program_id(0)
    tile = rows_of(step, TILE)
    grad = res_ref[tile].astype(FULL) + dot(pre_ref[tile], w0_ref[:, size.now : size.extra])
    after = rows_of(jnp.minimum(step + 1, pl.num_programs(0) - 1), TILE)
    later = dot(pre_ref[after], w0_ref[:, size.early : size.now])
    grad = grad + jnp.where(step < pl.num_programs(0) - 1, later, 0.0)
    sg_ref[...] = grad * mask_of(info_ref, step * TILE, TILE)


def forward_outputs(size, info_ref, x_ref, gated0_ref, gated1_ref, w0_ref, w1_ref, res_ref, skip_ref):
    step = pl.program_id(0)
    tile = rows_of(step, TILE)
    mask = mask_of(info_ref, step * TILE, TILE)
    channels = size.channels
    gated = jnp.concatenate([gated0_ref[tile], gated1_ref[tile]], axis=1)

    def projected(rows):
        both = jnp.concatenate([w0_ref[rows, :channels], w1_ref[rows, :channels]], axis=1)
        bias = out_bias_row(size, w0_ref[rows, size.extra :])
        return dot_cols(gated, both) + bias + out_bias_row(size, w1_ref[rows, size.extra :])

    res = projected(slice(0, channels))
    res_ref[...] = ((x_ref[tile].astype(FULL) + res) * mask).astype(LOW)
    skip_ref[...] = (projected(slice(channels, 2 * channels)) * mask).astype(LOW)


def add_and_part(left_ref, right_ref, *refs):
    for index, ref in enumerate(refs):
        ref[...] = add_low(left_ref[index], right_ref[index])


def put_side_by_side(*refs):
    for index, ref in enumerate(refs[:-1]):
        refs[-1][index] = ref[...]


def pack_layers(layers, *refs):
    sources, packs, kept = refs[:5], refs[5 : 5 + layers], refs[5 + layers : 10 + layers]
    sems = refs[-1]
    copies = [
        pltpu.make_async_copy(source, to, sems.at[index])
        for index, (source, to) in enumerate(zip(sources, kept))
    ]
    for copy in copies:
        copy.start()
    for copy in copies:
        copy.wait()
    conv_ref, cond_ref, conv_b_ref, out_ref, out_b_ref = kept
    rows = conv_ref.shape[1]
    same = lax.broadcasted_iota(jnp.int32, (rows, rows), 0)
    same = (same == lax.broadcasted_iota(jnp.int32, (rows, rows), 1)).astype(FULL).astype(LOW)
    biases = dot_cols(same, jnp.concatenate([conv_b_ref[...], out_b_ref[...]], axis=0))
    early, extra = out_ref.shape[2], out_ref.shape[2] + conv_ref.shape[2]
    mel = cond_ref.shape[2]
    for layer, to_ref in enumerate(packs):
        width = to_ref.shape[1] - extra
        place = lax.broadcasted_iota(jnp.int32, (rows, width), 1)
        cond = jnp.concatenate(
            [cond_ref[layer].astype(FULL), jnp.zeros((rows, width - mel), FULL)], axis=1
        )
        cond = jnp.where(place == mel, biases[:, layer : layer + 1], cond)
        cond = jnp.where(place == mel + 1, biases[:, layers + layer : layers + layer + 1], cond)
        to_ref[:, :early] = out_ref[layer]
        to_ref[:, early:extra] = conv_ref[layer]
        to_ref[:, extra:] = cond.astype(LOW)


def unpack_layers(layers, mel, *refs):
    conv_ref, cond_ref, conv_b_ref, out_ref, out_b_ref = refs[-5:]
    count = (len(refs) - 5) // layers
    rows = conv_ref.shape[1]
    same = lax.broadcasted_iota(jnp.int32, (rows, rows), 0)
    same = (same == lax.broadcasted_iota(jnp.int32, (rows, rows), 1)).astype(FULL)
    early, extra = out_ref.shape[2], out_ref.shape[2] + conv_ref.shape[2]
    for layer in range(layers):
        total = sum(ref[...].astype(FULL) for ref in refs[layer * count : (layer + 1) * count])
        out_ref[layer] = total[:, :early]
        conv_ref[layer] = total[:, early:extra]
        cond_ref[layer] = total[:, extra : extra + mel]
        biases = dot_rows(total[:, extra:], same, precision=lax.Precision.HIGHEST)
        conv_b_ref[layer : layer + 1] = biases[mel : mel + 1]
        out_b_ref[layer : layer + 1] = biases[mel + 1 : mel + 2]


def plain(kernel, operands, outs):
    return pl.pallas_call(
        kernel,
        out_shape=outs,
        compiler_params=pltpu.CompilerParams(vmem_limit_bytes=ROOM_SMALL * MIB),
    )(*operands)


def call(kernel, grid, info, operands, outs, scratch, flops, room):
    arrays = [x if spec else pltpu.with_memory_space_constraint(x, pltpu.VMEM) for x, spec in operands]
    shapes = [x if spec else pltpu.VMEM(x.shape, x.dtype) for x, spec in outs]
    moved = sum(x.size * x.dtype.itemsize for x, spec in (*operands, *outs) if spec)
    return pl.pallas_call(
        kernel,
        grid_spec=pltpu.PrefetchScalarGridSpec(
            num_scalar_prefetch=1,
            grid=(grid,),
            in_specs=[spec or KEPT for _, spec in operands],
            out_specs=[spec or KEPT for _, spec in outs],
            scratch_shapes=scratch,
        ),
        out_shape=shapes,
        compiler_params=pltpu.CompilerParams(
            vmem_limit_bytes=room * MIB, dimension_semantics=("arbitrary",)
        ),
        cost_estimate=pl.CostEstimate(flops=flops // HINT, bytes_accessed=moved // HINT, transcendentals=0),
    )(info, *arrays)


def shape_of(*shape, dtype=LOW):
    return jax.ShapeDtypeStruct(shape, dtype)


def tiled(width, place=lambda i: i):
    return pl.BlockSpec((TILE, width), lambda i, info: (place(i), 0))


def fixed(*shape, at=(0, 0)):
    return pl.BlockSpec(shape, lambda i, info: at)


KEPT = pl.BlockSpec(memory_space=pltpu.VMEM)


class Wires:
    def __init__(self, dp, cores, channels):
        self.rest = dp // 4
        assert dp == self.rest * 4 and self.rest & (self.rest - 1) == 0 and cores == 2
        self.devices = dp * 2
        self.rows = channels // self.devices
        self.direct = self.rows % 16 == 0
        self.dp = lax.axis_index(AXES[0])
        self.core = lax.axis_index(AXES[1])
        every = range(self.devices)
        self.sibling = [(i, i ^ 1) for i in every]
        self.first = [(i, i ^ (4 if i % 2 else 2)) for i in every]
        self.second = [(i, i ^ (2 if i % 2 else 4)) for i in every]

    def along_rest(self, distance):
        return [(i, i ^ (8 * distance)) for i in range(self.devices)]

    def hop(self, value, pairs):
        return lax.ppermute(value, AXES, pairs)

    def spread(self, blocks):
        return [blocks[0]] + [
            self.hop(blocks[k], self.along_rest(k)) for k in range(1, self.rest)
        ]

    def far_hops(self, mine, one, two):
        pieces = [mine, one, two, self.hop(one, self.second)]
        pieces += [self.hop(piece, self.sibling) for piece in pieces]
        return pieces if self.direct else [self.put_in_order(pieces)]

    def put_in_order(self, pieces):
        whole = jnp.zeros((self.rest, 2, 2, 2) + pieces[0].shape[1:], LOW)
        order = jnp.arange(self.rest) ^ (self.dp >> 2)
        for index, piece in enumerate(pieces):
            source = self.core ^ (index // 4)
            at_a, at_b = turned(self.dp, source, index % 2, (index // 2) % 2)
            whole = lax.dynamic_update_slice(
                whole, piece[order][:, None, None, None], (0, at_b, at_a, source, 0, 0)
            )
        return whole.reshape(-1, pieces[0].shape[2])

    def put_together(self, info_ref, pieces, w_ref):
        if not self.direct:
            w_ref[...] = pieces[0][...]
            return
        dp, core = info_ref[2], info_ref[3]
        for index, piece in enumerate(pieces):
            source = core ^ (index // 4)
            at_a, at_b = turned(dp, source, index % 2, (index // 2) % 2)
            for distance in range(self.rest):
                place = ((((dp >> 2) ^ distance) * 2 + at_b) * 2 + at_a) * 2 + source
                w_ref[rows_of(place, self.rows)] = piece[distance]

    def put_apart(self, info_ref, step, part_ref, here_ref, away_ref):
        if not self.direct:
            here_ref[rows_of(step, part_ref.shape[0])] = part_ref[...]
            return
        dp, core = info_ref[2], info_ref[3]
        blocks = part_ref.shape[0] // self.rows
        for block in range(blocks):
            at_b, at_a, owner = (block // 4) % 2, (block // 2) % 2, block % 2
            value = part_ref[block * self.rows : (block + 1) * self.rows]
            first, second = at_a ^ (dp & 1), at_b ^ ((dp >> 1) & 1)
            if owner:
                first, second = second, first
            distance = (step * (blocks // 8) + block // 8) ^ (dp >> 2)

            @pl.when(core == owner)
            def _():
                here_ref[first, second, distance] = value

            @pl.when(core != owner)
            def _():
                away_ref[first, second, distance] = value

    def apart(self, depth):
        if not self.direct:
            return [(shape_of(self.devices * self.rows, depth), None), (shape_of(16, LANES), None)]
        return [(shape_of(2, 2, self.rest, self.rows, depth), None)] * 2

    def by_distance(self, full):
        rows = full.shape[0] // self.devices
        blocks = full.reshape(self.rest, 2, 2, 2, rows, full.shape[1])
        blocks = blocks[jnp.arange(self.rest) ^ (self.dp >> 2)]
        parts = []
        for away in range(2):
            source = self.core ^ away
            for first in range(2):
                for second in range(2):
                    at_a, at_b = turned(self.dp, source, first, second)
                    parts.append(
                        lax.dynamic_slice(
                            blocks,
                            (0, at_b, at_a, source, 0, 0),
                            (self.rest, 1, 1, 1, rows, full.shape[1]),
                        )[:, 0, 0, 0]
                    )
        return jnp.stack(parts).reshape(2, 2, 2, self.rest, rows, full.shape[1])


def turned(dp, owner, first, second):
    along_a = jnp.where(owner == 0, first, second)
    along_b = jnp.where(owner == 0, second, first)
    return (dp & 1) ^ along_a, ((dp >> 1) & 1) ^ along_b


def add_low(left, right):
    return (left.astype(FULL) + right.astype(FULL)).astype(LOW)


def per_device(
    dp,
    cores,
    samples,
    mel,
    lengths,
    hops,
    conv_weight,
    cond_weight,
    conv_bias,
    out_weight,
    out_bias,
    grad_out,
    grad_skip,
):
    sample_count, channels = samples.shape[1:]
    frame_count, mel_count = mel.shape[1:]
    layers = conv_weight.shape[0]
    size = Sizes(channels, mel_count)
    gate = size.gate
    wires = Wires(dp, cores, gate)
    assert layers == 2 and sample_count % TILE == 0 and TILE == FIRST_DILATION
    steps = sample_count // TILE
    where = jnp.stack([wires.dp, wires.core]).astype(jnp.int32)
    info = jnp.concatenate([lengths, hops, where])
    x, go, gs = samples[0], grad_out[0], grad_skip[0]
    mel_table = jnp.concatenate([mel[0], jnp.ones((frame_count, 1), LOW)], axis=1)
    mel_table = jnp.pad(
        mel_table, ((0, LANES - frame_count), (0, size.extra_width - mel_count - 1))
    )

    conv_t, cond_t, out_t = (
        w.swapaxes(1, 2) for w in (conv_weight, cond_weight, out_weight)
    )
    rows = conv_t.shape[1]
    sources = (conv_t, cond_t, conv_bias, out_t, out_bias)
    own = pl.pallas_call(
        functools.partial(pack_layers, layers),
        in_specs=[pl.BlockSpec(memory_space=pl.ANY)] * len(sources),
        out_shape=[shape_of(rows, size.pack)] * layers,
        scratch_shapes=[pltpu.VMEM(source.shape, LOW) for source in sources]
        + [pltpu.SemaphoreType.DMA((len(sources),))],
        compiler_params=pltpu.CompilerParams(vmem_limit_bytes=ROOM_SMALL * MIB),
    )(*(pltpu.with_memory_space_constraint(source, pltpu.HBM) for source in sources))
    last_shape = shape_of(wires.rest, rows, size.pack)
    half_shape = shape_of(2, wires.rest, rows, size.pack)
    blocks_shape = [shape_of(rows, size.pack)] * wires.rest
    side_by_side = lambda blocks: plain(put_side_by_side, blocks, [last_shape])[0]
    near0 = wires.spread([own[0]] * wires.rest)
    near1 = wires.spread([own[1]] * wires.rest)
    mine0 = side_by_side(near0)
    one0, two0 = wires.hop(mine0, wires.first), wires.hop(mine0, wires.second)
    one0, two0, *near1 = lax.optimization_barrier((one0, two0, *near1))
    pieces0 = wires.far_hops(mine0, one0, two0)
    mine1 = side_by_side(near1)
    one1, two1 = wires.hop(mine1, wires.first), wires.hop(mine1, wires.second)

    table = fixed(LANES, size.extra_width)
    macs = sample_count * channels * channels
    kept = lambda *columns: [(shape_of(sample_count, c), None) for c in columns]
    whole_w = (shape_of(gate, size.pack), None)
    parts = 4
    width = gate // parts
    melg = (shape_of(LANES, size.extra_width, dtype=FULL), table)
    scratch = lambda *shape: pltpu.VMEM(shape, LOW)

    blocked = (shape_of(sample_count, channels), tiled(channels))
    keep = lambda *values: [(value, None) for value in values]

    low1, gated0, slope0, w0 = call(
        functools.partial(forward_0, size, wires),
        steps,
        info,
        [(x, None), (mel_table, table), *keep(*pieces0)],
        [*kept(channels, channels, gate), whole_w],
        [],
        10 * macs,
        ROOM_0,
    )
    one1, two1, low1 = lax.optimization_barrier((one1, two1, low1))
    gated1, pre1, w1, here1, away1, melg1 = call(
        functools.partial(layer_1, size, wires, steps),
        steps + parts,
        info,
        [(low1, None), (mel_table, table), (go, None), (gs, None)]
        + keep(*wires.far_hops(mine1, one1, two1)),
        [
            *kept(channels, gate),
            whole_w,
            *wires.apart(size.pack),
            melg,
        ],
        [
            scratch(sample_count, channels),
            scratch(sample_count, width),
            scratch(sample_count, LANES),
            scratch(width, size.pack),
        ],
        24 * macs,
        ROOM_1,
    )
    if not wires.direct:
        here1, away1 = wires.by_distance(here1)
    came1 = wires.hop(away1, wires.sibling)

    res0, pre0 = call(
        functools.partial(backward_0, size),
        steps,
        info,
        keep(pre1, w1, w0, go, gs, slope0),
        kept(channels, gate),
        [pltpu.VMEM((8, channels), FULL)],
        12 * macs,
        ROOM_2,
    )
    stay1, leave1 = plain(add_and_part, (here1, came1), [half_shape] * 2)
    pre0, stay1, leave1 = lax.optimization_barrier((pre0, stay1, leave1))
    came1 = wires.hop(leave1, wires.first)

    here0, away0, melg0 = call(
        functools.partial(weights_0, size, wires),
        parts,
        info,
        [*keep(pre0, res0, gs, x, gated0), (mel_table, table), (w0, None)],
        [*wires.apart(size.pack), melg],
        [
            scratch(sample_count, LANES),
            scratch(sample_count, width),
            scratch(width, size.pack),
        ],
        12 * macs,
        ROOM_3,
    )
    if not wires.direct:
        here0, away0 = wires.by_distance(here0)
    away0, came1 = lax.optimization_barrier((away0, came1))
    came0 = wires.hop(away0, wires.sibling)
    stay1, leave1 = plain(add_and_part, (stay1, came1), [last_shape] * 2)
    came1 = wires.hop(leave1, wires.second)
    came0, leave1 = lax.optimization_barrier((came0, leave1))
    stay0, leave0 = plain(add_and_part, (here0, came0), [half_shape] * 2)
    pre0, stay0, leave0 = lax.optimization_barrier((pre0, stay0, leave0))
    came0 = wires.hop(leave0, wires.first)

    (samples_grad,) = call(
        functools.partial(samples_gradient, size),
        steps,
        info,
        keep(res0, pre0, w0),
        [(shape_of(sample_count, channels, dtype=FULL), tiled(channels))],
        [],
        8 * macs,
        ROOM_4,
    )
    came0, came1, samples_grad = lax.optimization_barrier((came0, came1, samples_grad))
    parts1 = wires.spread(plain(add_and_part, (stay1, came1), blocks_shape))
    stay0, leave0 = plain(add_and_part, (stay0, came0), [last_shape] * 2)
    x, stay0, leave0 = lax.optimization_barrier((x, stay0, leave0))
    came0 = wires.hop(leave0, wires.second)
    residual_out, skip_output_sum = call(
        functools.partial(forward_outputs, size),
        steps,
        info,
        keep(x, gated0, gated1, w0, w1),
        [blocked, blocked],
        [],
        8 * macs,
        ROOM_5,
    )
    came0, residual_out = lax.optimization_barrier((came0, residual_out))
    parts0 = wires.spread(plain(add_and_part, (stay0, came0), blocks_shape))
    grads = plain(
        functools.partial(unpack_layers, layers, mel_count),
        (*parts0, *parts1),
        [
            shape_of(layers, rows, 2 * channels, dtype=FULL),
            shape_of(layers, rows, mel_count, dtype=FULL),
            shape_of(layers, rows, dtype=FULL),
            shape_of(layers, rows, channels, dtype=FULL),
            shape_of(layers, rows, dtype=FULL),
        ],
    )
    mel_grad = (melg0 + melg1)[:frame_count, :mel_count]
    conv_grad, cond_grad, conv_b_grad, out_grad, out_b_grad = grads
    return (
        residual_out[None],
        skip_output_sum[None],
        samples_grad[None],
        mel_grad[None],
        conv_grad.swapaxes(1, 2),
        cond_grad.swapaxes(1, 2),
        conv_b_grad,
        out_grad.swapaxes(1, 2),
        out_b_grad,
    )


def solution(mesh):
    dp, cores = mesh.shape["dp"], mesh.shape["group"]

    def everything(*arrays):
        return per_device(dp, cores, *arrays)

    clips = P(AXES, None, None)
    columns = P(None, None, AXES)
    biases = P(None, AXES)
    return jax.shard_map(
        everything,
        mesh=mesh,
        in_specs=(
            clips, clips, P(AXES), P(AXES), columns, columns, biases, columns, biases, clips, clips,
        ),
        out_specs=(clips, clips, clips, clips, columns, columns, biases, columns, biases),
        check_vma=False,
    )
```

```python
import functools

import jax
import jax.numpy as jnp
from jax import lax
from jax.experimental import pallas as pl
from jax.experimental.pallas import tpu as pltpu
from jax.sharding import PartitionSpec as P

FIRST_DILATION = 512
AXES = ("dp", "group")
LANES = 128
TILE = 512
PART = 256
MIB = 1024 * 1024
HINT = 4
ROOM_0, ROOM_1, ROOM_2, ROOM_3, ROOM_4, ROOM_5, ROOM_SMALL = 8, 13, 6, 8, 8, 8, 12
LOW = jnp.bfloat16
FULL = jnp.float32


def dot(left, right):
    return jnp.dot(left, right, preferred_element_type=FULL)


def dot_cols(left, right, **more):
    return lax.dot_general(
        left, right, (((1,), (1,)), ((), ())), preferred_element_type=FULL, **more
    )


def dot_rows(left, right, **more):
    return lax.dot_general(
        left, right, (((0,), (0,)), ((), ())), preferred_element_type=FULL, **more
    )


class Sizes:
    def __init__(self, channels, mel_count):
        self.channels = channels
        self.gate = 2 * channels
        self.mel = mel_count
        self.early = channels
        self.now = 2 * channels
        self.extra = 3 * channels
        self.extra_width = -(-(mel_count + 2) // LANES) * LANES
        self.pack = self.extra + self.extra_width


def mask_of(info_ref, start, rows):
    places = start + lax.broadcasted_iota(jnp.int32, (rows, 1), 0)
    return (places < info_ref[0]).astype(FULL)


def frames_of(info_ref, start, rows):
    places = start + lax.broadcasted_iota(jnp.int32, (rows, LANES), 0)
    first = lax.broadcasted_iota(jnp.int32, (rows, LANES), 1) * info_ref[1]
    return ((places >= first) & (places < first + info_ref[1])).astype(FULL).astype(LOW)


def masked(value, mask):
    return (value.astype(FULL) * mask).astype(LOW)


def out_bias_row(size, extra):
    column = lax.broadcasted_iota(jnp.int32, (8, size.extra_width), 1)
    pick = (column == size.mel + 1).astype(FULL).astype(LOW)
    return dot_cols(pick, extra)[0:1]


def gates(taps, w_ref, size, side):
    channels = size.channels
    width = channels // 2
    low = slice(side * width, (side + 1) * width)
    high = slice(channels + side * width, channels + (side + 1) * width)
    tangent = jnp.tanh(dot_cols(taps, w_ref[low, size.early :]))
    sig_gate = 0.5 * jnp.tanh(0.5 * dot_cols(taps, w_ref[high, size.early :])) + 0.5
    gated = tangent * sig_gate
    return low, high, gated, sig_gate * (1.0 - tangent * tangent), gated * (1.0 - sig_gate)


def rows_of(step, rows):
    return pl.ds(pl.multiple_of(step * rows, rows), rows)


def prepare(size, info_ref, x_ref, go_ref, gs_ref, mel_ref, low0_ref, cond_ref, frames_ref, proj1_ref):
    step = pl.program_id(0)
    tile = rows_of(step, TILE)
    mask = mask_of(info_ref, step * TILE, TILE)
    low0_ref[tile] = masked(x_ref[...], mask)
    proj1_ref[tile, : size.channels] = masked(go_ref[...], mask)
    proj1_ref[tile, size.channels :] = masked(gs_ref[...], mask)
    frames = frames_of(info_ref, step * TILE, TILE)
    frames_ref[tile] = frames
    cond_ref[tile] = dot(frames, mel_ref[...]).astype(LOW)


def forward_0(size, wires, info_ref, low0_ref, cond_ref, *refs):
    count = 8 if wires.direct else 1
    pieces, refs = refs[:count], refs[count:]
    low1_ref, prev1_ref, gated_ref, slope_ref, w_ref, bias_s, carry_s = refs
    step = pl.program_id(0)
    channels = size.channels

    @pl.when(step == 0)
    def _():
        wires.put_together(info_ref, pieces, w_ref)
        bias_s[...] = out_bias_row(size, w_ref[:channels, size.extra :])
        carry_s[...] = jnp.zeros_like(carry_s)

    tile = rows_of(step, TILE)
    mask = mask_of(info_ref, step * TILE, TILE)
    low = low0_ref[tile]
    before = low0_ref[rows_of(jnp.maximum(step - 1, 0), TILE)]
    prev = jnp.where(step > 0, before, jnp.zeros_like(before))
    taps = jnp.concatenate([prev, low, cond_ref[tile]], axis=1)
    for side in range(2):
        first, second, gated, slope_a, slope_b = gates(taps, w_ref, size, side)
        gated_ref[tile, first] = gated.astype(LOW)
        slope_ref[tile, first] = slope_a.astype(LOW)
        slope_ref[tile, second] = slope_b.astype(LOW)
    moved = dot_cols(gated_ref[tile], w_ref[:channels, :channels])
    low = ((low.astype(FULL) + moved + bias_s[...]) * mask).astype(LOW)
    low1_ref[tile] = low
    wide = low.astype(FULL)
    place = lax.broadcasted_iota(jnp.int32, (TILE, 1), 0)
    prev1_ref[tile] = jnp.where(place == 0, carry_s[7:8], pltpu.roll(wide, 1, 0)).astype(LOW)
    carry_s[...] = wide[TILE - 8 :]


def layer_1(size, wires, steps, info_ref, low_ref, prev_ref, cond_ref, frames_ref, proj_ref, mel_ref, *refs):
    count = 8 if wires.direct else 1
    pieces, refs = refs[:count], refs[count:]
    gated_ref, pre_ref, w_ref, here_ref, away_ref, melg_ref = refs
    step = pl.program_id(0)
    channels = size.channels

    @pl.when(step == 0)
    def _():
        wires.put_together(info_ref, pieces, w_ref)
        melg_ref[...] = jnp.zeros_like(melg_ref)

    @pl.when(step < steps)
    def _():
        tile = rows_of(step, TILE)
        taps = jnp.concatenate([prev_ref[tile], low_ref[tile], cond_ref[tile]], axis=1)
        grad_gated = dot(proj_ref[tile], w_ref[:, :channels])
        for side in range(2):
            first, second, gated, slope_a, slope_b = gates(taps, w_ref, size, side)
            gated_ref[tile, first] = gated.astype(LOW)
            pre_ref[tile, first] = (grad_gated[:, first] * slope_a).astype(LOW)
            pre_ref[tile, second] = (grad_gated[:, first] * slope_b).astype(LOW)

    @pl.when(step >= steps)
    def _():
        part = rows_of(step - steps, PART)
        pre = pre_ref[:, part]
        proj = proj_ref[:, part]
        grads = [
            dot_rows(proj, gated_ref[...]),
            dot_rows(pre, prev_ref[...]),
            dot_rows(pre, low_ref[...]),
            extra_grads(size, pre, proj, frames_ref, mel_ref, w_ref[part, size.extra :], melg_ref),
        ]
        wires.put_apart(info_ref, step - steps, grads, here_ref, away_ref)


def in_two(value):
    high = value.astype(LOW)
    return high, (value - high.astype(FULL)).astype(LOW)


def extra_grads(size, pre, proj, frames_ref, mel_ref, cond_weight, melg_ref):
    sums = in_two(dot_rows(pre, frames_ref[...]))
    extra = sum(dot(half, mel_ref[...]) for half in sums)
    melg_ref[...] += sum(dot_rows(half, cond_weight) for half in sums)
    total = jnp.sum(proj.astype(FULL), axis=0, keepdims=True)
    bias = jnp.broadcast_to(total, (LANES, total.shape[1])).T[:, 0:1]
    column = lax.broadcasted_iota(jnp.int32, extra.shape, 1)
    return jnp.where(column == size.mel + 1, bias, extra)


def backward_0(size, info_ref, pre1_ref, w1_ref, w0_ref, proj1_ref, slope_ref, proj_ref, pre0_ref, carry_ref):
    step = pl.program_id(0)
    channels = size.channels
    index = pl.num_programs(0) - 1 - step
    tile = rows_of(index, TILE)
    mask = mask_of(info_ref, index * TILE, TILE)

    @pl.when(step == 0)
    def _():
        carry_ref[...] = jnp.zeros_like(carry_ref)

    pre1 = pre1_ref[tile]
    early = dot(pre1, w1_ref[:, size.early : size.now])
    place = lax.broadcasted_iota(jnp.int32, (TILE, 1), 0)
    later = jnp.where(place == TILE - 1, carry_ref[0:1], pltpu.roll(early, TILE - 1, 0))
    carry_ref[...] = early[:8]
    now = dot(pre1, w1_ref[:, size.now : size.extra])
    res = ((proj1_ref[tile, :channels].astype(FULL) + now + later) * mask).astype(LOW)
    proj = jnp.concatenate([res, proj1_ref[tile, channels:]], axis=1)
    proj_ref[tile] = proj
    grad_gated = dot(proj, w0_ref[:, :channels])
    for half in (slice(0, channels), slice(channels, 2 * channels)):
        pre0_ref[tile, half] = (grad_gated * slope_ref[tile, half].astype(FULL)).astype(LOW)


def weights_0(size, wires, info_ref, pre_ref, proj_ref, x_ref, gated_ref, frames_ref, mel_ref, w_ref, here_ref, away_ref, melg_ref):
    step = pl.program_id(0)

    @pl.when(step == 0)
    def _():
        melg_ref[...] = jnp.zeros_like(melg_ref)

    part = rows_of(step, PART)
    pre = pre_ref[:, part]
    proj = proj_ref[:, part]
    shift = FIRST_DILATION
    grads = [
        dot_rows(proj, gated_ref[...]),
        dot_rows(pre[shift:], x_ref[: x_ref.shape[0] - shift]),
        dot_rows(pre, x_ref[...]),
        extra_grads(size, pre, proj, frames_ref, mel_ref, w_ref[part, size.extra :], melg_ref),
    ]
    wires.put_apart(info_ref, step, grads, here_ref, away_ref)


def samples_gradient(size, info_ref, proj_ref, pre_ref, w0_ref, sg_ref):
    step = pl.program_id(0)
    tile = rows_of(step, TILE)
    grad = proj_ref[tile, : size.channels].astype(FULL) + dot(pre_ref[tile], w0_ref[:, size.now : size.extra])
    after = rows_of(jnp.minimum(step + 1, pl.num_programs(0) - 1), TILE)
    later = dot(pre_ref[after], w0_ref[:, size.early : size.now])
    grad = grad + jnp.where(step < pl.num_programs(0) - 1, later, 0.0)
    sg_ref[...] = grad * mask_of(info_ref, step * TILE, TILE)


def forward_outputs(size, info_ref, low1_ref, gated0_ref, gated1_ref, w0_ref, w1_ref, res_ref, skip_ref, bias_s):
    step = pl.program_id(0)
    channels = size.channels

    @pl.when(step == 0)
    def _():
        bias_s[...] = out_bias_row(size, w1_ref[:, size.extra :])
        bias_s[:, channels:] += out_bias_row(size, w0_ref[channels:, size.extra :])

    tile = rows_of(step, TILE)
    mask = mask_of(info_ref, step * TILE, TILE)
    res = dot_cols(gated1_ref[tile], w1_ref[:channels, :channels]) + bias_s[:, :channels]
    res_ref[...] = ((low1_ref[tile].astype(FULL) + res) * mask).astype(LOW)
    skip = dot_cols(gated0_ref[tile], w0_ref[channels:, :channels])
    skip = skip + dot_cols(gated1_ref[tile], w1_ref[channels:, :channels])
    skip_ref[...] = ((skip + bias_s[:, channels:]) * mask).astype(LOW)


def add_and_part(left_ref, right_ref, *refs):
    for index, ref in enumerate(refs):
        ref[...] = add_low(left_ref[index], right_ref[index])


def mel_rows(mel_ref, table_ref, wide_s):
    frames, mel = mel_ref.shape
    wide_s[...] = jnp.zeros_like(wide_s)
    wide_s[:frames, :mel] = mel_ref[...].astype(FULL)
    wide_s[:frames, mel : mel + 1] = jnp.ones((frames, 1), FULL)
    table_ref[...] = wide_s[...].astype(LOW)


def put_side_by_side(*refs):
    for index, ref in enumerate(refs[:-1]):
        refs[-1][index] = ref[...]


def pack_layers(layers, *refs):
    sources, packs, kept = refs[:5], refs[5 : 5 + layers], refs[5 + layers : 10 + layers]
    sems = refs[-1]
    copies = [
        pltpu.make_async_copy(source, to, sems.at[index])
        for index, (source, to) in enumerate(zip(sources, kept))
    ]
    for copy in copies:
        copy.start()
    for copy in copies:
        copy.wait()
    conv_ref, cond_ref, conv_b_ref, out_ref, out_b_ref = kept
    rows = conv_ref.shape[1]
    same = lax.broadcasted_iota(jnp.int32, (rows, rows), 0)
    same = (same == lax.broadcasted_iota(jnp.int32, (rows, rows), 1)).astype(FULL).astype(LOW)
    biases = dot_cols(same, jnp.concatenate([conv_b_ref[...], out_b_ref[...]], axis=0))
    early, extra = out_ref.shape[2], out_ref.shape[2] + conv_ref.shape[2]
    mel = cond_ref.shape[2]
    for layer, to_ref in enumerate(packs):
        width = to_ref.shape[1] - extra
        place = lax.broadcasted_iota(jnp.int32, (rows, width), 1)
        cond = jnp.concatenate(
            [cond_ref[layer].astype(FULL), jnp.zeros((rows, width - mel), FULL)], axis=1
        )
        cond = jnp.where(place == mel, biases[:, layer : layer + 1], cond)
        cond = jnp.where(place == mel + 1, biases[:, layers + layer : layers + layer + 1], cond)
        to_ref[:, :early] = out_ref[layer]
        to_ref[:, early:extra] = conv_ref[layer]
        to_ref[:, extra:] = cond.astype(LOW)


def unpack_layers(layers, mel, *refs):
    conv_ref, cond_ref, conv_b_ref, out_ref, out_b_ref = refs[-5:]
    count = (len(refs) - 5) // layers
    rows = conv_ref.shape[1]
    same = lax.broadcasted_iota(jnp.int32, (rows, rows), 0)
    same = (same == lax.broadcasted_iota(jnp.int32, (rows, rows), 1)).astype(FULL)
    early, extra = out_ref.shape[2], out_ref.shape[2] + conv_ref.shape[2]
    for layer in range(layers):
        total = sum(ref[...].astype(FULL) for ref in refs[layer * count : (layer + 1) * count])
        out_ref[layer] = total[:, :early]
        conv_ref[layer] = total[:, early:extra]
        cond_ref[layer] = total[:, extra : extra + mel]
        biases = dot_rows(total[:, extra:], same, precision=lax.Precision.HIGHEST)
        conv_b_ref[layer : layer + 1] = biases[mel : mel + 1]
        out_b_ref[layer : layer + 1] = biases[mel + 1 : mel + 2]


def plain(kernel, operands, outs):
    return pl.pallas_call(
        kernel,
        out_shape=outs,
        compiler_params=pltpu.CompilerParams(vmem_limit_bytes=ROOM_SMALL * MIB),
    )(*operands)


def call(kernel, grid, info, operands, outs, scratch, flops, room):
    arrays = [x if spec else pltpu.with_memory_space_constraint(x, pltpu.VMEM) for x, spec in operands]
    shapes = [x if spec else pltpu.VMEM(x.shape, x.dtype) for x, spec in outs]
    moved = sum(x.size * x.dtype.itemsize for x, spec in (*operands, *outs) if spec)
    return pl.pallas_call(
        kernel,
        grid_spec=pltpu.PrefetchScalarGridSpec(
            num_scalar_prefetch=1,
            grid=(grid,),
            in_specs=[spec or KEPT for _, spec in operands],
            out_specs=[spec or KEPT for _, spec in outs],
            scratch_shapes=scratch,
        ),
        out_shape=shapes,
        compiler_params=pltpu.CompilerParams(
            vmem_limit_bytes=room * MIB, dimension_semantics=("arbitrary",)
        ),
        cost_estimate=pl.CostEstimate(flops=flops // HINT, bytes_accessed=moved // HINT, transcendentals=0),
    )(info, *arrays)


def at_home(value):
    return pltpu.with_memory_space_constraint(value, pltpu.HBM)


def shape_of(*shape, dtype=LOW):
    return jax.ShapeDtypeStruct(shape, dtype)


def tiled(width, place=lambda i: i):
    return pl.BlockSpec((TILE, width), lambda i, info: (place(i), 0))


def fixed(*shape, at=(0, 0)):
    return pl.BlockSpec(shape, lambda i, info: at)


KEPT = pl.BlockSpec(memory_space=pltpu.VMEM)


class Wires:
    def __init__(self, dp, cores, channels):
        self.rest = dp // 4
        assert dp == self.rest * 4 and self.rest & (self.rest - 1) == 0 and cores == 2
        self.devices = dp * 2
        self.rows = channels // self.devices
        self.direct = self.rows % 16 == 0
        self.dp = lax.axis_index(AXES[0])
        self.core = lax.axis_index(AXES[1])
        every = range(self.devices)
        self.sibling = [(i, i ^ 1) for i in every]
        self.first = [(i, i ^ (4 if i % 2 else 2)) for i in every]
        self.second = [(i, i ^ (2 if i % 2 else 4)) for i in every]

    def along_rest(self, distance):
        return [(i, i ^ (8 * distance)) for i in range(self.devices)]

    def hop(self, value, pairs):
        return lax.ppermute(value, AXES, pairs)

    def spread(self, blocks):
        return [blocks[0]] + [
            self.hop(blocks[k], self.along_rest(k)) for k in range(1, self.rest)
        ]

    def passed(self, *pieces):
        pieces = [*pieces, *(self.hop(piece, self.sibling) for piece in pieces)]
        return pieces if self.direct else [self.put_in_order(pieces)]

    def put_in_order(self, pieces):
        whole = jnp.zeros((self.rest, 2, 2, 2) + pieces[0].shape[1:], LOW)
        order = jnp.arange(self.rest) ^ (self.dp >> 2)
        for index, piece in enumerate(pieces):
            source = self.core ^ (index // 4)
            at_a, at_b = turned(self.dp, source, index % 2, (index // 2) % 2)
            whole = lax.dynamic_update_slice(
                whole, piece[order][:, None, None, None], (0, at_b, at_a, source, 0, 0)
            )
        return whole.reshape(-1, pieces[0].shape[2])

    def put_together(self, info_ref, pieces, w_ref):
        if not self.direct:
            w_ref[...] = pieces[0][...]
            return
        dp, core = info_ref[2], info_ref[3]
        for index, piece in enumerate(pieces):
            source = core ^ (index // 4)
            at_a, at_b = turned(dp, source, index % 2, (index // 2) % 2)
            for distance in range(self.rest):
                place = ((((dp >> 2) ^ distance) * 2 + at_b) * 2 + at_a) * 2 + source
                w_ref[rows_of(place, self.rows)] = piece[distance]

    def put_apart(self, info_ref, step, grads, here_ref, away_ref):
        start = 0
        for value in (grad.astype(LOW) for grad in grads):
            columns = slice(start, start + value.shape[1])
            start += value.shape[1]
            if not self.direct:
                here_ref[rows_of(step, value.shape[0]), columns] = value
                continue
            dp, core = info_ref[2], info_ref[3]
            blocks = value.shape[0] // self.rows
            for block in range(0, blocks, 2):
                at_b, at_a = (block // 4) % 2, (block // 2) % 2
                distance = (step * (blocks // 8) + block // 8) ^ (dp >> 2)
                on_a, on_b = at_a ^ (dp & 1), at_b ^ ((dp >> 1) & 1)
                even = value[block * self.rows : (block + 1) * self.rows]
                odd = value[(block + 1) * self.rows : (block + 2) * self.rows]
                first, second = jnp.where(core == 0, on_a, on_b), jnp.where(core == 0, on_b, on_a)
                here_ref[first, second, distance, :, columns] = jnp.where(core == 0, even, odd)
                away_ref[second, first, distance, :, columns] = jnp.where(core == 0, odd, even)

    def apart(self, depth):
        if not self.direct:
            return [(shape_of(self.devices * self.rows, depth), None), (shape_of(16, LANES), None)]
        return [(shape_of(2, 2, self.rest, self.rows, depth), None)] * 2

    def by_distance(self, full):
        rows = full.shape[0] // self.devices
        blocks = full.reshape(self.rest, 2, 2, 2, rows, full.shape[1])
        blocks = blocks[jnp.arange(self.rest) ^ (self.dp >> 2)]
        parts = []
        for away in range(2):
            source = self.core ^ away
            for first in range(2):
                for second in range(2):
                    at_a, at_b = turned(self.dp, source, first, second)
                    parts.append(
                        lax.dynamic_slice(
                            blocks,
                            (0, at_b, at_a, source, 0, 0),
                            (self.rest, 1, 1, 1, rows, full.shape[1]),
                        )[:, 0, 0, 0]
                    )
        return jnp.stack(parts).reshape(2, 2, 2, self.rest, rows, full.shape[1])


def turned(dp, owner, first, second):
    along_a = jnp.where(owner == 0, first, second)
    along_b = jnp.where(owner == 0, second, first)
    return (dp & 1) ^ along_a, ((dp >> 1) & 1) ^ along_b


def add_low(left, right):
    return (left.astype(FULL) + right.astype(FULL)).astype(LOW)


def per_device(
    dp,
    cores,
    samples,
    mel,
    lengths,
    hops,
    conv_weight,
    cond_weight,
    conv_bias,
    out_weight,
    out_bias,
    grad_out,
    grad_skip,
):
    sample_count, channels = samples.shape[1:]
    frame_count, mel_count = mel.shape[1:]
    layers = conv_weight.shape[0]
    size = Sizes(channels, mel_count)
    gate = size.gate
    wires = Wires(dp, cores, gate)
    assert layers == 2 and sample_count % TILE == 0 and TILE == FIRST_DILATION
    steps = sample_count // TILE
    where = jnp.stack([wires.dp, wires.core]).astype(jnp.int32)
    info = jnp.concatenate([lengths, hops, where])
    x, go, gs = samples[0], grad_out[0], grad_skip[0]
    conv_t, cond_t, out_t = (
        w.swapaxes(1, 2) for w in (conv_weight, cond_weight, out_weight)
    )
    rows = conv_t.shape[1]
    sources = (conv_t, cond_t, conv_bias, out_t, out_bias)
    own = pl.pallas_call(
        functools.partial(pack_layers, layers),
        in_specs=[pl.BlockSpec(memory_space=pl.ANY)] * len(sources),
        out_shape=[shape_of(rows, size.pack)] * layers,
        scratch_shapes=[pltpu.VMEM(source.shape, LOW) for source in sources]
        + [pltpu.SemaphoreType.DMA((len(sources),))],
        compiler_params=pltpu.CompilerParams(vmem_limit_bytes=ROOM_SMALL * MIB),
    )(*map(at_home, sources))
    last_shape = shape_of(wires.rest, rows, size.pack)
    half_shape = shape_of(2, wires.rest, rows, size.pack)
    blocks_shape = [shape_of(rows, size.pack)] * wires.rest
    side_by_side = lambda blocks: plain(put_side_by_side, blocks, [last_shape])[0]
    table = fixed(LANES, size.extra_width)
    macs = sample_count * channels * channels
    assert gate % PART == 0
    kept = lambda *columns: [(shape_of(sample_count, c), None) for c in columns]
    whole_w = (shape_of(gate, size.pack), None)
    parts = gate // PART
    melg = (shape_of(LANES, size.extra_width, dtype=FULL), table)
    scratch = lambda *shape: pltpu.VMEM(shape, LOW)

    blocked = (shape_of(sample_count, channels), tiled(channels))
    keep = lambda *values: [(value, None) for value in values]

    near0 = wires.spread([own[0]] * wires.rest)
    mine0 = side_by_side(near0)
    one0, two0 = wires.hop(mine0, wires.first), wires.hop(mine0, wires.second)
    mel_late, _ = lax.optimization_barrier((mel[0], mine0))
    mel_table = pl.pallas_call(
        mel_rows,
        out_shape=shape_of(LANES, size.extra_width),
        scratch_shapes=[pltpu.VMEM((LANES, size.extra_width), FULL)],
        compiler_params=pltpu.CompilerParams(vmem_limit_bytes=ROOM_SMALL * MIB),
    )(mel_late)
    own1, mel_table = lax.optimization_barrier((own[1], mel_table))
    near1 = wires.spread([own1] * wires.rest)
    mel_table, *near1 = lax.optimization_barrier((mel_table, *near1))
    mine1 = side_by_side(near1)
    low0, cond, frames, proj1 = call(
        functools.partial(prepare, size),
        steps,
        info,
        [*((at_home(value), tiled(channels)) for value in (x, go, gs)), (mel_table, table)],
        kept(channels, LANES, LANES, gate),
        [],
        macs,
        ROOM_0,
    )
    one0, two0, mine1 = lax.optimization_barrier((one0, two0, mine1))
    far0 = wires.hop(one0, wires.second)
    one1, two1 = wires.hop(mine1, wires.first), wires.hop(mine1, wires.second)
    far0, one1, two1, low0 = lax.optimization_barrier((far0, one1, two1, low0))
    low1, prev1, gated0, slope0, w0 = call(
        functools.partial(forward_0, size, wires),
        steps,
        info,
        keep(low0, cond, *wires.passed(mine0, one0, two0, far0)),
        [*kept(channels, channels, channels, gate), whole_w],
        [pltpu.VMEM((1, channels), FULL), pltpu.VMEM((8, channels), FULL)],
        10 * macs,
        ROOM_0,
    )
    far1 = wires.hop(one1, wires.second)
    far1, low1 = lax.optimization_barrier((far1, low1))
    gated1, pre1, w1, here1, away1, melg1 = call(
        functools.partial(layer_1, size, wires, steps),
        steps + parts,
        info,
        [*keep(low1, prev1, cond, frames, proj1), (mel_table, table)]
        + keep(*wires.passed(mine1, one1, two1, far1)),
        [*kept(channels, gate), whole_w, *wires.apart(size.pack), melg],
        [],
        24 * macs,
        ROOM_1,
    )
    if not wires.direct:
        here1, away1 = wires.by_distance(here1)
    came1 = wires.hop(away1, wires.sibling)

    proj0, pre0 = call(
        functools.partial(backward_0, size),
        steps,
        info,
        keep(pre1, w1, w0, proj1, slope0),
        kept(gate, gate),
        [pltpu.VMEM((8, channels), FULL)],
        12 * macs,
        ROOM_2,
    )
    stay1, leave1 = plain(add_and_part, (here1, came1), [half_shape] * 2)
    pre0, stay1, leave1 = lax.optimization_barrier((pre0, stay1, leave1))
    came1 = wires.hop(leave1, wires.first)

    here0, away0, melg0 = call(
        functools.partial(weights_0, size, wires),
        parts,
        info,
        [*keep(pre0, proj0, low0, gated0, frames), (mel_table, table), (w0, None)],
        [*wires.apart(size.pack), melg],
        [],
        12 * macs,
        ROOM_3,
    )
    if not wires.direct:
        here0, away0 = wires.by_distance(here0)
    away0, came1 = lax.optimization_barrier((away0, came1))
    came0 = wires.hop(away0, wires.sibling)
    stay1, leave1 = plain(add_and_part, (stay1, came1), [last_shape] * 2)
    came1 = wires.hop(leave1, wires.second)
    came0, leave1 = lax.optimization_barrier((came0, leave1))
    stay0, leave0 = plain(add_and_part, (here0, came0), [half_shape] * 2)
    pre0, stay0, leave0 = lax.optimization_barrier((pre0, stay0, leave0))
    came0 = wires.hop(leave0, wires.first)

    (samples_grad,) = call(
        functools.partial(samples_gradient, size),
        steps,
        info,
        keep(proj0, pre0, w0),
        [(shape_of(sample_count, channels, dtype=FULL), tiled(channels))],
        [],
        8 * macs,
        ROOM_4,
    )
    came0, came1, samples_grad = lax.optimization_barrier((came0, came1, samples_grad))
    parts1 = wires.spread(plain(add_and_part, (stay1, came1), blocks_shape))
    stay0, leave0 = plain(add_and_part, (stay0, came0), [last_shape] * 2)
    low1, stay0, leave0 = lax.optimization_barrier((low1, stay0, leave0))
    came0 = wires.hop(leave0, wires.second)
    residual_out, skip_output_sum = call(
        functools.partial(forward_outputs, size),
        steps,
        info,
        keep(low1, gated0, gated1, w0, w1),
        [blocked, blocked],
        [pltpu.VMEM((1, gate), FULL)],
        8 * macs,
        ROOM_5,
    )
    came0, residual_out = lax.optimization_barrier((came0, residual_out))
    parts0 = wires.spread(plain(add_and_part, (stay0, came0), blocks_shape))
    grads = plain(
        functools.partial(unpack_layers, layers, mel_count),
        (*parts0, *parts1),
        [
            shape_of(layers, rows, 2 * channels, dtype=FULL),
            shape_of(layers, rows, mel_count, dtype=FULL),
            shape_of(layers, rows, dtype=FULL),
            shape_of(layers, rows, channels, dtype=FULL),
            shape_of(layers, rows, dtype=FULL),
        ],
    )
    mel_grad = (melg0 + melg1)[:frame_count, :mel_count]
    conv_grad, cond_grad, conv_b_grad, out_grad, out_b_grad = grads
    return (
        residual_out[None],
        skip_output_sum[None],
        samples_grad[None],
        mel_grad[None],
        conv_grad.swapaxes(1, 2),
        cond_grad.swapaxes(1, 2),
        conv_b_grad,
        out_grad.swapaxes(1, 2),
        out_b_grad,
    )


def solution(mesh):
    dp, cores = mesh.shape["dp"], mesh.shape["group"]

    def everything(*arrays):
        return per_device(dp, cores, *arrays)

    clips = P(AXES, None, None)
    columns = P(None, None, AXES)
    biases = P(None, AXES)
    return jax.shard_map(
        everything,
        mesh=mesh,
        in_specs=(
            clips, clips, P(AXES), P(AXES), columns, columns, biases, columns, biases, clips, clips,
        ),
        out_specs=(clips, clips, clips, clips, columns, columns, biases, columns, biases),
        check_vma=False,
    )
```

```python
import functools

import jax
import jax.numpy as jnp
from jax import lax
from jax.experimental import pallas as pl
from jax.experimental.pallas import tpu as pltpu
from jax.sharding import PartitionSpec as P

FIRST_DILATION = 512
AXES = ("dp", "group")
LANES = 128
TILE = 512
PART = 256
MIB = 1024 * 1024
HINT = 4
ROOM_0, ROOM_1, ROOM_2, ROOM_3, ROOM_4, ROOM_5, ROOM_SMALL = 6, 4, 5, 3, 6, 5, 10
LOW = jnp.bfloat16
FULL = jnp.float32


def dot(left, right):
    return jnp.dot(left, right, preferred_element_type=FULL)


def dot_cols(left, right, **more):
    return lax.dot_general(
        left, right, (((1,), (1,)), ((), ())), preferred_element_type=FULL, **more
    )


def dot_rows(left, right, **more):
    return lax.dot_general(
        left, right, (((0,), (0,)), ((), ())), preferred_element_type=FULL, **more
    )


class Sizes:
    def __init__(self, channels, mel_count):
        self.channels = channels
        self.gate = 2 * channels
        self.mel = mel_count
        self.early = channels
        self.now = 2 * channels
        self.extra = 3 * channels
        self.extra_width = -(-(mel_count + 2) // LANES) * LANES
        self.pack = self.extra + self.extra_width


def mask_of(info_ref, start, rows):
    places = start + lax.broadcasted_iota(jnp.int32, (rows, 1), 0)
    return (places < info_ref[0]).astype(FULL)


def frames_of(info_ref, start, rows):
    places = start + lax.broadcasted_iota(jnp.int32, (rows, LANES), 0)
    first = lax.broadcasted_iota(jnp.int32, (rows, LANES), 1) * info_ref[1]
    return ((places >= first) & (places < first + info_ref[1])).astype(FULL).astype(LOW)


def masked(value, mask):
    return (value.astype(FULL) * mask).astype(LOW)


def out_bias_row(size, extra):
    column = lax.broadcasted_iota(jnp.int32, (8, size.extra_width), 1)
    pick = (column == size.mel + 1).astype(FULL).astype(LOW)
    return dot_cols(pick, extra)[0:1]


def gates(taps, w_ref, size, side):
    channels = size.channels
    width = channels // 2
    low = slice(side * width, (side + 1) * width)
    high = slice(channels + side * width, channels + (side + 1) * width)
    tangent = jnp.tanh(dot_cols(taps, w_ref[low, size.early :]))
    sig_gate = 0.5 * jnp.tanh(0.5 * dot_cols(taps, w_ref[high, size.early :])) + 0.5
    gated = tangent * sig_gate
    return low, high, gated, sig_gate * (1.0 - tangent * tangent), gated * (1.0 - sig_gate)


def rows_of(step, rows):
    return pl.ds(pl.multiple_of(step * rows, rows), rows)


def prepare(size, info_ref, x_ref, go_ref, gs_ref, mel_ref, low0_ref, place_ref, proj1_ref):
    step = pl.program_id(0)
    tile = rows_of(step, TILE)
    mask = mask_of(info_ref, step * TILE, TILE)
    low0_ref[tile] = masked(x_ref[...], mask)
    proj1_ref[tile, : size.channels] = masked(go_ref[...], mask)
    proj1_ref[tile, size.channels :] = masked(gs_ref[...], mask)
    frames = frames_of(info_ref, step * TILE, TILE)
    place_ref[tile, : size.extra_width] = dot(frames, mel_ref[...]).astype(LOW)
    place_ref[tile, size.extra_width :] = frames


def forward_0(size, wires, info_ref, low0_ref, place_ref, *refs):
    count = 8 if wires.direct else 1
    pieces, refs = refs[:count], refs[count:]
    taps1_ref, gated_ref, slope_ref, w_ref, bias_s, carry_s = refs
    step = pl.program_id(0)
    channels = size.channels

    @pl.when(step == 0)
    def _():
        wires.put_together(info_ref, pieces, w_ref)
        bias_s[...] = out_bias_row(size, w_ref[:channels, size.extra :])
        carry_s[...] = jnp.zeros_like(carry_s)

    tile = rows_of(step, TILE)
    mask = mask_of(info_ref, step * TILE, TILE)
    low = low0_ref[tile]
    before = low0_ref[rows_of(jnp.maximum(step - 1, 0), TILE)]
    prev = jnp.where(step > 0, before, jnp.zeros_like(before))
    taps = jnp.concatenate([prev, low, place_ref[tile, : size.extra_width]], axis=1)
    for side in range(2):
        first, second, gated, slope_a, slope_b = gates(taps, w_ref, size, side)
        gated_ref[tile, first] = gated.astype(LOW)
        slope_ref[tile, first] = slope_a.astype(LOW)
        slope_ref[tile, second] = slope_b.astype(LOW)
    moved = dot_cols(gated_ref[tile], w_ref[:channels, :channels])
    low = ((low.astype(FULL) + moved + bias_s[...]) * mask).astype(LOW)
    wide = low.astype(FULL)
    place = lax.broadcasted_iota(jnp.int32, (TILE, 1), 0)
    prev = jnp.where(place == 0, carry_s[7:8], pltpu.roll(wide, 1, 0)).astype(LOW)
    taps1_ref[tile, :channels] = prev
    taps1_ref[tile, channels : 2 * channels] = low
    taps1_ref[tile, 2 * channels :] = place_ref[tile]
    carry_s[...] = wide[TILE - 8 :]


def layer_1(size, wires, steps, info_ref, taps_ref, proj_ref, *refs):
    count = 8 if wires.direct else 1
    pieces, refs = refs[:count], refs[count:]
    gated_ref, pre_ref, w_ref, here_ref, away_ref, melg_ref = refs
    step = pl.program_id(0)
    channels = size.channels

    @pl.when(step == 0)
    def _():
        wires.put_together(info_ref, pieces, w_ref)
        melg_ref[...] = jnp.zeros_like(melg_ref)

    @pl.when(step < steps)
    def _():
        tile = rows_of(step, TILE)
        taps = taps_ref[tile, : size.pack - channels]
        grad_gated = dot(proj_ref[tile], w_ref[:, :channels])
        for side in range(2):
            first, second, gated, slope_a, slope_b = gates(taps, w_ref, size, side)
            gated_ref[tile, first] = gated.astype(LOW)
            pre_ref[tile, first] = (grad_gated[:, first] * slope_a).astype(LOW)
            pre_ref[tile, second] = (grad_gated[:, first] * slope_b).astype(LOW)

    @pl.when(step >= steps)
    def _():
        part = rows_of(step - steps, PART)
        pre = pre_ref[:, part]
        proj = proj_ref[:, part]
        both = dot_rows(pre, taps_ref[...])
        grads = [
            dot_rows(proj, gated_ref[...]),
            both[:, : 2 * channels],
            extra_grads(size, both[:, 2 * channels :], proj, w_ref[part, size.extra :], melg_ref),
        ]
        wires.put_apart(info_ref, step - steps, grads, here_ref, away_ref)


def in_two(value):
    high = value.astype(LOW)
    return high, (value - high.astype(FULL)).astype(LOW)


def extra_grads(size, both, proj, cond_weight, melg_ref):
    extra, sums = both[:, : size.extra_width], in_two(both[:, size.extra_width :])
    melg_ref[...] += sum(dot_rows(half, cond_weight) for half in sums)
    total = jnp.sum(proj.astype(FULL), axis=0, keepdims=True)
    bias = jnp.broadcast_to(total, (LANES, total.shape[1])).T[:, 0:1]
    column = lax.broadcasted_iota(jnp.int32, extra.shape, 1)
    return jnp.where(column == size.mel + 1, bias, extra)


def backward_0(size, last, info_ref, pre1_ref, w1_ref, w0_ref, proj1_ref, slope_ref, *refs):
    before, (proj_ref, pre0_ref, carry_ref) = refs[:-3], refs[-3:]
    step = pl.program_id(0)
    channels = size.channels
    index = last - step
    tile = rows_of(index, TILE)
    mask = mask_of(info_ref, index * TILE, TILE)

    @pl.when(step == 0)
    def _():
        carry_ref[...] = before[2][...] if before else jnp.zeros_like(carry_ref)

    pre1 = pre1_ref[tile]
    early = dot(pre1, w1_ref[:, size.early : size.now])
    place = lax.broadcasted_iota(jnp.int32, (TILE, 1), 0)
    later = jnp.where(place == TILE - 1, carry_ref[0:1], pltpu.roll(early, TILE - 1, 0))
    carry_ref[...] = early[:8]
    now = dot(pre1, w1_ref[:, size.now : size.extra])
    res = ((proj1_ref[tile, :channels].astype(FULL) + now + later) * mask).astype(LOW)
    proj_ref[tile, :channels] = res
    proj_ref[tile, channels:] = proj1_ref[tile, channels:]
    grad_gated = dot(proj_ref[tile], w0_ref[:, :channels])
    for half in (slice(0, channels), slice(channels, 2 * channels)):
        pre0_ref[tile, half] = (grad_gated * slope_ref[tile, half].astype(FULL)).astype(LOW)


def weights_0_early(size, wires, info_ref, pre_ref, proj_ref, x_ref, gated_ref, here_ref, away_ref):
    step = pl.program_id(0)
    part = rows_of(step, PART)
    shift = FIRST_DILATION
    grads = [
        dot_rows(proj_ref[:, part], gated_ref[...]),
        dot_rows(pre_ref[shift:, part], x_ref[: x_ref.shape[0] - shift]),
    ]
    wires.put_apart(info_ref, step, grads, here_ref, away_ref)


def weights_0_now(size, wires, info_ref, pre_ref, proj_ref, x_ref, place_ref, w_ref, here_ref, away_ref, melg_ref):
    step = pl.program_id(0)

    @pl.when(step == 0)
    def _():
        melg_ref[...] = jnp.zeros_like(melg_ref)

    part = rows_of(step, PART)
    pre = pre_ref[:, part]
    grads = [
        dot_rows(pre, x_ref[...]),
        extra_grads(size, dot_rows(pre, place_ref[...]), proj_ref[:, part], w_ref[part, size.extra :], melg_ref),
    ]
    wires.put_apart(info_ref, step, grads, here_ref, away_ref)


def samples_gradient(size, info_ref, proj_ref, pre_ref, w0_ref, sg_ref):
    step = pl.program_id(0)
    tile = rows_of(step, TILE)
    grad = proj_ref[tile, : size.channels].astype(FULL) + dot(pre_ref[tile], w0_ref[:, size.now : size.extra])
    after = rows_of(jnp.minimum(step + 1, pl.num_programs(0) - 1), TILE)
    later = dot(pre_ref[after], w0_ref[:, size.early : size.now])
    grad = grad + jnp.where(step < pl.num_programs(0) - 1, later, 0.0)
    sg_ref[...] = grad * mask_of(info_ref, step * TILE, TILE)


def forward_outputs(size, info_ref, taps1_ref, gated0_ref, gated1_ref, w0_ref, w1_ref, res_ref, skip_ref, bias_s):
    step = pl.program_id(0)
    channels = size.channels

    @pl.when(step == 0)
    def _():
        bias_s[...] = out_bias_row(size, w1_ref[:, size.extra :])
        bias_s[:, channels:] += out_bias_row(size, w0_ref[channels:, size.extra :])

    tile = rows_of(step, TILE)
    mask = mask_of(info_ref, step * TILE, TILE)
    res = dot_cols(gated1_ref[tile], w1_ref[:channels, :channels]) + bias_s[:, :channels]
    res_ref[...] = ((taps1_ref[tile, channels : 2 * channels].astype(FULL) + res) * mask).astype(LOW)
    skip = dot_cols(gated0_ref[tile], w0_ref[channels:, :channels])
    skip = skip + dot_cols(gated1_ref[tile], w1_ref[channels:, :channels])
    skip_ref[...] = ((skip + bias_s[:, channels:]) * mask).astype(LOW)


def add_and_part(left_ref, right_ref, *refs):
    for index, ref in enumerate(refs):
        ref[...] = add_low(left_ref[index], right_ref[index])


def mel_rows(mel_ref, table_ref, wide_s):
    frames, mel = mel_ref.shape
    wide_s[...] = jnp.zeros_like(wide_s)
    wide_s[:frames, :mel] = mel_ref[...].astype(FULL)
    wide_s[:frames, mel : mel + 1] = jnp.ones((frames, 1), FULL)
    table_ref[...] = wide_s[...].astype(LOW)


def add_both(left_a, right_a, left_b, right_b, *refs):
    cut = left_a.shape[-1]
    for index, ref in enumerate(refs):
        ref[..., :cut] = add_low(left_a[index], right_a[index])
        ref[..., cut:] = add_low(left_b[index], right_b[index])


def put_side_by_side(*refs):
    for index, ref in enumerate(refs[:-1]):
        refs[-1][index] = ref[...]


def pack_layers(layers, *refs):
    sources, packs, kept = refs[:5], refs[5 : 5 + layers], refs[5 + layers : 10 + layers]
    sems = refs[-1]
    copies = [
        pltpu.make_async_copy(source, to, sems.at[index])
        for index, (source, to) in enumerate(zip(sources, kept))
    ]
    for copy in copies:
        copy.start()
    for copy in copies:
        copy.wait()
    conv_ref, cond_ref, conv_b_ref, out_ref, out_b_ref = kept
    rows = conv_ref.shape[1]
    same = lax.broadcasted_iota(jnp.int32, (rows, rows), 0)
    same = (same == lax.broadcasted_iota(jnp.int32, (rows, rows), 1)).astype(FULL).astype(LOW)
    biases = dot_cols(same, jnp.concatenate([conv_b_ref[...], out_b_ref[...]], axis=0))
    early, extra = out_ref.shape[2], out_ref.shape[2] + conv_ref.shape[2]
    mel = cond_ref.shape[2]
    for layer, to_ref in enumerate(packs):
        width = to_ref.shape[1] - extra
        place = lax.broadcasted_iota(jnp.int32, (rows, width), 1)
        cond = jnp.concatenate(
            [cond_ref[layer].astype(FULL), jnp.zeros((rows, width - mel), FULL)], axis=1
        )
        cond = jnp.where(place == mel, biases[:, layer : layer + 1], cond)
        cond = jnp.where(place == mel + 1, biases[:, layers + layer : layers + layer + 1], cond)
        to_ref[:, :early] = out_ref[layer]
        to_ref[:, early:extra] = conv_ref[layer]
        to_ref[:, extra:] = cond.astype(LOW)


def unpack_layers(layers, mel, *refs):
    conv_ref, cond_ref, conv_b_ref, out_ref, out_b_ref = refs[-5:]
    count = (len(refs) - 5) // layers
    rows = conv_ref.shape[1]
    same = lax.broadcasted_iota(jnp.int32, (rows, rows), 0)
    same = (same == lax.broadcasted_iota(jnp.int32, (rows, rows), 1)).astype(FULL)
    early, extra = out_ref.shape[2], out_ref.shape[2] + conv_ref.shape[2]
    for layer in range(layers):
        total = sum(ref[...].astype(FULL) for ref in refs[layer * count : (layer + 1) * count])
        out_ref[layer] = total[:, :early]
        conv_ref[layer] = total[:, early:extra]
        cond_ref[layer] = total[:, extra : extra + mel]
        biases = dot_rows(total[:, extra:], same, precision=lax.Precision.HIGHEST)
        conv_b_ref[layer : layer + 1] = biases[mel : mel + 1]
        out_b_ref[layer : layer + 1] = biases[mel + 1 : mel + 2]


def plain(kernel, operands, outs):
    return pl.pallas_call(
        kernel,
        out_shape=outs,
        compiler_params=pltpu.CompilerParams(vmem_limit_bytes=ROOM_SMALL * MIB),
    )(*operands)


def call(kernel, grid, info, operands, outs, scratch, flops, room, onto=None):
    arrays = [x if spec else pltpu.with_memory_space_constraint(x, pltpu.VMEM) for x, spec in operands]
    shapes = [x if spec else pltpu.VMEM(x.shape, x.dtype) for x, spec in outs]
    moved = sum(x.size * x.dtype.itemsize for x, spec in (*operands, *outs) if spec)
    return pl.pallas_call(
        kernel,
        grid_spec=pltpu.PrefetchScalarGridSpec(
            num_scalar_prefetch=1,
            grid=(grid,),
            in_specs=[spec or KEPT for _, spec in operands],
            out_specs=[spec or KEPT for _, spec in outs],
            scratch_shapes=scratch,
        ),
        out_shape=shapes,
        input_output_aliases=onto or {},
        compiler_params=pltpu.CompilerParams(
            vmem_limit_bytes=room * MIB, dimension_semantics=("arbitrary",)
        ),
        cost_estimate=pl.CostEstimate(flops=flops // HINT, bytes_accessed=moved // HINT, transcendentals=0),
    )(info, *arrays)


def at_home(value):
    return pltpu.with_memory_space_constraint(value, pltpu.HBM)


def shape_of(*shape, dtype=LOW):
    return jax.ShapeDtypeStruct(shape, dtype)


def tiled(width, place=lambda i: i):
    return pl.BlockSpec((TILE, width), lambda i, info: (place(i), 0))


def fixed(*shape, at=(0, 0)):
    return pl.BlockSpec(shape, lambda i, info: at)


KEPT = pl.BlockSpec(memory_space=pltpu.VMEM)


class Wires:
    def __init__(self, dp, cores, channels):
        self.rest = dp // 4
        assert dp == self.rest * 4 and self.rest & (self.rest - 1) == 0 and cores == 2
        self.devices = dp * 2
        self.rows = channels // self.devices
        self.direct = self.rows % 16 == 0
        self.dp = lax.axis_index(AXES[0])
        self.core = lax.axis_index(AXES[1])
        every = range(self.devices)
        self.sibling = [(i, i ^ 1) for i in every]
        self.first = [(i, i ^ (4 if i % 2 else 2)) for i in every]
        self.second = [(i, i ^ (2 if i % 2 else 4)) for i in every]

    def along_rest(self, distance):
        return [(i, i ^ (8 * distance)) for i in range(self.devices)]

    def hop(self, value, pairs):
        return lax.ppermute(value, AXES, pairs)

    def spread(self, blocks):
        return [blocks[0]] + [
            self.hop(blocks[k], self.along_rest(k)) for k in range(1, self.rest)
        ]

    def passed(self, *pieces):
        pieces = [*pieces, *(self.hop(piece, self.sibling) for piece in pieces)]
        return pieces if self.direct else [self.put_in_order(pieces)]

    def put_in_order(self, pieces):
        whole = jnp.zeros((self.rest, 2, 2, 2) + pieces[0].shape[1:], LOW)
        order = jnp.arange(self.rest) ^ (self.dp >> 2)
        for index, piece in enumerate(pieces):
            source = self.core ^ (index // 4)
            at_a, at_b = turned(self.dp, source, index % 2, (index // 2) % 2)
            whole = lax.dynamic_update_slice(
                whole, piece[order][:, None, None, None], (0, at_b, at_a, source, 0, 0)
            )
        return whole.reshape(-1, pieces[0].shape[2])

    def put_together(self, info_ref, pieces, w_ref):
        if not self.direct:
            w_ref[...] = pieces[0][...]
            return
        dp, core = info_ref[2], info_ref[3]
        for index, piece in enumerate(pieces):
            source = core ^ (index // 4)
            at_a, at_b = turned(dp, source, index % 2, (index // 2) % 2)
            for distance in range(self.rest):
                place = ((((dp >> 2) ^ distance) * 2 + at_b) * 2 + at_a) * 2 + source
                w_ref[rows_of(place, self.rows)] = piece[distance]

    def put_apart(self, info_ref, step, grads, here_ref, away_ref):
        start = 0
        for value in (grad.astype(LOW) for grad in grads):
            columns = slice(start, start + value.shape[1])
            start += value.shape[1]
            if not self.direct:
                here_ref[rows_of(step, value.shape[0]), columns] = value
                continue
            dp, core = info_ref[2], info_ref[3]
            blocks = value.shape[0] // self.rows
            for block in range(0, blocks, 2):
                at_b, at_a = (block // 4) % 2, (block // 2) % 2
                distance = (step * (blocks // 8) + block // 8) ^ (dp >> 2)
                on_a, on_b = at_a ^ (dp & 1), at_b ^ ((dp >> 1) & 1)
                even = value[block * self.rows : (block + 1) * self.rows]
                odd = value[(block + 1) * self.rows : (block + 2) * self.rows]
                first, second = jnp.where(core == 0, on_a, on_b), jnp.where(core == 0, on_b, on_a)
                here_ref[first, second, distance, :, columns] = jnp.where(core == 0, even, odd)
                away_ref[second, first, distance, :, columns] = jnp.where(core == 0, odd, even)

    def apart(self, depth):
        if not self.direct:
            return [(shape_of(self.devices * self.rows, depth), None), (shape_of(16, LANES), None)]
        return [(shape_of(2, 2, self.rest, self.rows, depth), None)] * 2

    def by_distance(self, full):
        rows = full.shape[0] // self.devices
        blocks = full.reshape(self.rest, 2, 2, 2, rows, full.shape[1])
        blocks = blocks[jnp.arange(self.rest) ^ (self.dp >> 2)]
        parts = []
        for away in range(2):
            source = self.core ^ away
            for first in range(2):
                for second in range(2):
                    at_a, at_b = turned(self.dp, source, first, second)
                    parts.append(
                        lax.dynamic_slice(
                            blocks,
                            (0, at_b, at_a, source, 0, 0),
                            (self.rest, 1, 1, 1, rows, full.shape[1]),
                        )[:, 0, 0, 0]
                    )
        return jnp.stack(parts).reshape(2, 2, 2, self.rest, rows, full.shape[1])


def turned(dp, owner, first, second):
    along_a = jnp.where(owner == 0, first, second)
    along_b = jnp.where(owner == 0, second, first)
    return (dp & 1) ^ along_a, ((dp >> 1) & 1) ^ along_b


def add_low(left, right):
    return (left.astype(FULL) + right.astype(FULL)).astype(LOW)


def per_device(
    dp,
    cores,
    samples,
    mel,
    lengths,
    hops,
    conv_weight,
    cond_weight,
    conv_bias,
    out_weight,
    out_bias,
    grad_out,
    grad_skip,
):
    sample_count, channels = samples.shape[1:]
    frame_count, mel_count = mel.shape[1:]
    layers = conv_weight.shape[0]
    size = Sizes(channels, mel_count)
    gate = size.gate
    wires = Wires(dp, cores, gate)
    assert layers == 2 and sample_count % TILE == 0 and TILE == FIRST_DILATION
    steps = sample_count // TILE
    where = jnp.stack([wires.dp, wires.core]).astype(jnp.int32)
    info = jnp.concatenate([lengths, hops, where])
    x, go, gs = samples[0], grad_out[0], grad_skip[0]
    conv_t, cond_t, out_t = (
        w.swapaxes(1, 2) for w in (conv_weight, cond_weight, out_weight)
    )
    rows = conv_t.shape[1]
    sources = (conv_t, cond_t, conv_bias, out_t, out_bias)
    own = pl.pallas_call(
        functools.partial(pack_layers, layers),
        in_specs=[pl.BlockSpec(memory_space=pl.ANY)] * len(sources),
        out_shape=[shape_of(rows, size.pack)] * layers,
        scratch_shapes=[pltpu.VMEM(source.shape, LOW) for source in sources]
        + [pltpu.SemaphoreType.DMA((len(sources),))],
        compiler_params=pltpu.CompilerParams(vmem_limit_bytes=ROOM_SMALL * MIB),
    )(*map(at_home, sources))
    last_shape = shape_of(wires.rest, rows, size.pack)
    half_shape = shape_of(2, wires.rest, rows, size.pack)
    blocks_shape = [shape_of(rows, size.pack)] * wires.rest
    side_by_side = lambda blocks: plain(put_side_by_side, blocks, [last_shape])[0]
    table = fixed(LANES, size.extra_width)
    macs = sample_count * channels * channels
    assert gate % PART == 0
    kept = lambda *columns: [(shape_of(sample_count, c), None) for c in columns]
    whole_w = (shape_of(gate, size.pack), None)
    parts = gate // PART
    melg = (shape_of(LANES, size.extra_width, dtype=FULL), table)
    scratch = lambda *shape: pltpu.VMEM(shape, LOW)

    blocked = (shape_of(sample_count, channels), tiled(channels))
    keep = lambda *values: [(value, None) for value in values]

    near0 = wires.spread([own[0]] * wires.rest)
    mine0 = side_by_side(near0)
    one0, two0 = wires.hop(mine0, wires.first), wires.hop(mine0, wires.second)
    mel_late, _ = lax.optimization_barrier((mel[0], mine0))
    mel_table = pl.pallas_call(
        mel_rows,
        out_shape=shape_of(LANES, size.extra_width),
        scratch_shapes=[pltpu.VMEM((LANES, size.extra_width), FULL)],
        compiler_params=pltpu.CompilerParams(vmem_limit_bytes=ROOM_SMALL * MIB),
    )(mel_late)
    own1, mel_table = lax.optimization_barrier((own[1], mel_table))
    near1 = wires.spread([own1] * wires.rest)
    mel_table, *near1 = lax.optimization_barrier((mel_table, *near1))
    mine1 = side_by_side(near1)
    low0, place, proj1 = call(
        functools.partial(prepare, size),
        steps,
        info,
        [*((at_home(value), tiled(channels)) for value in (x, go, gs)), (mel_table, table)],
        kept(channels, size.extra_width + LANES, gate),
        [],
        macs,
        ROOM_0,
    )
    one0, two0, mine1 = lax.optimization_barrier((one0, two0, mine1))
    far0 = wires.hop(one0, wires.second)
    one1, two1 = wires.hop(mine1, wires.first), wires.hop(mine1, wires.second)
    far0, one1, two1, low0 = lax.optimization_barrier((far0, one1, two1, low0))
    taps1, gated0, slope0, w0 = call(
        functools.partial(forward_0, size, wires),
        steps,
        info,
        keep(low0, place, *wires.passed(mine0, one0, two0, far0)),
        [*kept(gate + size.extra_width + LANES, channels, gate), whole_w],
        [pltpu.VMEM((1, channels), FULL), pltpu.VMEM((8, channels), FULL)],
        10 * macs,
        ROOM_0,
    )
    far1 = wires.hop(one1, wires.second)
    far1, taps1 = lax.optimization_barrier((far1, taps1))
    gated1, pre1, w1, here1, away1, melg1 = call(
        functools.partial(layer_1, size, wires, steps),
        steps + parts,
        info,
        keep(taps1, proj1, *wires.passed(mine1, one1, two1, far1)),
        [*kept(channels, gate), whole_w, *wires.apart(size.pack), melg],
        [],
        24 * macs,
        ROOM_1,
    )
    if not wires.direct:
        here1, away1 = wires.by_distance(here1)
    came1 = wires.hop(away1, wires.sibling)

    carry = (shape_of(8, channels, dtype=FULL), None)
    begun = call(
        functools.partial(backward_0, size, steps - 1),
        steps - steps // 2,
        info,
        keep(pre1, w1, w0, proj1, slope0),
        [*kept(gate, gate), carry],
        [],
        6 * macs,
        ROOM_2,
    )
    stay1, leave1 = plain(add_and_part, (here1, came1), [half_shape] * 2)
    begun, stay1, leave1 = lax.optimization_barrier((begun, stay1, leave1))
    came1 = wires.hop(leave1, wires.first)
    proj0, pre0, _ = call(
        functools.partial(backward_0, size, steps // 2 - 1),
        steps // 2,
        info,
        keep(pre1, w1, w0, proj1, slope0, *begun),
        [*kept(gate, gate), carry],
        [],
        6 * macs,
        ROOM_2,
        {6: 0, 7: 1},
    )

    cut = lambda depth, *lead: shape_of(*lead, wires.rest, rows, depth)
    depths = (size.now, size.pack - size.now)
    here_a, away_a = call(
        functools.partial(weights_0_early, size, wires),
        parts,
        info,
        keep(pre0, proj0, low0, gated0),
        wires.apart(depths[0]),
        [],
        7 * macs,
        ROOM_3,
    )
    here_b, away_b, melg0 = call(
        functools.partial(weights_0_now, size, wires),
        parts,
        info,
        keep(pre0, proj0, low0, place, w0),
        [*wires.apart(depths[1]), melg],
        [],
        5 * macs,
        ROOM_3,
    )
    if not wires.direct:
        here_a, away_a = wires.by_distance(here_a)
        here_b, away_b = wires.by_distance(here_b)
    came_a = wires.hop(away_a, wires.sibling)
    came_a, here_b = lax.optimization_barrier((came_a, here_b))
    away_b, came1 = lax.optimization_barrier((away_b, came1))
    came_b = wires.hop(away_b, wires.sibling)
    stay_a, leave_a = plain(add_and_part, (here_a, came_a), [cut(depths[0], 2)] * 2)
    came_a = wires.hop(leave_a, wires.first)
    stay1, leave_a = lax.optimization_barrier((stay1, leave_a))
    stay1, leave1 = plain(add_and_part, (stay1, came1), [last_shape] * 2)
    came1 = wires.hop(leave1, wires.second)
    came_b, leave1 = lax.optimization_barrier((came_b, leave1))
    stay_b, leave_b = plain(add_and_part, (here_b, came_b), [cut(depths[1], 2)] * 2)
    came_b = wires.hop(leave_b, wires.first)
    pre0, taps1, leave_b = lax.optimization_barrier((pre0, taps1, leave_b))

    (samples_grad,) = call(
        functools.partial(samples_gradient, size),
        steps,
        info,
        keep(proj0, pre0, w0),
        [(shape_of(sample_count, channels, dtype=FULL), tiled(channels))],
        [],
        8 * macs,
        ROOM_4,
    )
    residual_out, skip_output_sum = call(
        functools.partial(forward_outputs, size),
        steps,
        info,
        keep(taps1, gated0, gated1, w0, w1),
        [blocked, blocked],
        [pltpu.VMEM((1, gate), FULL)],
        8 * macs,
        ROOM_5,
    )
    came_a, came_b, came1, samples_grad, residual_out = lax.optimization_barrier(
        (came_a, came_b, came1, samples_grad, residual_out)
    )
    parts1 = wires.spread(plain(add_and_part, (stay1, came1), blocks_shape))
    stay0, leave0 = plain(add_both, (stay_a, came_a, stay_b, came_b), [last_shape] * 2)
    came0 = wires.hop(leave0, wires.second)
    parts0 = wires.spread(plain(add_and_part, (stay0, came0), blocks_shape))
    grads = plain(
        functools.partial(unpack_layers, layers, mel_count),
        (*parts0, *parts1),
        [
            shape_of(layers, rows, 2 * channels, dtype=FULL),
            shape_of(layers, rows, mel_count, dtype=FULL),
            shape_of(layers, rows, dtype=FULL),
            shape_of(layers, rows, channels, dtype=FULL),
            shape_of(layers, rows, dtype=FULL),
        ],
    )
    mel_grad = (melg0 + melg1)[:frame_count, :mel_count]
    conv_grad, cond_grad, conv_b_grad, out_grad, out_b_grad = grads
    return (
        residual_out[None],
        skip_output_sum[None],
        samples_grad[None],
        mel_grad[None],
        conv_grad.swapaxes(1, 2),
        cond_grad.swapaxes(1, 2),
        conv_b_grad,
        out_grad.swapaxes(1, 2),
        out_b_grad,
    )


def solution(mesh):
    dp, cores = mesh.shape["dp"], mesh.shape["group"]

    def everything(*arrays):
        return per_device(dp, cores, *arrays)

    clips = P(AXES, None, None)
    columns = P(None, None, AXES)
    biases = P(None, AXES)
    return jax.shard_map(
        everything,
        mesh=mesh,
        in_specs=(
            clips, clips, P(AXES), P(AXES), columns, columns, biases, columns, biases, clips, clips,
        ),
        out_specs=(clips, clips, clips, clips, columns, columns, biases, columns, biases),
        check_vma=False,
    )
```

```python
import functools

import jax
import jax.numpy as jnp
from jax import lax
from jax.experimental import pallas as pl
from jax.experimental.pallas import tpu as pltpu
from jax.sharding import PartitionSpec as P

FIRST_DILATION = 512
AXES = ("dp", "group")
LANES = 128
TILE = 512
WIDE = 1024
PART = 512
PART_0 = 1024
MIB = 1024 * 1024
HINT = 4
ROOM_0, ROOM_1, ROOM_2, ROOM_3, ROOM_4, ROOM_5, ROOM_SMALL = 7, 8, 6, 7, 6, 6, 6
LOW = jnp.bfloat16
FULL = jnp.float32


def dot(left, right):
    return jnp.dot(left, right, preferred_element_type=FULL)


def dot_cols(left, right, **more):
    return lax.dot_general(
        left, right, (((1,), (1,)), ((), ())), preferred_element_type=FULL, **more
    )


def dot_rows(left, right, **more):
    return lax.dot_general(
        left, right, (((0,), (0,)), ((), ())), preferred_element_type=FULL, **more
    )


class Sizes:
    def __init__(self, channels, mel_count):
        self.channels = channels
        self.gate = 2 * channels
        self.mel = mel_count
        self.early = channels
        self.now = 2 * channels
        self.extra = 3 * channels
        self.extra_width = -(-(mel_count + 2) // LANES) * LANES
        self.pack = self.extra + self.extra_width


def mask_of(info_ref, start, rows):
    places = start + lax.broadcasted_iota(jnp.int32, (rows, 1), 0)
    return (places < info_ref[0]).astype(FULL)


def frames_of(info_ref, start, rows):
    places = start + lax.broadcasted_iota(jnp.int32, (rows, LANES), 0)
    first = lax.broadcasted_iota(jnp.int32, (rows, LANES), 1) * info_ref[1]
    return ((places >= first) & (places < first + info_ref[1])).astype(FULL).astype(LOW)


def masked(value, mask):
    return (value.astype(FULL) * mask).astype(LOW)


def out_bias_row(size, extra):
    column = lax.broadcasted_iota(jnp.int32, (8, size.extra_width), 1)
    pick = (column == size.mel + 1).astype(FULL).astype(LOW)
    return dot_cols(pick, extra)[0:1]


def gates(taps, w_ref, size, side):
    channels = size.channels
    width = channels // 2
    low = slice(side * width, (side + 1) * width)
    high = slice(channels + side * width, channels + (side + 1) * width)
    tangent = jnp.tanh(dot_cols(taps, w_ref[low, size.early :]))
    sig_gate = 0.5 * jnp.tanh(0.5 * dot_cols(taps, w_ref[high, size.early :])) + 0.5
    gated = tangent * sig_gate
    return low, high, gated, sig_gate * (1.0 - tangent * tangent), gated * (1.0 - sig_gate)


def rows_of(step, rows):
    return pl.ds(pl.multiple_of(step * rows, rows), rows)


def prepare(size, info_ref, x_ref, go_ref, gs_ref, mel_ref, taps0_ref, proj1_ref):
    step = pl.program_id(0)
    channels = size.channels
    tile = rows_of(step, TILE)
    mask = mask_of(info_ref, step * TILE, TILE)
    low = masked(x_ref[...], mask)
    taps0_ref[tile, channels : 2 * channels] = low

    @pl.when(step == 0)
    def _():
        taps0_ref[:TILE, :channels] = jnp.zeros((TILE, channels), LOW)

    @pl.when(step < pl.num_programs(0) - 1)
    def _():
        taps0_ref[rows_of(step + 1, TILE), :channels] = low

    proj1_ref[tile, :channels] = masked(go_ref[...], mask)
    proj1_ref[tile, channels:] = masked(gs_ref[...], mask)
    frames = frames_of(info_ref, step * TILE, TILE)
    place = 2 * channels + size.extra_width
    taps0_ref[tile, 2 * channels : place] = dot(frames, mel_ref[...]).astype(LOW)
    taps0_ref[tile, place:] = frames


def forward_0(size, wires, info_ref, taps0_ref, *refs):
    count = 8 if wires.direct else 1
    pieces, refs = refs[:count], refs[count:]
    taps1_ref, gated_ref, slope_ref, w_ref, bias_s, carry_s = refs
    step = pl.program_id(0)
    channels = size.channels

    @pl.when(step == 0)
    def _():
        wires.put_together(info_ref, pieces, w_ref)
        bias_s[...] = out_bias_row(size, w_ref[:channels, size.extra :])
        carry_s[...] = jnp.zeros_like(carry_s)

    tile = rows_of(step, WIDE)
    mask = mask_of(info_ref, step * WIDE, WIDE)
    taps = taps0_ref[tile, : size.pack - channels]
    for side in range(2):
        first, second, gated, slope_a, slope_b = gates(taps, w_ref, size, side)
        gated_ref[tile, first] = gated.astype(LOW)
        slope_ref[tile, first] = slope_a.astype(LOW)
        slope_ref[tile, second] = slope_b.astype(LOW)
    moved = dot_cols(gated_ref[tile], w_ref[:channels, :channels])
    hidden = taps0_ref[tile, channels : 2 * channels].astype(FULL)
    low = ((hidden + moved + bias_s[...]) * mask).astype(LOW)
    wide = low.astype(FULL)
    place = lax.broadcasted_iota(jnp.int32, (WIDE, 1), 0)
    prev = jnp.where(place == 0, carry_s[7:8], pltpu.roll(wide, 1, 0)).astype(LOW)
    taps1_ref[tile, :channels] = prev
    taps1_ref[tile, channels : 2 * channels] = low
    taps1_ref[tile, 2 * channels :] = taps0_ref[tile, 2 * channels :]
    carry_s[...] = wide[WIDE - 8 :]


def layer_1(size, wires, steps, info_ref, taps_ref, proj_ref, *refs):
    count = 8 if wires.direct else 1
    pieces, refs = refs[:count], refs[count:]
    gated_ref, pre_ref, w_ref, sums_ref, here_ref, away_ref = refs
    step = pl.program_id(0)
    channels = size.channels

    @pl.when(step == 0)
    def _():
        wires.put_together(info_ref, pieces, w_ref)

    @pl.when(step < steps)
    def _():
        tile = rows_of(step, TILE)
        taps = taps_ref[tile, : size.pack - channels]
        grad_gated = dot(proj_ref[tile], w_ref[:, :channels])
        for side in range(2):
            first, second, gated, slope_a, slope_b = gates(taps, w_ref, size, side)
            gated_ref[tile, first] = gated.astype(LOW)
            pre_ref[tile, first] = (grad_gated[:, first] * slope_a).astype(LOW)
            pre_ref[tile, second] = (grad_gated[:, first] * slope_b).astype(LOW)

    @pl.when(step >= steps)
    def _():
        part = rows_of(step - steps, PART)
        proj = proj_ref[:, part]
        both = dot_rows(pre_ref[:, part], taps_ref[...])
        sums_ref[part] = both[:, size.pack - channels :]
        grads = [
            dot_rows(proj, gated_ref[...]),
            both[:, : 2 * channels],
            extra_grads(size, both[:, 2 * channels : size.pack - channels], proj),
        ]
        wires.put_apart(info_ref, step - steps, grads, here_ref, away_ref)


def in_two(value):
    high = value.astype(LOW)
    return high, (value - high.astype(FULL)).astype(LOW)


def extra_grads(size, extra, proj):
    total = jnp.sum(proj.astype(FULL), axis=0, keepdims=True)
    bias = jnp.broadcast_to(total, (LANES, total.shape[1])).T[:, 0:1]
    column = lax.broadcasted_iota(jnp.int32, extra.shape, 1)
    return jnp.where(column == size.mel + 1, bias, extra)


def backward_0(size, last, info_ref, pre1_ref, w1_ref, w0_ref, proj1_ref, slope_ref, *refs):
    before, (proj_ref, pre0_ref, carry_ref) = refs[:-3], refs[-3:]
    step = pl.program_id(0)
    channels = size.channels
    index = last - step
    tile = rows_of(index, TILE)
    mask = mask_of(info_ref, index * TILE, TILE)

    @pl.when(step == 0)
    def _():
        carry_ref[...] = before[2][...] if before else jnp.zeros_like(carry_ref)

    pre1 = pre1_ref[tile]
    early = dot(pre1, w1_ref[:, size.early : size.now])
    place = lax.broadcasted_iota(jnp.int32, (TILE, 1), 0)
    later = jnp.where(place == TILE - 1, carry_ref[0:1], pltpu.roll(early, TILE - 1, 0))
    carry_ref[...] = early[:8]
    now = dot(pre1, w1_ref[:, size.now : size.extra])
    res = ((proj1_ref[tile, :channels].astype(FULL) + now + later) * mask).astype(LOW)
    proj_ref[tile, :channels] = res
    proj_ref[tile, channels:] = proj1_ref[tile, channels:]
    grad_gated = dot(proj_ref[tile], w0_ref[:, :channels])
    for half in (slice(0, channels), slice(channels, 2 * channels)):
        pre0_ref[tile, half] = (grad_gated * slope_ref[tile, half].astype(FULL)).astype(LOW)


def weights_0_early(size, wires, info_ref, pre_ref, proj_ref, taps_ref, gated_ref, here_ref, away_ref):
    step = pl.program_id(0)
    now = slice(size.channels, 2 * size.channels)
    part = rows_of(step, PART_0)
    shift = FIRST_DILATION
    grads = [
        dot_rows(proj_ref[:, part], gated_ref[...]),
        dot_rows(pre_ref[shift:, part], taps_ref[: taps_ref.shape[0] - shift, now]),
    ]
    wires.put_apart(info_ref, step, grads, here_ref, away_ref)


def weights_0_now(size, wires, info_ref, pre_ref, proj_ref, taps_ref, sums_ref, here_ref, away_ref):
    step = pl.program_id(0)
    part = rows_of(step, PART_0)
    channels = size.channels
    both = dot_rows(pre_ref[:, part], taps_ref[:, channels:])
    sums_ref[part] = both[:, channels + size.extra_width :]
    grads = [
        both[:, :channels],
        extra_grads(size, both[:, channels : channels + size.extra_width], proj_ref[:, part]),
    ]
    wires.put_apart(info_ref, step, grads, here_ref, away_ref)


def samples_gradient(size, info_ref, proj_ref, pre_ref, w0_ref, sg_ref):
    step = pl.program_id(0)
    tile = rows_of(step, TILE)
    grad = proj_ref[tile, : size.channels].astype(FULL) + dot(pre_ref[tile], w0_ref[:, size.now : size.extra])
    after = rows_of(jnp.minimum(step + 1, pl.num_programs(0) - 1), TILE)
    later = dot(pre_ref[after], w0_ref[:, size.early : size.now])
    grad = grad + jnp.where(step < pl.num_programs(0) - 1, later, 0.0)
    sg_ref[...] = grad * mask_of(info_ref, step * TILE, TILE)


def forward_outputs(size, info_ref, taps1_ref, gated0_ref, gated1_ref, w0_ref, w1_ref, sums0_ref, sums1_ref, res_ref, skip_ref, mel_ref, bias_s):
    step = pl.program_id(0)
    channels = size.channels

    @pl.when(step == 0)
    def _():
        bias_s[...] = out_bias_row(size, w1_ref[:, size.extra :])
        bias_s[:, channels:] += out_bias_row(size, w0_ref[channels:, size.extra :])
        mel_ref[...] = sum(
            dot_rows(half, w_ref[:, size.extra :])
            for sums_ref, w_ref in ((sums0_ref, w0_ref), (sums1_ref, w1_ref))
            for half in in_two(sums_ref[...])
        )

    tile = rows_of(step, TILE)
    mask = mask_of(info_ref, step * TILE, TILE)
    res = dot_cols(gated1_ref[tile], w1_ref[:channels, :channels]) + bias_s[:, :channels]
    res_ref[...] = ((taps1_ref[tile, channels : 2 * channels].astype(FULL) + res) * mask).astype(LOW)
    skip = dot_cols(gated0_ref[tile], w0_ref[channels:, :channels])
    skip = skip + dot_cols(gated1_ref[tile], w1_ref[channels:, :channels])
    skip_ref[...] = ((skip + bias_s[:, channels:]) * mask).astype(LOW)


def add_and_part(left_ref, right_ref, *refs):
    for index, ref in enumerate(refs):
        ref[...] = add_low(left_ref[index], right_ref[index])


def mel_rows(mel_ref, table_ref, wide_s):
    frames, mel = mel_ref.shape
    wide_s[...] = jnp.zeros_like(wide_s)
    wide_s[:frames, :mel] = mel_ref[...].astype(FULL)
    wide_s[:frames, mel : mel + 1] = jnp.ones((frames, 1), FULL)
    table_ref[...] = wide_s[...].astype(LOW)


def add_both(left_a, right_a, left_b, right_b, *refs):
    cut = left_a.shape[-1]
    for index, ref in enumerate(refs):
        ref[..., :cut] = add_low(left_a[index], right_a[index])
        ref[..., cut:] = add_low(left_b[index], right_b[index])


def hand_on(from_ref, to_ref):
    to_ref[...] = from_ref[...]


def put_side_by_side(*refs):
    for index, ref in enumerate(refs[:-1]):
        refs[-1][index] = ref[...]


def pack_layers(layers, *refs):
    sources, packs, table_ref = refs[:6], refs[6 : 6 + layers], refs[6 + layers]
    kept, wide_s, sems = refs[7 + layers : 13 + layers], refs[-2], refs[-1]
    copies = [
        pltpu.make_async_copy(source, to, sems.at[index])
        for index, (source, to) in enumerate(zip(sources, kept))
    ]
    for copy in copies:
        copy.start()
    for copy in copies:
        copy.wait()
    conv_ref, cond_ref, conv_b_ref, out_ref, out_b_ref, mel_ref = kept
    mel_rows(mel_ref, table_ref, wide_s)
    rows = conv_ref.shape[1]
    same = lax.broadcasted_iota(jnp.int32, (rows, rows), 0)
    same = (same == lax.broadcasted_iota(jnp.int32, (rows, rows), 1)).astype(FULL).astype(LOW)
    biases = dot_cols(same, jnp.concatenate([conv_b_ref[...], out_b_ref[...]], axis=0))
    early, extra = out_ref.shape[2], out_ref.shape[2] + conv_ref.shape[2]
    mel = cond_ref.shape[2]
    for layer, to_ref in enumerate(packs):
        width = to_ref.shape[1] - extra
        place = lax.broadcasted_iota(jnp.int32, (rows, width), 1)
        cond = jnp.concatenate(
            [cond_ref[layer].astype(FULL), jnp.zeros((rows, width - mel), FULL)], axis=1
        )
        cond = jnp.where(place == mel, biases[:, layer : layer + 1], cond)
        cond = jnp.where(place == mel + 1, biases[:, layers + layer : layers + layer + 1], cond)
        to_ref[:, :early] = out_ref[layer]
        to_ref[:, early:extra] = conv_ref[layer]
        to_ref[:, extra:] = cond.astype(LOW)


def unpack_layers(layers, mel, *refs):
    conv_ref, cond_ref, conv_b_ref, out_ref, out_b_ref = refs[-5:]
    count = (len(refs) - 5) // layers
    rows = conv_ref.shape[1]
    same = lax.broadcasted_iota(jnp.int32, (rows, rows), 0)
    same = (same == lax.broadcasted_iota(jnp.int32, (rows, rows), 1)).astype(FULL)
    early, extra = out_ref.shape[2], out_ref.shape[2] + conv_ref.shape[2]
    for layer in range(layers):
        total = sum(ref[...].astype(FULL) for ref in refs[layer * count : (layer + 1) * count])
        out_ref[layer] = total[:, :early]
        conv_ref[layer] = total[:, early:extra]
        cond_ref[layer] = total[:, extra : extra + mel]
        biases = dot_rows(total[:, extra:], same, precision=lax.Precision.HIGHEST)
        conv_b_ref[layer : layer + 1] = biases[mel : mel + 1]
        out_b_ref[layer : layer + 1] = biases[mel + 1 : mel + 2]


def in_vmem(value):
    return pltpu.with_memory_space_constraint(value, pltpu.VMEM)


def plain(kernel, operands, outs, at_end=False):
    shapes = outs if at_end else [pltpu.VMEM(x.shape, x.dtype) for x in outs]
    return pl.pallas_call(
        kernel,
        out_shape=shapes,
        in_specs=[KEPT] * len(operands),
        out_specs=[KEPT] * len(outs),
        compiler_params=pltpu.CompilerParams(vmem_limit_bytes=ROOM_SMALL * MIB),
    )(*map(in_vmem, operands))


def call(kernel, grid, info, operands, outs, scratch, flops, room, onto=None):
    arrays = [x if spec else in_vmem(x) for x, spec in operands]
    shapes = [x if spec else pltpu.VMEM(x.shape, x.dtype) for x, spec in outs]
    moved = sum(x.size * x.dtype.itemsize for x, spec in (*operands, *outs) if spec)
    return pl.pallas_call(
        kernel,
        grid_spec=pltpu.PrefetchScalarGridSpec(
            num_scalar_prefetch=1,
            grid=(grid,),
            in_specs=[spec or KEPT for _, spec in operands],
            out_specs=[spec or KEPT for _, spec in outs],
            scratch_shapes=scratch,
        ),
        out_shape=shapes,
        input_output_aliases=onto or {},
        compiler_params=pltpu.CompilerParams(
            vmem_limit_bytes=room * MIB, dimension_semantics=("arbitrary",)
        ),
        cost_estimate=pl.CostEstimate(flops=flops // HINT, bytes_accessed=moved // HINT, transcendentals=0),
    )(info, *arrays)


def at_home(value):
    return pltpu.with_memory_space_constraint(value, pltpu.HBM)


def shape_of(*shape, dtype=LOW):
    return jax.ShapeDtypeStruct(shape, dtype)


def tiled(width, place=lambda i: i):
    return pl.BlockSpec((TILE, width), lambda i, info: (place(i), 0))


def fixed(*shape, at=(0, 0)):
    return pl.BlockSpec(shape, lambda i, info: at)


KEPT = pl.BlockSpec(memory_space=pltpu.VMEM)


class Wires:
    def __init__(self, dp, cores, channels):
        self.rest = dp // 4
        assert dp == self.rest * 4 and self.rest & (self.rest - 1) == 0 and cores == 2
        self.devices = dp * 2
        self.rows = channels // self.devices
        self.direct = self.rows % 16 == 0
        self.dp = lax.axis_index(AXES[0])
        self.core = lax.axis_index(AXES[1])
        every = range(self.devices)
        self.sibling = [(i, i ^ 1) for i in every]
        self.first = [(i, i ^ (4 if i % 2 else 2)) for i in every]
        self.second = [(i, i ^ (2 if i % 2 else 4)) for i in every]

    def along_rest(self, distance):
        return [(i, i ^ (8 * distance)) for i in range(self.devices)]

    def hop(self, value, pairs):
        return lax.ppermute(value, AXES, pairs)

    def spread(self, blocks):
        return [blocks[0]] + [
            self.hop(blocks[k], self.along_rest(k)) for k in range(1, self.rest)
        ]

    def passed(self, *pieces):
        pieces = [*pieces, *(self.hop(piece, self.sibling) for piece in pieces)]
        return pieces if self.direct else [self.put_in_order(pieces)]

    def put_in_order(self, pieces):
        whole = jnp.zeros((self.rest, 2, 2, 2) + pieces[0].shape[1:], LOW)
        order = jnp.arange(self.rest) ^ (self.dp >> 2)
        for index, piece in enumerate(pieces):
            source = self.core ^ (index // 4)
            at_a, at_b = turned(self.dp, source, index % 2, (index // 2) % 2)
            whole = lax.dynamic_update_slice(
                whole, piece[order][:, None, None, None], (0, at_b, at_a, source, 0, 0)
            )
        return whole.reshape(-1, pieces[0].shape[2])

    def put_together(self, info_ref, pieces, w_ref):
        if not self.direct:
            w_ref[...] = pieces[0][...]
            return
        dp, core = info_ref[2], info_ref[3]
        for index, piece in enumerate(pieces):
            source = core ^ (index // 4)
            at_a, at_b = turned(dp, source, index % 2, (index // 2) % 2)
            for distance in range(self.rest):
                place = ((((dp >> 2) ^ distance) * 2 + at_b) * 2 + at_a) * 2 + source
                w_ref[rows_of(place, self.rows)] = piece[distance]

    def put_apart(self, info_ref, step, grads, here_ref, away_ref):
        start = 0
        for value in (grad.astype(LOW) for grad in grads):
            columns = slice(start, start + value.shape[1])
            start += value.shape[1]
            if not self.direct:
                here_ref[rows_of(step, value.shape[0]), columns] = value
                continue
            dp, core = info_ref[2], info_ref[3]
            blocks = value.shape[0] // self.rows
            for block in range(0, blocks, 2):
                at_b, at_a = (block // 4) % 2, (block // 2) % 2
                distance = (step * (blocks // 8) + block // 8) ^ (dp >> 2)
                on_a, on_b = at_a ^ (dp & 1), at_b ^ ((dp >> 1) & 1)
                even = value[block * self.rows : (block + 1) * self.rows]
                odd = value[(block + 1) * self.rows : (block + 2) * self.rows]
                first, second = jnp.where(core == 0, on_a, on_b), jnp.where(core == 0, on_b, on_a)
                here_ref[first, second, distance, :, columns] = jnp.where(core == 0, even, odd)
                away_ref[second, first, distance, :, columns] = jnp.where(core == 0, odd, even)

    def apart(self, depth):
        if not self.direct:
            return [(shape_of(self.devices * self.rows, depth), None), (shape_of(16, LANES), None)]
        return [(shape_of(2, 2, self.rest, self.rows, depth), None)] * 2

    def by_distance(self, full):
        rows = full.shape[0] // self.devices
        blocks = full.reshape(self.rest, 2, 2, 2, rows, full.shape[1])
        blocks = blocks[jnp.arange(self.rest) ^ (self.dp >> 2)]
        parts = []
        for away in range(2):
            source = self.core ^ away
            for first in range(2):
                for second in range(2):
                    at_a, at_b = turned(self.dp, source, first, second)
                    parts.append(
                        lax.dynamic_slice(
                            blocks,
                            (0, at_b, at_a, source, 0, 0),
                            (self.rest, 1, 1, 1, rows, full.shape[1]),
                        )[:, 0, 0, 0]
                    )
        return jnp.stack(parts).reshape(2, 2, 2, self.rest, rows, full.shape[1])


def turned(dp, owner, first, second):
    along_a = jnp.where(owner == 0, first, second)
    along_b = jnp.where(owner == 0, second, first)
    return (dp & 1) ^ along_a, ((dp >> 1) & 1) ^ along_b


def add_low(left, right):
    return (left.astype(FULL) + right.astype(FULL)).astype(LOW)


def per_device(
    dp,
    cores,
    samples,
    mel,
    lengths,
    hops,
    conv_weight,
    cond_weight,
    conv_bias,
    out_weight,
    out_bias,
    grad_out,
    grad_skip,
):
    sample_count, channels = samples.shape[1:]
    frame_count, mel_count = mel.shape[1:]
    layers = conv_weight.shape[0]
    size = Sizes(channels, mel_count)
    gate = size.gate
    wires = Wires(dp, cores, gate)
    assert layers == 2 and sample_count % TILE == 0 and TILE == FIRST_DILATION
    steps = sample_count // TILE
    where = jnp.stack([wires.dp, wires.core]).astype(jnp.int32)
    info = jnp.concatenate([lengths, hops, where])
    x, go, gs = samples[0], grad_out[0], grad_skip[0]
    conv_t, cond_t, out_t = (
        w.swapaxes(1, 2) for w in (conv_weight, cond_weight, out_weight)
    )
    rows = conv_t.shape[1]
    sources = (conv_t, cond_t, conv_bias, out_t, out_bias, mel[0])
    own0, own1, mel_table = pl.pallas_call(
        functools.partial(pack_layers, layers),
        in_specs=[pl.BlockSpec(memory_space=pl.ANY)] * len(sources),
        out_shape=[shape_of(rows, size.pack)] * layers + [shape_of(LANES, size.extra_width)],
        scratch_shapes=[pltpu.VMEM(source.shape, LOW) for source in sources]
        + [pltpu.VMEM((LANES, size.extra_width), FULL), pltpu.SemaphoreType.DMA((len(sources),))],
        compiler_params=pltpu.CompilerParams(vmem_limit_bytes=ROOM_SMALL * MIB),
    )(*map(at_home, sources))
    last_shape = shape_of(wires.rest, rows, size.pack)
    half_shape = shape_of(2, wires.rest, rows, size.pack)
    blocks_shape = [shape_of(rows, size.pack)] * wires.rest
    side_by_side = lambda blocks: plain(put_side_by_side, blocks, [last_shape])[0]
    table = fixed(LANES, size.extra_width)
    macs = sample_count * channels * channels
    assert gate % PART == 0 and gate % PART_0 == 0 and sample_count % WIDE == 0
    kept = lambda *columns: [(shape_of(sample_count, c), None) for c in columns]
    whole_w = (shape_of(gate, size.pack), None)
    parts = gate // PART
    mel_sums = (shape_of(LANES, size.extra_width, dtype=FULL), table)
    frame_sums = (shape_of(gate, LANES, dtype=FULL), None)
    scratch = lambda *shape: pltpu.VMEM(shape, LOW)

    blocked = (shape_of(sample_count, channels), tiled(channels))
    keep = lambda *values: [(value, None) for value in values]

    near0 = wires.spread([own0] * wires.rest)
    mine0 = side_by_side(near0)
    one0, two0 = wires.hop(mine0, wires.first), wires.hop(mine0, wires.second)
    own1, _ = lax.optimization_barrier((own1, mine0))
    (own1,) = plain(hand_on, (own1,), [shape_of(rows, size.pack)])
    near1 = wires.spread([own1] * wires.rest)
    mel_table, *near1 = lax.optimization_barrier((mel_table, *near1))
    mine1 = side_by_side(near1)
    taps0, proj1 = call(
        functools.partial(prepare, size),
        steps,
        info,
        [*((at_home(value), tiled(channels)) for value in (x, go, gs)), (mel_table, table)],
        kept(gate + size.extra_width + LANES, gate),
        [],
        macs,
        ROOM_0,
    )
    one0, two0, mine1 = lax.optimization_barrier((one0, two0, mine1))
    far0 = wires.hop(one0, wires.second)
    one1, two1 = wires.hop(mine1, wires.first), wires.hop(mine1, wires.second)
    far0, one1, two1, taps0 = lax.optimization_barrier((far0, one1, two1, taps0))
    taps1, gated0, slope0, w0 = call(
        functools.partial(forward_0, size, wires),
        sample_count // WIDE,
        info,
        keep(taps0, *wires.passed(mine0, one0, two0, far0)),
        [*kept(gate + size.extra_width + LANES, channels, gate), whole_w],
        [pltpu.VMEM((1, channels), FULL), pltpu.VMEM((8, channels), FULL)],
        10 * macs,
        ROOM_0,
    )
    far1 = wires.hop(one1, wires.second)
    far1, taps1 = lax.optimization_barrier((far1, taps1))
    gated1, pre1, w1, sums1, here1, away1 = call(
        functools.partial(layer_1, size, wires, steps),
        steps + parts,
        info,
        keep(taps1, proj1, *wires.passed(mine1, one1, two1, far1)),
        [*kept(channels, gate), whole_w, frame_sums, *wires.apart(size.pack)],
        [],
        24 * macs,
        ROOM_1,
    )
    if not wires.direct:
        here1, away1 = wires.by_distance(here1)
    came1 = wires.hop(away1, wires.sibling)

    carry = (shape_of(8, channels, dtype=FULL), None)
    begun = call(
        functools.partial(backward_0, size, steps - 1),
        steps - steps // 2,
        info,
        keep(pre1, w1, w0, proj1, slope0),
        [*kept(gate, gate), carry],
        [],
        6 * macs,
        ROOM_2,
    )
    stay1, leave1 = plain(add_and_part, (here1, came1), [half_shape] * 2)
    begun, stay1, leave1 = lax.optimization_barrier((begun, stay1, leave1))
    came1 = wires.hop(leave1, wires.first)
    proj0, pre0, _ = call(
        functools.partial(backward_0, size, steps // 2 - 1),
        steps // 2,
        info,
        keep(pre1, w1, w0, proj1, slope0, *begun),
        [*kept(gate, gate), carry],
        [],
        6 * macs,
        ROOM_2,
        {6: 0, 7: 1},
    )

    cut = lambda depth, *lead: shape_of(*lead, wires.rest, rows, depth)
    depths = (size.now, size.pack - size.now)
    here_a, away_a = call(
        functools.partial(weights_0_early, size, wires),
        gate // PART_0,
        info,
        keep(pre0, proj0, taps0, gated0),
        wires.apart(depths[0]),
        [],
        7 * macs,
        ROOM_3,
    )
    sums0, here_b, away_b = call(
        functools.partial(weights_0_now, size, wires),
        gate // PART_0,
        info,
        keep(pre0, proj0, taps0),
        [frame_sums, *wires.apart(depths[1])],
        [],
        5 * macs,
        ROOM_3,
    )
    if not wires.direct:
        here_a, away_a = wires.by_distance(here_a)
        here_b, away_b = wires.by_distance(here_b)
    came_a = wires.hop(away_a, wires.sibling)
    came_a, here_b = lax.optimization_barrier((came_a, here_b))
    away_b, came1 = lax.optimization_barrier((away_b, came1))
    came_b = wires.hop(away_b, wires.sibling)
    stay_a, leave_a = plain(add_and_part, (here_a, came_a), [cut(depths[0], 2)] * 2)
    came_a = wires.hop(leave_a, wires.first)
    stay1, leave_a = lax.optimization_barrier((stay1, leave_a))
    stay1, leave1 = plain(add_and_part, (stay1, came1), [last_shape] * 2)
    came1 = wires.hop(leave1, wires.second)
    came_b, leave1 = lax.optimization_barrier((came_b, leave1))
    stay_b, leave_b = plain(add_and_part, (here_b, came_b), [cut(depths[1], 2)] * 2)
    came_b = wires.hop(leave_b, wires.first)
    pre0, taps1, leave_b = lax.optimization_barrier((pre0, taps1, leave_b))

    (samples_grad,) = call(
        functools.partial(samples_gradient, size),
        steps,
        info,
        keep(proj0, pre0, w0),
        [(shape_of(sample_count, channels, dtype=FULL), tiled(channels))],
        [],
        8 * macs,
        ROOM_4,
    )
    residual_out, skip_output_sum, mel_grad = call(
        functools.partial(forward_outputs, size),
        steps,
        info,
        keep(taps1, gated0, gated1, w0, w1, sums0, sums1),
        [blocked, blocked, mel_sums],
        [pltpu.VMEM((1, gate), FULL)],
        8 * macs,
        ROOM_5,
    )
    came_a, came_b, came1, samples_grad, residual_out = lax.optimization_barrier(
        (came_a, came_b, came1, samples_grad, residual_out)
    )
    parts1 = wires.spread(plain(add_and_part, (stay1, came1), blocks_shape))
    stay0, leave0 = plain(add_both, (stay_a, came_a, stay_b, came_b), [last_shape] * 2)
    came0 = wires.hop(leave0, wires.second)
    parts0 = wires.spread(plain(add_and_part, (stay0, came0), blocks_shape))
    grads = plain(
        functools.partial(unpack_layers, layers, mel_count),
        (*parts0, *parts1),
        [
            shape_of(layers, rows, 2 * channels, dtype=FULL),
            shape_of(layers, rows, mel_count, dtype=FULL),
            shape_of(layers, rows, dtype=FULL),
            shape_of(layers, rows, channels, dtype=FULL),
            shape_of(layers, rows, dtype=FULL),
        ],
        at_end=True,
    )
    conv_grad, cond_grad, conv_b_grad, out_grad, out_b_grad = grads
    return (
        residual_out[None],
        skip_output_sum[None],
        samples_grad[None],
        mel_grad[:frame_count, :mel_count][None],
        conv_grad.swapaxes(1, 2),
        cond_grad.swapaxes(1, 2),
        conv_b_grad,
        out_grad.swapaxes(1, 2),
        out_b_grad,
    )


def solution(mesh):
    dp, cores = mesh.shape["dp"], mesh.shape["group"]

    def everything(*arrays):
        return per_device(dp, cores, *arrays)

    clips = P(AXES, None, None)
    columns = P(None, None, AXES)
    biases = P(None, AXES)
    return jax.shard_map(
        everything,
        mesh=mesh,
        in_specs=(
            clips, clips, P(AXES), P(AXES), columns, columns, biases, columns, biases, clips, clips,
        ),
        out_specs=(clips, clips, clips, clips, columns, columns, biases, columns, biases),
        check_vma=False,
    )
```

```python
import functools

import jax
import jax.numpy as jnp
from jax import lax
from jax.experimental import pallas as pl
from jax.experimental.pallas import tpu as pltpu
from jax.sharding import PartitionSpec as P

FIRST_DILATION = 512
AXES = ("dp", "group")
LANES = 128
TILE = 512
WIDE = 1024
PART = 512
PART_0 = 1024
MIB = 1024 * 1024
HINT = 4
ROOM_0, ROOM_1, ROOM_2, ROOM_3, ROOM_4, ROOM_5, ROOM_SMALL = 7, 8, 6, 7, 6, 6, 6
LOW = jnp.bfloat16
FULL = jnp.float32


def dot(left, right):
    return jnp.dot(left, right, preferred_element_type=FULL)


def dot_cols(left, right, **more):
    return lax.dot_general(
        left, right, (((1,), (1,)), ((), ())), preferred_element_type=FULL, **more
    )


def dot_rows(left, right, **more):
    return lax.dot_general(
        left, right, (((0,), (0,)), ((), ())), preferred_element_type=FULL, **more
    )


class Sizes:
    def __init__(self, channels, mel_count):
        self.channels = channels
        self.gate = 2 * channels
        self.mel = mel_count
        self.early = channels
        self.now = 2 * channels
        self.extra = 3 * channels
        self.extra_width = -(-(mel_count + 2) // LANES) * LANES
        self.pack = self.extra + self.extra_width


def mask_of(info_ref, start, rows):
    places = start + lax.broadcasted_iota(jnp.int32, (rows, 1), 0)
    return (places < info_ref[0]).astype(FULL)


def frames_of(info_ref, start, rows):
    places = start + lax.broadcasted_iota(jnp.int32, (rows, LANES), 0)
    first = lax.broadcasted_iota(jnp.int32, (rows, LANES), 1) * info_ref[1]
    return ((places >= first) & (places < first + info_ref[1])).astype(FULL).astype(LOW)


def masked(value, mask):
    return (value.astype(FULL) * mask).astype(LOW)


def out_bias_row(size, extra):
    column = lax.broadcasted_iota(jnp.int32, (8, size.extra_width), 1)
    pick = (column == size.mel + 1).astype(FULL).astype(LOW)
    return dot_cols(pick, extra)[0:1]


def gates(taps, w_ref, size, side):
    channels = size.channels
    width = channels // 2
    low = slice(side * width, (side + 1) * width)
    high = slice(channels + side * width, channels + (side + 1) * width)
    tangent = jnp.tanh(dot_cols(taps, w_ref[low, size.early :]))
    sig_gate = 0.5 * jnp.tanh(0.5 * dot_cols(taps, w_ref[high, size.early :])) + 0.5
    gated = tangent * sig_gate
    return low, high, gated, sig_gate * (1.0 - tangent * tangent), gated * (1.0 - sig_gate)


def rows_of(step, rows):
    return pl.ds(pl.multiple_of(step * rows, rows), rows)


def prepare(size, info_ref, x_ref, go_ref, gs_ref, mel_ref, taps0_ref, proj1_ref):
    step = pl.program_id(0)
    channels = size.channels
    tile = rows_of(step, TILE)
    mask = mask_of(info_ref, step * TILE, TILE)
    low = masked(x_ref[...], mask)
    taps0_ref[tile, channels : 2 * channels] = low

    @pl.when(step == 0)
    def _():
        taps0_ref[:TILE, :channels] = jnp.zeros((TILE, channels), LOW)

    @pl.when(step < pl.num_programs(0) - 1)
    def _():
        taps0_ref[rows_of(step + 1, TILE), :channels] = low

    proj1_ref[tile, :channels] = masked(go_ref[...], mask)
    proj1_ref[tile, channels:] = masked(gs_ref[...], mask)
    frames = frames_of(info_ref, step * TILE, TILE)
    place = 2 * channels + size.extra_width
    taps0_ref[tile, 2 * channels : place] = dot(frames, mel_ref[...]).astype(LOW)
    taps0_ref[tile, place:] = frames


def forward_0(size, wires, info_ref, taps0_ref, *refs):
    count = 8 if wires.direct else 1
    pieces, refs = refs[:count], refs[count:]
    taps1_ref, gated_ref, slope_ref, w_ref, bias_s, carry_s = refs
    step = pl.program_id(0)
    channels = size.channels

    @pl.when(step == 0)
    def _():
        wires.put_together(info_ref, pieces, w_ref)
        bias_s[...] = out_bias_row(size, w_ref[:channels, size.extra :])
        carry_s[...] = jnp.zeros_like(carry_s)

    tile = rows_of(step, WIDE)
    mask = mask_of(info_ref, step * WIDE, WIDE)
    taps = taps0_ref[tile, : size.pack - channels]
    for side in range(2):
        first, second, gated, slope_a, slope_b = gates(taps, w_ref, size, side)
        gated_ref[tile, first] = gated.astype(LOW)
        slope_ref[tile, first] = slope_a.astype(LOW)
        slope_ref[tile, second] = slope_b.astype(LOW)
    moved = dot_cols(gated_ref[tile], w_ref[:channels, :channels])
    hidden = taps0_ref[tile, channels : 2 * channels].astype(FULL)
    low = ((hidden + moved + bias_s[...]) * mask).astype(LOW)
    wide = low.astype(FULL)
    place = lax.broadcasted_iota(jnp.int32, (WIDE, 1), 0)
    prev = jnp.where(place == 0, carry_s[7:8], pltpu.roll(wide, 1, 0)).astype(LOW)
    taps1_ref[tile, :channels] = prev
    taps1_ref[tile, channels : 2 * channels] = low
    taps1_ref[tile, 2 * channels :] = taps0_ref[tile, 2 * channels :]
    carry_s[...] = wide[WIDE - 8 :]


def layer_1(size, wires, steps, info_ref, taps_ref, proj_ref, *refs):
    count = 8 if wires.direct else 1
    pieces, refs = refs[:count], refs[count:]
    gated_ref, pre_ref, w_ref, sums_ref, here_ref, away_ref = refs
    step = pl.program_id(0)
    channels = size.channels

    @pl.when(step == 0)
    def _():
        wires.put_together(info_ref, pieces, w_ref)

    @pl.when(step < steps)
    def _():
        tile = rows_of(step, TILE)
        taps = taps_ref[tile, : size.pack - channels]
        grad_gated = dot(proj_ref[tile], w_ref[:, :channels])
        for side in range(2):
            first, second, gated, slope_a, slope_b = gates(taps, w_ref, size, side)
            gated_ref[tile, first] = gated.astype(LOW)
            pre_ref[tile, first] = (grad_gated[:, first] * slope_a).astype(LOW)
            pre_ref[tile, second] = (grad_gated[:, first] * slope_b).astype(LOW)

    @pl.when(step >= steps)
    def _():
        part = rows_of(step - steps, PART)
        proj = proj_ref[:, part]
        both = dot_rows(pre_ref[:, part], taps_ref[...])
        sums_ref[part] = both[:, size.pack - channels :]
        grads = [
            dot_rows(proj, gated_ref[...]),
            both[:, : 2 * channels],
            extra_grads(size, both[:, 2 * channels : size.pack - channels], proj),
        ]
        wires.put_apart(info_ref, step - steps, grads, here_ref, away_ref)


def in_two(value):
    high = value.astype(LOW)
    return high, (value - high.astype(FULL)).astype(LOW)


def extra_grads(size, extra, proj):
    total = jnp.sum(proj.astype(FULL), axis=0, keepdims=True)
    bias = jnp.broadcast_to(total, (LANES, total.shape[1])).T[:, 0:1]
    column = lax.broadcasted_iota(jnp.int32, extra.shape, 1)
    return jnp.where(column == size.mel + 1, bias, extra)


def backward_0(size, last, info_ref, pre1_ref, w1_ref, w0_ref, proj1_ref, slope_ref, *refs):
    before, (proj_ref, pre0_ref, carry_ref) = refs[:-3], refs[-3:]
    step = pl.program_id(0)
    channels = size.channels
    index = last - step
    tile = rows_of(index, TILE)
    mask = mask_of(info_ref, index * TILE, TILE)

    @pl.when(step == 0)
    def _():
        carry_ref[...] = before[2][...] if before else jnp.zeros_like(carry_ref)

    pre1 = pre1_ref[tile]
    early = dot(pre1, w1_ref[:, size.early : size.now])
    place = lax.broadcasted_iota(jnp.int32, (TILE, 1), 0)
    later = jnp.where(place == TILE - 1, carry_ref[0:1], pltpu.roll(early, TILE - 1, 0))
    carry_ref[...] = early[:8]
    now = dot(pre1, w1_ref[:, size.now : size.extra])
    res = ((proj1_ref[tile, :channels].astype(FULL) + now + later) * mask).astype(LOW)
    proj_ref[tile, :channels] = res
    proj_ref[tile, channels:] = proj1_ref[tile, channels:]
    grad_gated = dot(proj_ref[tile], w0_ref[:, :channels])
    for half in (slice(0, channels), slice(channels, 2 * channels)):
        pre0_ref[tile, half] = (grad_gated * slope_ref[tile, half].astype(FULL)).astype(LOW)


def weights_0_early(size, wires, info_ref, pre_ref, proj_ref, taps_ref, gated_ref, here_ref, away_ref):
    step = pl.program_id(0)
    now = slice(size.channels, 2 * size.channels)
    part = rows_of(step, PART_0)
    shift = FIRST_DILATION
    grads = [
        dot_rows(proj_ref[:, part], gated_ref[...]),
        dot_rows(pre_ref[shift:, part], taps_ref[: taps_ref.shape[0] - shift, now]),
    ]
    wires.put_apart(info_ref, step, grads, here_ref, away_ref)


def weights_0_now(size, wires, info_ref, pre_ref, proj_ref, taps_ref, sums_ref, here_ref, away_ref):
    step = pl.program_id(0)
    part = rows_of(step, PART_0)
    channels = size.channels
    both = dot_rows(pre_ref[:, part], taps_ref[:, channels:])
    sums_ref[part] = both[:, channels + size.extra_width :]
    grads = [
        both[:, :channels],
        extra_grads(size, both[:, channels : channels + size.extra_width], proj_ref[:, part]),
    ]
    wires.put_apart(info_ref, step, grads, here_ref, away_ref)


def samples_gradient(size, info_ref, proj_ref, pre_ref, w0_ref, sg_ref):
    step = pl.program_id(0)
    tile = rows_of(step, TILE)
    grad = proj_ref[tile, : size.channels].astype(FULL) + dot(pre_ref[tile], w0_ref[:, size.now : size.extra])
    after = rows_of(jnp.minimum(step + 1, pl.num_programs(0) - 1), TILE)
    later = dot(pre_ref[after], w0_ref[:, size.early : size.now])
    grad = grad + jnp.where(step < pl.num_programs(0) - 1, later, 0.0)
    sg_ref[...] = grad * mask_of(info_ref, step * TILE, TILE)


def forward_outputs(size, info_ref, taps1_ref, gated0_ref, gated1_ref, w0_ref, w1_ref, sums0_ref, sums1_ref, res_ref, skip_ref, mel_ref, bias_s):
    step = pl.program_id(0)
    channels = size.channels

    @pl.when(step == 0)
    def _():
        bias_s[...] = out_bias_row(size, w1_ref[:, size.extra :])
        bias_s[:, channels:] += out_bias_row(size, w0_ref[channels:, size.extra :])
        mel_ref[...] = sum(
            dot_rows(half, w_ref[:, size.extra :])
            for sums_ref, w_ref in ((sums0_ref, w0_ref), (sums1_ref, w1_ref))
            for half in in_two(sums_ref[...])
        )

    tile = rows_of(step, TILE)
    mask = mask_of(info_ref, step * TILE, TILE)
    res = dot_cols(gated1_ref[tile], w1_ref[:channels, :channels]) + bias_s[:, :channels]
    res_ref[...] = ((taps1_ref[tile, channels : 2 * channels].astype(FULL) + res) * mask).astype(LOW)
    skip = dot_cols(gated0_ref[tile], w0_ref[channels:, :channels])
    skip = skip + dot_cols(gated1_ref[tile], w1_ref[channels:, :channels])
    skip_ref[...] = ((skip + bias_s[:, channels:]) * mask).astype(LOW)


def add_and_part(left_ref, right_ref, *refs):
    for index, ref in enumerate(refs):
        ref[...] = add_low(left_ref[index], right_ref[index])


def mel_rows(mel_ref, table_ref, wide_s):
    frames, mel = mel_ref.shape
    wide_s[...] = jnp.zeros_like(wide_s)
    wide_s[:frames, :mel] = mel_ref[...].astype(FULL)
    wide_s[:frames, mel : mel + 1] = jnp.ones((frames, 1), FULL)
    table_ref[...] = wide_s[...].astype(LOW)


def add_both(left_a, right_a, left_b, right_b, *refs):
    cut = left_a.shape[-1]
    for index, ref in enumerate(refs):
        ref[..., :cut] = add_low(left_a[index], right_a[index])
        ref[..., cut:] = add_low(left_b[index], right_b[index])


def hand_on(from_ref, to_ref):
    to_ref[...] = from_ref[...]


def put_side_by_side(*refs):
    for index, ref in enumerate(refs[:-1]):
        refs[-1][index] = ref[...]


def pack_layers(layers, *refs):
    sources, packs, table_ref = refs[:6], refs[6 : 6 + layers], refs[6 + layers]
    kept, wide_s, sems = refs[7 + layers : 13 + layers], refs[-2], refs[-1]
    copies = [
        pltpu.make_async_copy(source, to, sems.at[index])
        for index, (source, to) in enumerate(zip(sources, kept))
    ]
    for copy in copies:
        copy.start()
    for copy in copies:
        copy.wait()
    conv_ref, cond_ref, conv_b_ref, out_ref, out_b_ref, mel_ref = kept
    mel_rows(mel_ref, table_ref, wide_s)
    rows = conv_ref.shape[1]
    same = lax.broadcasted_iota(jnp.int32, (rows, rows), 0)
    same = (same == lax.broadcasted_iota(jnp.int32, (rows, rows), 1)).astype(FULL).astype(LOW)
    biases = dot_cols(same, jnp.concatenate([conv_b_ref[...], out_b_ref[...]], axis=0))
    early, extra = out_ref.shape[2], out_ref.shape[2] + conv_ref.shape[2]
    mel = cond_ref.shape[2]
    for layer, to_ref in enumerate(packs):
        width = to_ref.shape[1] - extra
        place = lax.broadcasted_iota(jnp.int32, (rows, width), 1)
        cond = jnp.concatenate(
            [cond_ref[layer].astype(FULL), jnp.zeros((rows, width - mel), FULL)], axis=1
        )
        cond = jnp.where(place == mel, biases[:, layer : layer + 1], cond)
        cond = jnp.where(place == mel + 1, biases[:, layers + layer : layers + layer + 1], cond)
        to_ref[:, :early] = out_ref[layer]
        to_ref[:, early:extra] = conv_ref[layer]
        to_ref[:, extra:] = cond.astype(LOW)


def unpack_layers(layers, mel, *refs):
    conv_ref, cond_ref, conv_b_ref, out_ref, out_b_ref = refs[-5:]
    count = (len(refs) - 5) // layers
    rows = conv_ref.shape[1]
    same = lax.broadcasted_iota(jnp.int32, (rows, rows), 0)
    same = (same == lax.broadcasted_iota(jnp.int32, (rows, rows), 1)).astype(FULL)
    early, extra = out_ref.shape[2], out_ref.shape[2] + conv_ref.shape[2]
    for layer in range(layers):
        total = sum(ref[...].astype(FULL) for ref in refs[layer * count : (layer + 1) * count])
        out_ref[layer] = total[:, :early]
        conv_ref[layer] = total[:, early:extra]
        cond_ref[layer] = total[:, extra : extra + mel]
        biases = dot_rows(total[:, extra:], same, precision=lax.Precision.HIGHEST)
        conv_b_ref[layer : layer + 1] = biases[mel : mel + 1]
        out_b_ref[layer : layer + 1] = biases[mel + 1 : mel + 2]


def in_vmem(value):
    return pltpu.with_memory_space_constraint(value, pltpu.VMEM)


def plain(kernel, operands, outs, at_end=False):
    shapes = outs if at_end else [pltpu.VMEM(x.shape, x.dtype) for x in outs]
    return pl.pallas_call(
        kernel,
        out_shape=shapes,
        in_specs=[KEPT] * len(operands),
        out_specs=[KEPT] * len(outs),
        compiler_params=pltpu.CompilerParams(vmem_limit_bytes=ROOM_SMALL * MIB),
    )(*map(in_vmem, operands))


def call(kernel, grid, info, operands, outs, scratch, flops, room, onto=None):
    arrays = [x if spec else in_vmem(x) for x, spec in operands]
    shapes = [x if spec else pltpu.VMEM(x.shape, x.dtype) for x, spec in outs]
    moved = sum(x.size * x.dtype.itemsize for x, spec in (*operands, *outs) if spec)
    return pl.pallas_call(
        kernel,
        grid_spec=pltpu.PrefetchScalarGridSpec(
            num_scalar_prefetch=1,
            grid=(grid,),
            in_specs=[spec or KEPT for _, spec in operands],
            out_specs=[spec or KEPT for _, spec in outs],
            scratch_shapes=scratch,
        ),
        out_shape=shapes,
        input_output_aliases=onto or {},
        compiler_params=pltpu.CompilerParams(
            vmem_limit_bytes=room * MIB, dimension_semantics=("arbitrary",)
        ),
        cost_estimate=pl.CostEstimate(flops=flops // HINT, bytes_accessed=moved // HINT, transcendentals=0),
    )(info, *arrays)


def at_home(value):
    return pltpu.with_memory_space_constraint(value, pltpu.HBM)


def shape_of(*shape, dtype=LOW):
    return jax.ShapeDtypeStruct(shape, dtype)


def tiled(width, place=lambda i: i):
    return pl.BlockSpec((TILE, width), lambda i, info: (place(i), 0))


def fixed(*shape, at=(0, 0)):
    return pl.BlockSpec(shape, lambda i, info: at)


KEPT = pl.BlockSpec(memory_space=pltpu.VMEM)


class Wires:
    def __init__(self, dp, cores, channels):
        self.rest = dp // 4
        assert dp == self.rest * 4 and self.rest & (self.rest - 1) == 0 and cores == 2
        self.devices = dp * 2
        self.rows = channels // self.devices
        self.direct = self.rows % 16 == 0
        self.dp = lax.axis_index(AXES[0])
        self.core = lax.axis_index(AXES[1])
        every = range(self.devices)
        self.sibling = [(i, i ^ 1) for i in every]
        self.first = [(i, i ^ (4 if i % 2 else 2)) for i in every]
        self.second = [(i, i ^ (2 if i % 2 else 4)) for i in every]

    def along_rest(self, distance):
        return [(i, i ^ (8 * distance)) for i in range(self.devices)]

    def hop(self, value, pairs):
        return lax.ppermute(value, AXES, pairs)

    def spread(self, blocks):
        return [blocks[0]] + [
            self.hop(blocks[k], self.along_rest(k)) for k in range(1, self.rest)
        ]

    def passed(self, *pieces):
        pieces = [*pieces, *(self.hop(piece, self.sibling) for piece in pieces)]
        return pieces if self.direct else [self.put_in_order(pieces)]

    def put_in_order(self, pieces):
        whole = jnp.zeros((self.rest, 2, 2, 2) + pieces[0].shape[1:], LOW)
        order = jnp.arange(self.rest) ^ (self.dp >> 2)
        for index, piece in enumerate(pieces):
            source = self.core ^ (index // 4)
            at_a, at_b = turned(self.dp, source, index % 2, (index // 2) % 2)
            whole = lax.dynamic_update_slice(
                whole, piece[order][:, None, None, None], (0, at_b, at_a, source, 0, 0)
            )
        return whole.reshape(-1, pieces[0].shape[2])

    def put_together(self, info_ref, pieces, w_ref):
        if not self.direct:
            w_ref[...] = pieces[0][...]
            return
        dp, core = info_ref[2], info_ref[3]
        for index, piece in enumerate(pieces):
            source = core ^ (index // 4)
            at_a, at_b = turned(dp, source, index % 2, (index // 2) % 2)
            for distance in range(self.rest):
                place = ((((dp >> 2) ^ distance) * 2 + at_b) * 2 + at_a) * 2 + source
                w_ref[rows_of(place, self.rows)] = piece[distance]

    def put_apart(self, info_ref, step, grads, here_ref, away_ref):
        start = 0
        for value in (grad.astype(LOW) for grad in grads):
            columns = slice(start, start + value.shape[1])
            start += value.shape[1]
            if not self.direct:
                here_ref[rows_of(step, value.shape[0]), columns] = value
                continue
            dp, core = info_ref[2], info_ref[3]
            blocks = value.shape[0] // self.rows
            for block in range(0, blocks, 2):
                at_b, at_a = (block // 4) % 2, (block // 2) % 2
                distance = (step * (blocks // 8) + block // 8) ^ (dp >> 2)
                on_a, on_b = at_a ^ (dp & 1), at_b ^ ((dp >> 1) & 1)
                even = value[block * self.rows : (block + 1) * self.rows]
                odd = value[(block + 1) * self.rows : (block + 2) * self.rows]
                first, second = jnp.where(core == 0, on_a, on_b), jnp.where(core == 0, on_b, on_a)
                here_ref[first, second, distance, :, columns] = jnp.where(core == 0, even, odd)
                away_ref[second, first, distance, :, columns] = jnp.where(core == 0, odd, even)

    def apart(self, depth):
        if not self.direct:
            return [(shape_of(self.devices * self.rows, depth), None), (shape_of(16, LANES), None)]
        return [(shape_of(2, 2, self.rest, self.rows, depth), None)] * 2

    def by_distance(self, full):
        rows = full.shape[0] // self.devices
        blocks = full.reshape(self.rest, 2, 2, 2, rows, full.shape[1])
        blocks = blocks[jnp.arange(self.rest) ^ (self.dp >> 2)]
        parts = []
        for away in range(2):
            source = self.core ^ away
            for first in range(2):
                for second in range(2):
                    at_a, at_b = turned(self.dp, source, first, second)
                    parts.append(
                        lax.dynamic_slice(
                            blocks,
                            (0, at_b, at_a, source, 0, 0),
                            (self.rest, 1, 1, 1, rows, full.shape[1]),
                        )[:, 0, 0, 0]
                    )
        return jnp.stack(parts).reshape(2, 2, 2, self.rest, rows, full.shape[1])


def turned(dp, owner, first, second):
    along_a = jnp.where(owner == 0, first, second)
    along_b = jnp.where(owner == 0, second, first)
    return (dp & 1) ^ along_a, ((dp >> 1) & 1) ^ along_b


def add_low(left, right):
    return (left.astype(FULL) + right.astype(FULL)).astype(LOW)


def per_device(
    dp,
    cores,
    samples,
    mel,
    lengths,
    hops,
    conv_weight,
    cond_weight,
    conv_bias,
    out_weight,
    out_bias,
    grad_out,
    grad_skip,
):
    sample_count, channels = samples.shape[1:]
    frame_count, mel_count = mel.shape[1:]
    layers = conv_weight.shape[0]
    size = Sizes(channels, mel_count)
    gate = size.gate
    wires = Wires(dp, cores, gate)
    assert layers == 2 and sample_count % TILE == 0 and TILE == FIRST_DILATION
    steps = sample_count // TILE
    where = jnp.stack([wires.dp, wires.core]).astype(jnp.int32)
    info = jnp.concatenate([lengths, hops, where])
    x, go, gs = samples[0], grad_out[0], grad_skip[0]
    conv_t, cond_t, out_t = (
        w.swapaxes(1, 2) for w in (conv_weight, cond_weight, out_weight)
    )
    rows = conv_t.shape[1]
    sources = (conv_t, cond_t, conv_bias, out_t, out_bias, mel[0])
    own0, own1, mel_table = pl.pallas_call(
        functools.partial(pack_layers, layers),
        in_specs=[pl.BlockSpec(memory_space=pl.ANY)] * len(sources),
        out_shape=[shape_of(rows, size.pack)] * layers + [shape_of(LANES, size.extra_width)],
        scratch_shapes=[pltpu.VMEM(source.shape, LOW) for source in sources]
        + [pltpu.VMEM((LANES, size.extra_width), FULL), pltpu.SemaphoreType.DMA((len(sources),))],
        compiler_params=pltpu.CompilerParams(vmem_limit_bytes=ROOM_SMALL * MIB),
    )(*map(at_home, sources))
    last_shape = shape_of(wires.rest, rows, size.pack)
    half_shape = shape_of(2, wires.rest, rows, size.pack)
    blocks_shape = [shape_of(rows, size.pack)] * wires.rest
    side_by_side = lambda blocks: plain(put_side_by_side, blocks, [last_shape])[0]
    table = fixed(LANES, size.extra_width)
    macs = sample_count * channels * channels
    assert gate % PART == 0 and gate % PART_0 == 0 and sample_count % WIDE == 0
    kept = lambda *columns: [(shape_of(sample_count, c), None) for c in columns]
    whole_w = (shape_of(gate, size.pack), None)
    parts = gate // PART
    mel_sums = (shape_of(LANES, size.extra_width, dtype=FULL), table)
    frame_sums = (shape_of(gate, LANES, dtype=FULL), None)
    scratch = lambda *shape: pltpu.VMEM(shape, LOW)

    blocked = (shape_of(sample_count, channels), tiled(channels))
    keep = lambda *values: [(value, None) for value in values]

    near0 = wires.spread([own0] * wires.rest)
    taps0, proj1 = call(
        functools.partial(prepare, size),
        steps,
        info,
        [*((at_home(value), tiled(channels)) for value in (x, go, gs)), (mel_table, table)],
        kept(gate + size.extra_width + LANES, gate),
        [],
        macs,
        ROOM_0,
    )
    taps0, proj1, *near0 = lax.optimization_barrier((taps0, proj1, *near0))
    mine0 = side_by_side(near0)
    one0, two0 = wires.hop(mine0, wires.first), wires.hop(mine0, wires.second)
    own1, _ = lax.optimization_barrier((own1, mine0))
    (own1,) = plain(hand_on, (own1,), [shape_of(rows, size.pack)])
    near1 = wires.spread([own1] * wires.rest)
    near1 = lax.optimization_barrier(near1[::-1])[::-1]
    mine1 = side_by_side(near1)
    mine1, two0, one0 = lax.optimization_barrier((mine1, two0, one0))
    far0 = wires.hop(one0, wires.second)
    one1, two1 = wires.hop(mine1, wires.first), wires.hop(mine1, wires.second)
    two1, one1, far0 = lax.optimization_barrier((two1, one1, far0))
    pieces0 = wires.passed(mine0, one0, two0, far0)
    taps1, gated0, slope0, w0 = call(
        functools.partial(forward_0, size, wires),
        sample_count // WIDE,
        info,
        keep(taps0, *pieces0),
        [*kept(gate + size.extra_width + LANES, channels, gate), whole_w],
        [pltpu.VMEM((1, channels), FULL), pltpu.VMEM((8, channels), FULL)],
        10 * macs,
        ROOM_0,
    )
    far1 = wires.hop(one1, wires.second)
    far1, taps1 = lax.optimization_barrier((far1, taps1))
    gated1, pre1, w1, sums1, here1, away1 = call(
        functools.partial(layer_1, size, wires, steps),
        steps + parts,
        info,
        keep(taps1, proj1, *wires.passed(mine1, one1, two1, far1)),
        [*kept(channels, gate), whole_w, frame_sums, *wires.apart(size.pack)],
        [],
        24 * macs,
        ROOM_1,
    )
    if not wires.direct:
        here1, away1 = wires.by_distance(here1)
    came1 = wires.hop(away1, wires.sibling)

    carry = (shape_of(8, channels, dtype=FULL), None)
    begun = call(
        functools.partial(backward_0, size, steps - 1),
        steps - steps // 2,
        info,
        keep(pre1, w1, w0, proj1, slope0),
        [*kept(gate, gate), carry],
        [],
        6 * macs,
        ROOM_2,
    )
    stay1, leave1 = plain(add_and_part, (here1, came1), [half_shape] * 2)
    begun, stay1, leave1 = lax.optimization_barrier((begun, stay1, leave1))
    came1 = wires.hop(leave1, wires.first)
    proj0, pre0, _ = call(
        functools.partial(backward_0, size, steps // 2 - 1),
        steps // 2,
        info,
        keep(pre1, w1, w0, proj1, slope0, *begun),
        [*kept(gate, gate), carry],
        [],
        6 * macs,
        ROOM_2,
        {6: 0, 7: 1},
    )

    cut = lambda depth, *lead: shape_of(*lead, wires.rest, rows, depth)
    depths = (size.now, size.pack - size.now)
    here_a, away_a = call(
        functools.partial(weights_0_early, size, wires),
        gate // PART_0,
        info,
        keep(pre0, proj0, taps0, gated0),
        wires.apart(depths[0]),
        [],
        7 * macs,
        ROOM_3,
    )
    sums0, here_b, away_b = call(
        functools.partial(weights_0_now, size, wires),
        gate // PART_0,
        info,
        keep(pre0, proj0, taps0),
        [frame_sums, *wires.apart(depths[1])],
        [],
        5 * macs,
        ROOM_3,
    )
    if not wires.direct:
        here_a, away_a = wires.by_distance(here_a)
        here_b, away_b = wires.by_distance(here_b)
    came_a = wires.hop(away_a, wires.sibling)
    came_a, here_b = lax.optimization_barrier((came_a, here_b))
    away_b, came1 = lax.optimization_barrier((away_b, came1))
    came_b = wires.hop(away_b, wires.sibling)
    stay_a, leave_a = plain(add_and_part, (here_a, came_a), [cut(depths[0], 2)] * 2)
    came_a = wires.hop(leave_a, wires.first)
    stay1, leave_a = lax.optimization_barrier((stay1, leave_a))
    stay1, leave1 = plain(add_and_part, (stay1, came1), [last_shape] * 2)
    came1 = wires.hop(leave1, wires.second)
    came_b, leave1 = lax.optimization_barrier((came_b, leave1))
    stay_b, leave_b = plain(add_and_part, (here_b, came_b), [cut(depths[1], 2)] * 2)
    came_b = wires.hop(leave_b, wires.first)
    pre0, taps1, leave_b = lax.optimization_barrier((pre0, taps1, leave_b))

    (samples_grad,) = call(
        functools.partial(samples_gradient, size),
        steps,
        info,
        keep(proj0, pre0, w0),
        [(shape_of(sample_count, channels, dtype=FULL), tiled(channels))],
        [],
        8 * macs,
        ROOM_4,
    )
    residual_out, skip_output_sum, mel_grad = call(
        functools.partial(forward_outputs, size),
        steps,
        info,
        keep(taps1, gated0, gated1, w0, w1, sums0, sums1),
        [blocked, blocked, mel_sums],
        [pltpu.VMEM((1, gate), FULL)],
        8 * macs,
        ROOM_5,
    )
    came_a, came_b, came1, samples_grad, residual_out = lax.optimization_barrier(
        (came_a, came_b, came1, samples_grad, residual_out)
    )
    parts1 = lax.optimization_barrier(wires.spread(plain(add_and_part, (stay1, came1), blocks_shape))[::-1])[::-1]
    stay0, leave0 = plain(add_both, (stay_a, came_a, stay_b, came_b), [last_shape] * 2)
    came0 = wires.hop(leave0, wires.second)
    parts0 = wires.spread(plain(add_and_part, (stay0, came0), blocks_shape))
    grads = plain(
        functools.partial(unpack_layers, layers, mel_count),
        (*parts0, *parts1),
        [
            shape_of(layers, rows, 2 * channels, dtype=FULL),
            shape_of(layers, rows, mel_count, dtype=FULL),
            shape_of(layers, rows, dtype=FULL),
            shape_of(layers, rows, channels, dtype=FULL),
            shape_of(layers, rows, dtype=FULL),
        ],
        at_end=True,
    )
    conv_grad, cond_grad, conv_b_grad, out_grad, out_b_grad = grads
    return (
        residual_out[None],
        skip_output_sum[None],
        samples_grad[None],
        mel_grad[:frame_count, :mel_count][None],
        conv_grad.swapaxes(1, 2),
        cond_grad.swapaxes(1, 2),
        conv_b_grad,
        out_grad.swapaxes(1, 2),
        out_b_grad,
    )


def solution(mesh):
    dp, cores = mesh.shape["dp"], mesh.shape["group"]

    def everything(*arrays):
        return per_device(dp, cores, *arrays)

    clips = P(AXES, None, None)
    columns = P(None, None, AXES)
    biases = P(None, AXES)
    return jax.shard_map(
        everything,
        mesh=mesh,
        in_specs=(
            clips, clips, P(AXES), P(AXES), columns, columns, biases, columns, biases, clips, clips,
        ),
        out_specs=(clips, clips, clips, clips, columns, columns, biases, columns, biases),
        check_vma=False,
    )
```

```python
import functools

import jax
import jax.numpy as jnp
from jax import lax
from jax.experimental import pallas as pl
from jax.experimental.pallas import tpu as pltpu
from jax.sharding import PartitionSpec as P

FIRST_DILATION = 512
AXES = ("dp", "group")
LANES = 128
TILE = 512
WIDE = 1024
PART = 512
PART_0 = 1024
MIB = 1024 * 1024
HINT = 4
ROOM_0, ROOM_1, ROOM_2, ROOM_3, ROOM_4, ROOM_5, ROOM_SMALL = 7, 8, 8, 7, 6, 6, 6
LOW = jnp.bfloat16
FULL = jnp.float32


def dot(left, right):
    return jnp.dot(left, right, preferred_element_type=FULL)


def dot_cols(left, right, **more):
    return lax.dot_general(
        left, right, (((1,), (1,)), ((), ())), preferred_element_type=FULL, **more
    )


def dot_rows(left, right, **more):
    return lax.dot_general(
        left, right, (((0,), (0,)), ((), ())), preferred_element_type=FULL, **more
    )


class Sizes:
    def __init__(self, channels, mel_count):
        self.channels = channels
        self.gate = 2 * channels
        self.mel = mel_count
        self.early = channels
        self.now = 2 * channels
        self.extra = 3 * channels
        self.extra_width = -(-(mel_count + 2) // LANES) * LANES
        self.pack = self.extra + self.extra_width


def mask_of(info_ref, start, rows):
    places = start + lax.broadcasted_iota(jnp.int32, (rows, 1), 0)
    return (places < info_ref[0]).astype(FULL)


def frames_of(info_ref, start, rows):
    places = start + lax.broadcasted_iota(jnp.int32, (rows, LANES), 0)
    first = lax.broadcasted_iota(jnp.int32, (rows, LANES), 1) * info_ref[1]
    return ((places >= first) & (places < first + info_ref[1])).astype(FULL).astype(LOW)


def masked(value, mask):
    return (value.astype(FULL) * mask).astype(LOW)


def out_bias_row(size, extra):
    column = lax.broadcasted_iota(jnp.int32, (8, size.extra_width), 1)
    pick = (column == size.mel + 1).astype(FULL).astype(LOW)
    return dot_cols(pick, extra)[0:1]


def gates(taps, w_ref, size, side):
    channels = size.channels
    width = channels // 2
    low = slice(side * width, (side + 1) * width)
    high = slice(channels + side * width, channels + (side + 1) * width)
    tangent = jnp.tanh(dot_cols(taps, w_ref[low, size.early :]))
    sig_gate = 0.5 * jnp.tanh(0.5 * dot_cols(taps, w_ref[high, size.early :])) + 0.5
    gated = tangent * sig_gate
    return low, high, gated, sig_gate * (1.0 - tangent * tangent), gated * (1.0 - sig_gate)


def rows_of(step, rows):
    return pl.ds(pl.multiple_of(step * rows, rows), rows)


def prepare(size, info_ref, x_ref, go_ref, gs_ref, mel_ref, taps0_ref, proj1_ref):
    step = pl.program_id(0)
    channels = size.channels
    tile = rows_of(step, TILE)
    mask = mask_of(info_ref, step * TILE, TILE)
    low = masked(x_ref[...], mask)
    taps0_ref[tile, channels : 2 * channels] = low

    @pl.when(step == 0)
    def _():
        taps0_ref[:TILE, :channels] = jnp.zeros((TILE, channels), LOW)

    @pl.when(step < pl.num_programs(0) - 1)
    def _():
        taps0_ref[rows_of(step + 1, TILE), :channels] = low

    proj1_ref[tile, :channels] = masked(go_ref[...], mask)
    proj1_ref[tile, channels:] = masked(gs_ref[...], mask)
    frames = frames_of(info_ref, step * TILE, TILE)
    place = 2 * channels + size.extra_width
    taps0_ref[tile, 2 * channels : place] = dot(frames, mel_ref[...]).astype(LOW)
    taps0_ref[tile, place:] = frames


def forward_0(size, wires, info_ref, taps0_ref, *refs):
    count = 8 if wires.direct else 1
    pieces, refs = refs[:count], refs[count:]
    taps1_ref, gated_ref, slope_ref, w_ref, bias_s, carry_s = refs
    step = pl.program_id(0)
    channels = size.channels

    @pl.when(step == 0)
    def _():
        wires.put_together(info_ref, pieces, w_ref)
        bias_s[...] = out_bias_row(size, w_ref[:channels, size.extra :])
        carry_s[...] = jnp.zeros_like(carry_s)

    tile = rows_of(step, WIDE)
    mask = mask_of(info_ref, step * WIDE, WIDE)
    taps = taps0_ref[tile, : size.pack - channels]
    for side in range(2):
        first, second, gated, slope_a, slope_b = gates(taps, w_ref, size, side)
        gated_ref[tile, first] = gated.astype(LOW)
        slope_ref[tile, first] = slope_a.astype(LOW)
        slope_ref[tile, second] = slope_b.astype(LOW)
    moved = dot_cols(gated_ref[tile], w_ref[:channels, :channels])
    hidden = taps0_ref[tile, channels : 2 * channels].astype(FULL)
    low = ((hidden + moved + bias_s[...]) * mask).astype(LOW)
    wide = low.astype(FULL)
    place = lax.broadcasted_iota(jnp.int32, (WIDE, 1), 0)
    prev = jnp.where(place == 0, carry_s[7:8], pltpu.roll(wide, 1, 0)).astype(LOW)
    taps1_ref[tile, :channels] = prev
    taps1_ref[tile, channels : 2 * channels] = low
    taps1_ref[tile, 2 * channels :] = taps0_ref[tile, 2 * channels :]
    carry_s[...] = wide[WIDE - 8 :]


def layer_1(size, wires, steps, info_ref, taps_ref, proj_ref, *refs):
    count = 8 if wires.direct else 1
    pieces, refs = refs[:count], refs[count:]
    gated_ref, pre_ref, w_ref, sums_ref, here_ref, away_ref = refs
    step = pl.program_id(0)
    channels = size.channels

    @pl.when(step == 0)
    def _():
        wires.put_together(info_ref, pieces, w_ref)

    @pl.when(step < steps)
    def _():
        tile = rows_of(step, TILE)
        taps = taps_ref[tile, : size.pack - channels]
        grad_gated = dot(proj_ref[tile], w_ref[:, :channels])
        for side in range(2):
            first, second, gated, slope_a, slope_b = gates(taps, w_ref, size, side)
            gated_ref[tile, first] = gated.astype(LOW)
            pre_ref[tile, first] = (grad_gated[:, first] * slope_a).astype(LOW)
            pre_ref[tile, second] = (grad_gated[:, first] * slope_b).astype(LOW)

    @pl.when(step >= steps)
    def _():
        part = rows_of(step - steps, PART)
        proj = proj_ref[:, part]
        both = dot_rows(pre_ref[:, part], taps_ref[...])
        sums_ref[part] = both[:, size.pack - channels :]
        grads = [
            dot_rows(proj, gated_ref[...]),
            both[:, : 2 * channels],
            extra_grads(size, both[:, 2 * channels : size.pack - channels], proj),
        ]
        wires.put_apart(info_ref, step - steps, grads, here_ref, away_ref)


def in_two(value):
    high = value.astype(LOW)
    return high, (value - high.astype(FULL)).astype(LOW)


def extra_grads(size, extra, proj):
    total = jnp.sum(proj.astype(FULL), axis=0, keepdims=True)
    bias = jnp.broadcast_to(total, (LANES, total.shape[1])).T[:, 0:1]
    column = lax.broadcasted_iota(jnp.int32, extra.shape, 1)
    return jnp.where(column == size.mel + 1, bias, extra)


def backward_0(size, last, info_ref, pre1_ref, w1_ref, w0_ref, proj1_ref, slope_ref, *refs):
    before, (proj_ref, pre0_ref, carry_ref) = refs[:-3], refs[-3:]
    step = pl.program_id(0)
    channels = size.channels
    index = last - step
    tile = rows_of(index, WIDE)
    mask = mask_of(info_ref, index * WIDE, WIDE)

    @pl.when(step == 0)
    def _():
        carry_ref[...] = before[2][...] if before else jnp.zeros_like(carry_ref)

    pre1 = pre1_ref[tile]
    early = dot(pre1, w1_ref[:, size.early : size.now])
    place = lax.broadcasted_iota(jnp.int32, (WIDE, 1), 0)
    later = jnp.where(place == WIDE - 1, carry_ref[0:1], pltpu.roll(early, WIDE - 1, 0))
    carry_ref[...] = early[:8]
    now = dot(pre1, w1_ref[:, size.now : size.extra])
    res = ((proj1_ref[tile, :channels].astype(FULL) + now + later) * mask).astype(LOW)
    proj_ref[tile, :channels] = res
    proj_ref[tile, channels:] = proj1_ref[tile, channels:]
    grad_gated = dot(proj_ref[tile], w0_ref[:, :channels])
    for half in (slice(0, channels), slice(channels, 2 * channels)):
        pre0_ref[tile, half] = (grad_gated * slope_ref[tile, half].astype(FULL)).astype(LOW)


def weights_0_early(size, wires, info_ref, pre_ref, proj_ref, taps_ref, gated_ref, here_ref, away_ref):
    step = pl.program_id(0)
    now = slice(size.channels, 2 * size.channels)
    part = rows_of(step, PART_0)
    shift = FIRST_DILATION
    grads = [
        dot_rows(proj_ref[:, part], gated_ref[...]),
        dot_rows(pre_ref[shift:, part], taps_ref[: taps_ref.shape[0] - shift, now]),
    ]
    wires.put_apart(info_ref, step, grads, here_ref, away_ref)


def weights_0_now(size, wires, info_ref, pre_ref, proj_ref, taps_ref, sums_ref, here_ref, away_ref):
    step = pl.program_id(0)
    part = rows_of(step, PART_0)
    channels = size.channels
    both = dot_rows(pre_ref[:, part], taps_ref[:, channels:])
    sums_ref[part] = both[:, channels + size.extra_width :]
    grads = [
        both[:, :channels],
        extra_grads(size, both[:, channels : channels + size.extra_width], proj_ref[:, part]),
    ]
    wires.put_apart(info_ref, step, grads, here_ref, away_ref)


def samples_gradient(size, info_ref, proj_ref, pre_ref, w0_ref, sg_ref):
    step = pl.program_id(0)
    tile = rows_of(step, TILE)
    grad = proj_ref[tile, : size.channels].astype(FULL) + dot(pre_ref[tile], w0_ref[:, size.now : size.extra])
    after = rows_of(jnp.minimum(step + 1, pl.num_programs(0) - 1), TILE)
    later = dot(pre_ref[after], w0_ref[:, size.early : size.now])
    grad = grad + jnp.where(step < pl.num_programs(0) - 1, later, 0.0)
    sg_ref[...] = grad * mask_of(info_ref, step * TILE, TILE)


def forward_outputs(size, info_ref, taps1_ref, gated0_ref, gated1_ref, w0_ref, w1_ref, sums0_ref, sums1_ref, res_ref, skip_ref, mel_ref, bias_s):
    step = pl.program_id(0)
    channels = size.channels

    @pl.when(step == 0)
    def _():
        bias_s[...] = out_bias_row(size, w1_ref[:, size.extra :])
        bias_s[:, channels:] += out_bias_row(size, w0_ref[channels:, size.extra :])
        mel_ref[...] = sum(
            dot_rows(half, w_ref[:, size.extra :])
            for sums_ref, w_ref in ((sums0_ref, w0_ref), (sums1_ref, w1_ref))
            for half in in_two(sums_ref[...])
        )

    tile = rows_of(step, TILE)
    mask = mask_of(info_ref, step * TILE, TILE)
    res = dot_cols(gated1_ref[tile], w1_ref[:channels, :channels]) + bias_s[:, :channels]
    res_ref[...] = ((taps1_ref[tile, channels : 2 * channels].astype(FULL) + res) * mask).astype(LOW)
    skip = dot_cols(gated0_ref[tile], w0_ref[channels:, :channels])
    skip = skip + dot_cols(gated1_ref[tile], w1_ref[channels:, :channels])
    skip_ref[...] = ((skip + bias_s[:, channels:]) * mask).astype(LOW)


def add_and_part(left_ref, right_ref, *refs):
    for index, ref in enumerate(refs):
        ref[...] = add_low(left_ref[index], right_ref[index])


def mel_rows(mel_ref, table_ref, wide_s):
    frames, mel = mel_ref.shape
    wide_s[...] = jnp.zeros_like(wide_s)
    wide_s[:frames, :mel] = mel_ref[...].astype(FULL)
    wide_s[:frames, mel : mel + 1] = jnp.ones((frames, 1), FULL)
    table_ref[...] = wide_s[...].astype(LOW)


def add_both(left_a, right_a, left_b, right_b, *refs):
    cut = left_a.shape[-1]
    for index, ref in enumerate(refs):
        ref[..., :cut] = add_low(left_a[index], right_a[index])
        ref[..., cut:] = add_low(left_b[index], right_b[index])


def hand_on(from_ref, to_ref):
    to_ref[...] = from_ref[...]


def put_side_by_side(*refs):
    for index, ref in enumerate(refs[:-1]):
        refs[-1][index] = ref[...]


def pack_layers(layers, *refs):
    sources, packs, table_ref = refs[:6], refs[6 : 6 + layers], refs[6 + layers]
    kept, wide_s, sems = refs[7 + layers : 13 + layers], refs[-2], refs[-1]
    copies = [
        pltpu.make_async_copy(source, to, sems.at[index])
        for index, (source, to) in enumerate(zip(sources, kept))
    ]
    for copy in copies:
        copy.start()
    for copy in copies:
        copy.wait()
    conv_ref, cond_ref, conv_b_ref, out_ref, out_b_ref, mel_ref = kept
    mel_rows(mel_ref, table_ref, wide_s)
    rows = conv_ref.shape[1]
    same = lax.broadcasted_iota(jnp.int32, (rows, rows), 0)
    same = (same == lax.broadcasted_iota(jnp.int32, (rows, rows), 1)).astype(FULL).astype(LOW)
    biases = dot_cols(same, jnp.concatenate([conv_b_ref[...], out_b_ref[...]], axis=0))
    early, extra = out_ref.shape[2], out_ref.shape[2] + conv_ref.shape[2]
    mel = cond_ref.shape[2]
    for layer, to_ref in enumerate(packs):
        width = to_ref.shape[1] - extra
        place = lax.broadcasted_iota(jnp.int32, (rows, width), 1)
        cond = jnp.concatenate(
            [cond_ref[layer].astype(FULL), jnp.zeros((rows, width - mel), FULL)], axis=1
        )
        cond = jnp.where(place == mel, biases[:, layer : layer + 1], cond)
        cond = jnp.where(place == mel + 1, biases[:, layers + layer : layers + layer + 1], cond)
        to_ref[:, :early] = out_ref[layer]
        to_ref[:, early:extra] = conv_ref[layer]
        to_ref[:, extra:] = cond.astype(LOW)


def unpack_layers(layers, mel, *refs):
    conv_ref, cond_ref, conv_b_ref, out_ref, out_b_ref = refs[-5:]
    count = (len(refs) - 5) // layers
    rows = conv_ref.shape[1]
    same = lax.broadcasted_iota(jnp.int32, (rows, rows), 0)
    same = (same == lax.broadcasted_iota(jnp.int32, (rows, rows), 1)).astype(FULL)
    early, extra = out_ref.shape[2], out_ref.shape[2] + conv_ref.shape[2]
    for layer in range(layers):
        total = sum(ref[...].astype(FULL) for ref in refs[layer * count : (layer + 1) * count])
        out_ref[layer] = total[:, :early]
        conv_ref[layer] = total[:, early:extra]
        cond_ref[layer] = total[:, extra : extra + mel]
        biases = dot_rows(total[:, extra:], same, precision=lax.Precision.HIGHEST)
        conv_b_ref[layer : layer + 1] = biases[mel : mel + 1]
        out_b_ref[layer : layer + 1] = biases[mel + 1 : mel + 2]


def in_vmem(value):
    return pltpu.with_memory_space_constraint(value, pltpu.VMEM)


def plain(kernel, operands, outs, at_end=False):
    shapes = outs if at_end else [pltpu.VMEM(x.shape, x.dtype) for x in outs]
    return pl.pallas_call(
        kernel,
        out_shape=shapes,
        in_specs=[KEPT] * len(operands),
        out_specs=[KEPT] * len(outs),
        compiler_params=pltpu.CompilerParams(vmem_limit_bytes=ROOM_SMALL * MIB),
    )(*map(in_vmem, operands))


def call(kernel, grid, info, operands, outs, scratch, flops, room, onto=None):
    arrays = [x if spec else in_vmem(x) for x, spec in operands]
    shapes = [x if spec else pltpu.VMEM(x.shape, x.dtype) for x, spec in outs]
    moved = sum(x.size * x.dtype.itemsize for x, spec in (*operands, *outs) if spec)
    return pl.pallas_call(
        kernel,
        grid_spec=pltpu.PrefetchScalarGridSpec(
            num_scalar_prefetch=1,
            grid=(grid,),
            in_specs=[spec or KEPT for _, spec in operands],
            out_specs=[spec or KEPT for _, spec in outs],
            scratch_shapes=scratch,
        ),
        out_shape=shapes,
        input_output_aliases=onto or {},
        compiler_params=pltpu.CompilerParams(
            vmem_limit_bytes=room * MIB, dimension_semantics=("arbitrary",)
        ),
        cost_estimate=pl.CostEstimate(flops=flops // HINT, bytes_accessed=moved // HINT, transcendentals=0),
    )(info, *arrays)


def at_home(value):
    return pltpu.with_memory_space_constraint(value, pltpu.HBM)


def shape_of(*shape, dtype=LOW):
    return jax.ShapeDtypeStruct(shape, dtype)


def tiled(width, place=lambda i: i):
    return pl.BlockSpec((TILE, width), lambda i, info: (place(i), 0))


def fixed(*shape, at=(0, 0)):
    return pl.BlockSpec(shape, lambda i, info: at)


KEPT = pl.BlockSpec(memory_space=pltpu.VMEM)


class Wires:
    def __init__(self, dp, cores, channels):
        self.rest = dp // 4
        assert dp == self.rest * 4 and self.rest & (self.rest - 1) == 0 and cores == 2
        self.devices = dp * 2
        self.rows = channels // self.devices
        self.direct = self.rows % 16 == 0
        self.dp = lax.axis_index(AXES[0])
        self.core = lax.axis_index(AXES[1])
        every = range(self.devices)
        self.sibling = [(i, i ^ 1) for i in every]
        self.first = [(i, i ^ (4 if i % 2 else 2)) for i in every]
        self.second = [(i, i ^ (2 if i % 2 else 4)) for i in every]

    def along_rest(self, distance):
        return [(i, i ^ (8 * distance)) for i in range(self.devices)]

    def hop(self, value, pairs):
        return lax.ppermute(value, AXES, pairs)

    def spread(self, blocks):
        return [blocks[0]] + [
            self.hop(blocks[k], self.along_rest(k)) for k in range(1, self.rest)
        ]

    def passed(self, *pieces):
        pieces = [*pieces, *(self.hop(piece, self.sibling) for piece in pieces)]
        return pieces if self.direct else [self.put_in_order(pieces)]

    def put_in_order(self, pieces):
        whole = jnp.zeros((self.rest, 2, 2, 2) + pieces[0].shape[1:], LOW)
        order = jnp.arange(self.rest) ^ (self.dp >> 2)
        for index, piece in enumerate(pieces):
            source = self.core ^ (index // 4)
            at_a, at_b = turned(self.dp, source, index % 2, (index // 2) % 2)
            whole = lax.dynamic_update_slice(
                whole, piece[order][:, None, None, None], (0, at_b, at_a, source, 0, 0)
            )
        return whole.reshape(-1, pieces[0].shape[2])

    def put_together(self, info_ref, pieces, w_ref):
        if not self.direct:
            w_ref[...] = pieces[0][...]
            return
        dp, core = info_ref[2], info_ref[3]
        for index, piece in enumerate(pieces):
            source = core ^ (index // 4)
            at_a, at_b = turned(dp, source, index % 2, (index // 2) % 2)
            for distance in range(self.rest):
                place = ((((dp >> 2) ^ distance) * 2 + at_b) * 2 + at_a) * 2 + source
                w_ref[rows_of(place, self.rows)] = piece[distance]

    def put_apart(self, info_ref, step, grads, here_ref, away_ref):
        start = 0
        for value in (grad.astype(LOW) for grad in grads):
            columns = slice(start, start + value.shape[1])
            start += value.shape[1]
            if not self.direct:
                here_ref[rows_of(step, value.shape[0]), columns] = value
                continue
            dp, core = info_ref[2], info_ref[3]
            blocks = value.shape[0] // self.rows
            for block in range(0, blocks, 2):
                at_b, at_a = (block // 4) % 2, (block // 2) % 2
                distance = (step * (blocks // 8) + block // 8) ^ (dp >> 2)
                on_a, on_b = at_a ^ (dp & 1), at_b ^ ((dp >> 1) & 1)
                even = value[block * self.rows : (block + 1) * self.rows]
                odd = value[(block + 1) * self.rows : (block + 2) * self.rows]
                first, second = jnp.where(core == 0, on_a, on_b), jnp.where(core == 0, on_b, on_a)
                here_ref[first, second, distance, :, columns] = jnp.where(core == 0, even, odd)
                away_ref[second, first, distance, :, columns] = jnp.where(core == 0, odd, even)

    def apart(self, depth):
        if not self.direct:
            return [(shape_of(self.devices * self.rows, depth), None), (shape_of(16, LANES), None)]
        return [(shape_of(2, 2, self.rest, self.rows, depth), None)] * 2

    def by_distance(self, full):
        rows = full.shape[0] // self.devices
        blocks = full.reshape(self.rest, 2, 2, 2, rows, full.shape[1])
        blocks = blocks[jnp.arange(self.rest) ^ (self.dp >> 2)]
        parts = []
        for away in range(2):
            source = self.core ^ away
            for first in range(2):
                for second in range(2):
                    at_a, at_b = turned(self.dp, source, first, second)
                    parts.append(
                        lax.dynamic_slice(
                            blocks,
                            (0, at_b, at_a, source, 0, 0),
                            (self.rest, 1, 1, 1, rows, full.shape[1]),
                        )[:, 0, 0, 0]
                    )
        return jnp.stack(parts).reshape(2, 2, 2, self.rest, rows, full.shape[1])


def turned(dp, owner, first, second):
    along_a = jnp.where(owner == 0, first, second)
    along_b = jnp.where(owner == 0, second, first)
    return (dp & 1) ^ along_a, ((dp >> 1) & 1) ^ along_b


def add_low(left, right):
    return (left.astype(FULL) + right.astype(FULL)).astype(LOW)


def per_device(
    dp,
    cores,
    samples,
    mel,
    lengths,
    hops,
    conv_weight,
    cond_weight,
    conv_bias,
    out_weight,
    out_bias,
    grad_out,
    grad_skip,
):
    sample_count, channels = samples.shape[1:]
    frame_count, mel_count = mel.shape[1:]
    layers = conv_weight.shape[0]
    size = Sizes(channels, mel_count)
    gate = size.gate
    wires = Wires(dp, cores, gate)
    assert layers == 2 and sample_count % TILE == 0 and TILE == FIRST_DILATION
    steps, wide_steps = sample_count // TILE, sample_count // WIDE
    where = jnp.stack([wires.dp, wires.core]).astype(jnp.int32)
    info = jnp.concatenate([lengths, hops, where])
    x, go, gs = samples[0], grad_out[0], grad_skip[0]
    conv_t, cond_t, out_t = (
        w.swapaxes(1, 2) for w in (conv_weight, cond_weight, out_weight)
    )
    rows = conv_t.shape[1]
    sources = (conv_t, cond_t, conv_bias, out_t, out_bias, mel[0])
    own0, own1, mel_table = pl.pallas_call(
        functools.partial(pack_layers, layers),
        in_specs=[pl.BlockSpec(memory_space=pl.ANY)] * len(sources),
        out_shape=[shape_of(rows, size.pack)] * layers + [shape_of(LANES, size.extra_width)],
        scratch_shapes=[pltpu.VMEM(source.shape, LOW) for source in sources]
        + [pltpu.VMEM((LANES, size.extra_width), FULL), pltpu.SemaphoreType.DMA((len(sources),))],
        compiler_params=pltpu.CompilerParams(vmem_limit_bytes=ROOM_SMALL * MIB),
    )(*map(at_home, sources))
    last_shape = shape_of(wires.rest, rows, size.pack)
    half_shape = shape_of(2, wires.rest, rows, size.pack)
    blocks_shape = [shape_of(rows, size.pack)] * wires.rest
    side_by_side = lambda blocks: plain(put_side_by_side, blocks, [last_shape])[0]
    table = fixed(LANES, size.extra_width)
    macs = sample_count * channels * channels
    assert gate % PART == 0 and gate % PART_0 == 0 and sample_count % WIDE == 0
    kept = lambda *columns: [(shape_of(sample_count, c), None) for c in columns]
    whole_w = (shape_of(gate, size.pack), None)
    parts = gate // PART
    mel_sums = (shape_of(LANES, size.extra_width, dtype=FULL), table)
    frame_sums = (shape_of(gate, LANES, dtype=FULL), None)
    scratch = lambda *shape: pltpu.VMEM(shape, LOW)

    blocked = (shape_of(sample_count, channels), tiled(channels))
    keep = lambda *values: [(value, None) for value in values]

    near0 = wires.spread([own0] * wires.rest)
    taps0, proj1 = call(
        functools.partial(prepare, size),
        steps,
        info,
        [*((at_home(value), tiled(channels)) for value in (x, go, gs)), (mel_table, table)],
        kept(gate + size.extra_width + LANES, gate),
        [],
        macs,
        ROOM_0,
    )
    taps0, proj1, *near0 = lax.optimization_barrier((taps0, proj1, *near0))
    mine0 = side_by_side(near0)
    one0, two0 = wires.hop(mine0, wires.first), wires.hop(mine0, wires.second)
    own1, _ = lax.optimization_barrier((own1, mine0))
    (own1,) = plain(hand_on, (own1,), [shape_of(rows, size.pack)])
    near1 = wires.spread([own1] * wires.rest)
    near1 = lax.optimization_barrier(near1[::-1])[::-1]
    mine1 = side_by_side(near1)
    mine1, two0, one0 = lax.optimization_barrier((mine1, two0, one0))
    far0 = wires.hop(one0, wires.second)
    one1, two1 = wires.hop(mine1, wires.first), wires.hop(mine1, wires.second)
    two1, one1, far0 = lax.optimization_barrier((two1, one1, far0))
    pieces0 = wires.passed(mine0, one0, two0, far0)
    taps1, gated0, slope0, w0 = call(
        functools.partial(forward_0, size, wires),
        sample_count // WIDE,
        info,
        keep(taps0, *pieces0),
        [*kept(gate + size.extra_width + LANES, channels, gate), whole_w],
        [pltpu.VMEM((1, channels), FULL), pltpu.VMEM((8, channels), FULL)],
        10 * macs,
        ROOM_0,
    )
    far1 = wires.hop(one1, wires.second)
    taps1, far1 = lax.optimization_barrier((taps1, far1))
    gated1, pre1, w1, sums1, here1, away1 = call(
        functools.partial(layer_1, size, wires, steps),
        steps + parts,
        info,
        keep(taps1, proj1, *wires.passed(mine1, one1, two1, far1)),
        [*kept(channels, gate), whole_w, frame_sums, *wires.apart(size.pack)],
        [],
        24 * macs,
        ROOM_1,
    )
    if not wires.direct:
        here1, away1 = wires.by_distance(here1)
    came1 = wires.hop(away1, wires.sibling)

    carry = (shape_of(8, channels, dtype=FULL), None)
    begun = call(
        functools.partial(backward_0, size, wide_steps - 1),
        wide_steps - wide_steps // 2,
        info,
        keep(pre1, w1, w0, proj1, slope0),
        [*kept(gate, gate), carry],
        [],
        6 * macs,
        ROOM_2,
    )
    stay1, leave1 = plain(add_and_part, (here1, came1), [half_shape] * 2)
    begun, stay1, leave1 = lax.optimization_barrier((begun, stay1, leave1))
    came1 = wires.hop(leave1, wires.first)
    proj0, pre0, _ = call(
        functools.partial(backward_0, size, wide_steps // 2 - 1),
        wide_steps // 2,
        info,
        keep(pre1, w1, w0, proj1, slope0, *begun),
        [*kept(gate, gate), carry],
        [],
        6 * macs,
        ROOM_2,
        {6: 0, 7: 1},
    )

    cut = lambda depth, *lead: shape_of(*lead, wires.rest, rows, depth)
    depths = (size.now, size.pack - size.now)
    here_a, away_a = call(
        functools.partial(weights_0_early, size, wires),
        gate // PART_0,
        info,
        keep(pre0, proj0, taps0, gated0),
        wires.apart(depths[0]),
        [],
        7 * macs,
        ROOM_3,
    )
    sums0, here_b, away_b = call(
        functools.partial(weights_0_now, size, wires),
        gate // PART_0,
        info,
        keep(pre0, proj0, taps0),
        [frame_sums, *wires.apart(depths[1])],
        [],
        5 * macs,
        ROOM_3,
    )
    if not wires.direct:
        here_a, away_a = wires.by_distance(here_a)
        here_b, away_b = wires.by_distance(here_b)
    came_a = wires.hop(away_a, wires.sibling)
    came_a, here_b = lax.optimization_barrier((came_a, here_b))
    away_b, came1 = lax.optimization_barrier((away_b, came1))
    came_b = wires.hop(away_b, wires.sibling)
    stay_a, leave_a = plain(add_and_part, (here_a, came_a), [cut(depths[0], 2)] * 2)
    came_a = wires.hop(leave_a, wires.first)
    stay1, leave_a = lax.optimization_barrier((stay1, leave_a))
    stay1, leave1 = plain(add_and_part, (stay1, came1), [last_shape] * 2)
    came1 = wires.hop(leave1, wires.second)
    came_b, leave1 = lax.optimization_barrier((came_b, leave1))
    stay_b, leave_b = plain(add_and_part, (here_b, came_b), [cut(depths[1], 2)] * 2)
    came_b = wires.hop(leave_b, wires.first)
    pre0, taps1, leave_b = lax.optimization_barrier((pre0, taps1, leave_b))

    (samples_grad,) = call(
        functools.partial(samples_gradient, size),
        steps,
        info,
        keep(proj0, pre0, w0),
        [(shape_of(sample_count, channels, dtype=FULL), tiled(channels))],
        [],
        8 * macs,
        ROOM_4,
    )
    residual_out, skip_output_sum, mel_grad = call(
        functools.partial(forward_outputs, size),
        steps,
        info,
        keep(taps1, gated0, gated1, w0, w1, sums0, sums1),
        [blocked, blocked, mel_sums],
        [pltpu.VMEM((1, gate), FULL)],
        8 * macs,
        ROOM_5,
    )
    came_a, came_b, came1, samples_grad, residual_out = lax.optimization_barrier(
        (came_a, came_b, came1, samples_grad, residual_out)
    )
    parts1 = lax.optimization_barrier(wires.spread(plain(add_and_part, (stay1, came1), blocks_shape))[::-1])[::-1]
    stay0, leave0 = plain(add_both, (stay_a, came_a, stay_b, came_b), [last_shape] * 2)
    came0 = wires.hop(leave0, wires.second)
    parts0 = wires.spread(plain(add_and_part, (stay0, came0), blocks_shape))
    grads = plain(
        functools.partial(unpack_layers, layers, mel_count),
        (*parts0, *parts1),
        [
            shape_of(layers, rows, 2 * channels, dtype=FULL),
            shape_of(layers, rows, mel_count, dtype=FULL),
            shape_of(layers, rows, dtype=FULL),
            shape_of(layers, rows, channels, dtype=FULL),
            shape_of(layers, rows, dtype=FULL),
        ],
        at_end=True,
    )
    conv_grad, cond_grad, conv_b_grad, out_grad, out_b_grad = grads
    return (
        residual_out[None],
        skip_output_sum[None],
        samples_grad[None],
        mel_grad[:frame_count, :mel_count][None],
        conv_grad.swapaxes(1, 2),
        cond_grad.swapaxes(1, 2),
        conv_b_grad,
        out_grad.swapaxes(1, 2),
        out_b_grad,
    )


def solution(mesh):
    dp, cores = mesh.shape["dp"], mesh.shape["group"]

    def everything(*arrays):
        return per_device(dp, cores, *arrays)

    clips = P(AXES, None, None)
    columns = P(None, None, AXES)
    biases = P(None, AXES)
    return jax.shard_map(
        everything,
        mesh=mesh,
        in_specs=(
            clips, clips, P(AXES), P(AXES), columns, columns, biases, columns, biases, clips, clips,
        ),
        out_specs=(clips, clips, clips, clips, columns, columns, biases, columns, biases),
        check_vma=False,
    )
```

```python
import functools

import jax
import jax.numpy as jnp
from jax import lax
from jax.experimental import pallas as pl
from jax.experimental.pallas import tpu as pltpu
from jax.sharding import PartitionSpec as P

FIRST_DILATION = 512
AXES = ("dp", "group")
LANES = 128
TILE = 512
WIDE = 1024
PART = 512
PART_0 = 1024
MIB = 1024 * 1024
HINT = 4
ROOM_0, ROOM_1, ROOM_2, ROOM_3, ROOM_4, ROOM_5, ROOM_SMALL = 7, 8, 8, 7, 6, 6, 6
LOW = jnp.bfloat16
FULL = jnp.float32


def dot(left, right):
    return jnp.dot(left, right, preferred_element_type=FULL)


def dot_cols(left, right, **more):
    return lax.dot_general(
        left, right, (((1,), (1,)), ((), ())), preferred_element_type=FULL, **more
    )


def dot_rows(left, right, **more):
    return lax.dot_general(
        left, right, (((0,), (0,)), ((), ())), preferred_element_type=FULL, **more
    )


class Sizes:
    def __init__(self, channels, mel_count):
        self.channels = channels
        self.gate = 2 * channels
        self.mel = mel_count
        self.early = channels
        self.now = 2 * channels
        self.extra = 3 * channels
        self.extra_width = -(-(mel_count + 2) // LANES) * LANES
        self.pack = self.extra + self.extra_width


def mask_of(info_ref, start, rows):
    places = start + lax.broadcasted_iota(jnp.int32, (rows, 1), 0)
    return (places < info_ref[0]).astype(FULL)


def frames_of(info_ref, start, rows):
    places = start + lax.broadcasted_iota(jnp.int32, (rows, LANES), 0)
    first = lax.broadcasted_iota(jnp.int32, (rows, LANES), 1) * info_ref[1]
    return ((places >= first) & (places < first + info_ref[1])).astype(FULL).astype(LOW)


def masked(value, mask):
    return (value.astype(FULL) * mask).astype(LOW)


def out_bias_row(size, extra):
    column = lax.broadcasted_iota(jnp.int32, (8, size.extra_width), 1)
    pick = (column == size.mel + 1).astype(FULL).astype(LOW)
    return dot_cols(pick, extra)[0:1]


def gates(taps, w_ref, size, side):
    channels = size.channels
    width = channels // 2
    low = slice(side * width, (side + 1) * width)
    high = slice(channels + side * width, channels + (side + 1) * width)
    tangent = jnp.tanh(dot_cols(taps, w_ref[low, size.early :]))
    sig_gate = 0.5 * jnp.tanh(0.5 * dot_cols(taps, w_ref[high, size.early :])) + 0.5
    gated = tangent * sig_gate
    return low, high, gated, sig_gate * (1.0 - tangent * tangent), gated * (1.0 - sig_gate)


def rows_of(step, rows):
    return pl.ds(pl.multiple_of(step * rows, rows), rows)


def prepare(size, info_ref, x_ref, go_ref, gs_ref, mel_ref, taps0_ref, proj1_ref):
    step = pl.program_id(0)
    channels = size.channels
    tile = rows_of(step, TILE)
    mask = mask_of(info_ref, step * TILE, TILE)
    low = masked(x_ref[...], mask)
    taps0_ref[tile, channels : 2 * channels] = low

    @pl.when(step == 0)
    def _():
        taps0_ref[:TILE, :channels] = jnp.zeros((TILE, channels), LOW)

    @pl.when(step < pl.num_programs(0) - 1)
    def _():
        taps0_ref[rows_of(step + 1, TILE), :channels] = low

    proj1_ref[tile, :channels] = masked(go_ref[...], mask)
    proj1_ref[tile, channels:] = masked(gs_ref[...], mask)
    frames = frames_of(info_ref, step * TILE, TILE)
    place = 2 * channels + size.extra_width
    taps0_ref[tile, 2 * channels : place] = dot(frames, mel_ref[...]).astype(LOW)
    taps0_ref[tile, place:] = frames


def forward_0(size, wires, info_ref, taps0_ref, *refs):
    count = 8 if wires.direct else 1
    pieces, refs = refs[:count], refs[count:]
    taps1_ref, gated_ref, slope_ref, w_ref, bias_s, carry_s = refs
    step = pl.program_id(0)
    channels = size.channels

    @pl.when(step == 0)
    def _():
        wires.put_together(info_ref, pieces, w_ref)
        bias_s[...] = out_bias_row(size, w_ref[:channels, size.extra :])
        carry_s[...] = jnp.zeros_like(carry_s)

    tile = rows_of(step, WIDE)
    mask = mask_of(info_ref, step * WIDE, WIDE)
    taps = taps0_ref[tile, : size.pack - channels]
    for side in range(2):
        first, second, gated, slope_a, slope_b = gates(taps, w_ref, size, side)
        gated_ref[tile, first] = gated.astype(LOW)
        slope_ref[tile, first] = slope_a.astype(LOW)
        slope_ref[tile, second] = slope_b.astype(LOW)
    moved = dot_cols(gated_ref[tile], w_ref[:channels, :channels])
    hidden = taps0_ref[tile, channels : 2 * channels].astype(FULL)
    low = ((hidden + moved + bias_s[...]) * mask).astype(LOW)
    wide = low.astype(FULL)
    place = lax.broadcasted_iota(jnp.int32, (WIDE, 1), 0)
    prev = jnp.where(place == 0, carry_s[7:8], pltpu.roll(wide, 1, 0)).astype(LOW)
    taps1_ref[tile, :channels] = prev
    taps1_ref[tile, channels : 2 * channels] = low
    taps1_ref[tile, 2 * channels :] = taps0_ref[tile, 2 * channels :]
    carry_s[...] = wide[WIDE - 8 :]


def layer_1(size, wires, steps, info_ref, taps_ref, proj_ref, *refs):
    count = 8 if wires.direct else 1
    pieces, refs = refs[:count], refs[count:]
    gated_ref, pre_ref, w_ref, sums_ref, here_ref, away_ref = refs
    step = pl.program_id(0)
    channels = size.channels

    @pl.when(step == 0)
    def _():
        wires.put_together(info_ref, pieces, w_ref)

    @pl.when(step < steps)
    def _():
        tile = rows_of(step, TILE)
        taps = taps_ref[tile, : size.pack - channels]
        grad_gated = dot(proj_ref[tile], w_ref[:, :channels])
        for side in range(2):
            first, second, gated, slope_a, slope_b = gates(taps, w_ref, size, side)
            gated_ref[tile, first] = gated.astype(LOW)
            pre_ref[tile, first] = (grad_gated[:, first] * slope_a).astype(LOW)
            pre_ref[tile, second] = (grad_gated[:, first] * slope_b).astype(LOW)

    @pl.when(step >= steps)
    def _():
        part = rows_of(step - steps, PART)
        proj = proj_ref[:, part]
        both = dot_rows(pre_ref[:, part], taps_ref[...])
        sums_ref[part] = both[:, size.pack - channels :]
        grads = [
            dot_rows(proj, gated_ref[...]),
            both[:, : 2 * channels],
            extra_grads(size, both[:, 2 * channels : size.pack - channels], proj),
        ]
        wires.put_apart(info_ref, step - steps, grads, here_ref, away_ref)


def in_two(value):
    high = value.astype(LOW)
    return high, (value - high.astype(FULL)).astype(LOW)


def extra_grads(size, extra, proj):
    total = jnp.sum(proj.astype(FULL), axis=0, keepdims=True)
    bias = jnp.broadcast_to(total, (LANES, total.shape[1])).T[:, 0:1]
    column = lax.broadcasted_iota(jnp.int32, extra.shape, 1)
    return jnp.where(column == size.mel + 1, bias, extra)


def backward_0(size, last, info_ref, pre1_ref, w1_ref, w0_ref, proj1_ref, slope_ref, *refs):
    before, (proj_ref, pre0_ref, carry_ref) = refs[:-3], refs[-3:]
    step = pl.program_id(0)
    channels = size.channels
    index = last - step
    tile = rows_of(index, WIDE)
    mask = mask_of(info_ref, index * WIDE, WIDE)

    @pl.when(step == 0)
    def _():
        carry_ref[...] = before[2][...] if before else jnp.zeros_like(carry_ref)

    pre1 = pre1_ref[tile]
    early = dot(pre1, w1_ref[:, size.early : size.now])
    place = lax.broadcasted_iota(jnp.int32, (WIDE, 1), 0)
    later = jnp.where(place == WIDE - 1, carry_ref[0:1], pltpu.roll(early, WIDE - 1, 0))
    carry_ref[...] = early[:8]
    now = dot(pre1, w1_ref[:, size.now : size.extra])
    res = ((proj1_ref[tile, :channels].astype(FULL) + now + later) * mask).astype(LOW)
    proj_ref[tile, :channels] = res
    proj_ref[tile, channels:] = proj1_ref[tile, channels:]
    grad_gated = dot(proj_ref[tile], w0_ref[:, :channels])
    for half in (slice(0, channels), slice(channels, 2 * channels)):
        pre0_ref[tile, half] = (grad_gated * slope_ref[tile, half].astype(FULL)).astype(LOW)


def weights_0_early(size, wires, info_ref, pre_ref, proj_ref, taps_ref, gated_ref, here_ref, away_ref):
    step = pl.program_id(0)
    now = slice(size.channels, 2 * size.channels)
    part = rows_of(step, PART_0)
    shift = FIRST_DILATION
    grads = [
        dot_rows(proj_ref[:, part], gated_ref[...]),
        dot_rows(pre_ref[shift:, part], taps_ref[: taps_ref.shape[0] - shift, now]),
    ]
    wires.put_apart(info_ref, step, grads, here_ref, away_ref)


def weights_0_now(size, wires, info_ref, pre_ref, proj_ref, taps_ref, sums_ref, here_ref, away_ref):
    step = pl.program_id(0)
    part = rows_of(step, PART_0)
    channels = size.channels
    both = dot_rows(pre_ref[:, part], taps_ref[:, channels:])
    sums_ref[part] = both[:, channels + size.extra_width :]
    grads = [
        both[:, :channels],
        extra_grads(size, both[:, channels : channels + size.extra_width], proj_ref[:, part]),
    ]
    wires.put_apart(info_ref, step, grads, here_ref, away_ref)


def samples_gradient(size, info_ref, proj_ref, pre_ref, w0_ref, sg_ref):
    step = pl.program_id(0)
    tile = rows_of(step, TILE)
    grad = proj_ref[tile, : size.channels].astype(FULL) + dot(pre_ref[tile], w0_ref[:, size.now : size.extra])
    after = rows_of(jnp.minimum(step + 1, pl.num_programs(0) - 1), TILE)
    later = dot(pre_ref[after], w0_ref[:, size.early : size.now])
    grad = grad + jnp.where(step < pl.num_programs(0) - 1, later, 0.0)
    sg_ref[...] = grad * mask_of(info_ref, step * TILE, TILE)


def forward_outputs(size, info_ref, taps1_ref, gated0_ref, gated1_ref, w0_ref, w1_ref, sums0_ref, sums1_ref, res_ref, skip_ref, mel_ref, bias_s):
    step = pl.program_id(0)
    channels = size.channels

    @pl.when(step == 0)
    def _():
        bias_s[...] = out_bias_row(size, w1_ref[:, size.extra :])
        bias_s[:, channels:] += out_bias_row(size, w0_ref[channels:, size.extra :])
        mel_ref[...] = sum(
            dot_rows(half, w_ref[:, size.extra :])
            for sums_ref, w_ref in ((sums0_ref, w0_ref), (sums1_ref, w1_ref))
            for half in in_two(sums_ref[...])
        )

    tile = rows_of(step, TILE)
    mask = mask_of(info_ref, step * TILE, TILE)
    res = dot_cols(gated1_ref[tile], w1_ref[:channels, :channels]) + bias_s[:, :channels]
    res_ref[...] = ((taps1_ref[tile, channels : 2 * channels].astype(FULL) + res) * mask).astype(LOW)
    skip = dot_cols(gated0_ref[tile], w0_ref[channels:, :channels])
    skip = skip + dot_cols(gated1_ref[tile], w1_ref[channels:, :channels])
    skip_ref[...] = ((skip + bias_s[:, channels:]) * mask).astype(LOW)


def add_and_part(left_ref, right_ref, *refs):
    for index, ref in enumerate(refs):
        ref[...] = add_low(left_ref[index], right_ref[index])


def mel_rows(mel_ref, table_ref, wide_s):
    frames, mel = mel_ref.shape
    wide_s[...] = jnp.zeros_like(wide_s)
    wide_s[:frames, :mel] = mel_ref[...].astype(FULL)
    wide_s[:frames, mel : mel + 1] = jnp.ones((frames, 1), FULL)
    table_ref[...] = wide_s[...].astype(LOW)


def add_both(left_a, right_a, left_b, right_b, *refs):
    cut = left_a.shape[-1]
    for index, ref in enumerate(refs):
        ref[..., :cut] = add_low(left_a[index], right_a[index])
        ref[..., cut:] = add_low(left_b[index], right_b[index])


def hand_on(from_ref, to_ref):
    to_ref[...] = from_ref[...]


def put_side_by_side(*refs):
    for index, ref in enumerate(refs[:-1]):
        refs[-1][index] = ref[...]


def pack_layers(layers, *refs):
    sources, packs, table_ref = refs[:6], refs[6 : 6 + layers], refs[6 + layers]
    kept, wide_s, sems = refs[7 + layers : 13 + layers], refs[-2], refs[-1]
    copies = [
        pltpu.make_async_copy(source, to, sems.at[index])
        for index, (source, to) in enumerate(zip(sources, kept))
    ]
    for copy in copies:
        copy.start()
    for copy in copies:
        copy.wait()
    conv_ref, cond_ref, conv_b_ref, out_ref, out_b_ref, mel_ref = kept
    mel_rows(mel_ref, table_ref, wide_s)
    rows = conv_ref.shape[1]
    same = lax.broadcasted_iota(jnp.int32, (rows, rows), 0)
    same = (same == lax.broadcasted_iota(jnp.int32, (rows, rows), 1)).astype(FULL).astype(LOW)
    biases = dot_cols(same, jnp.concatenate([conv_b_ref[...], out_b_ref[...]], axis=0))
    early, extra = out_ref.shape[2], out_ref.shape[2] + conv_ref.shape[2]
    mel = cond_ref.shape[2]
    for layer, to_ref in enumerate(packs):
        width = to_ref.shape[1] - extra
        place = lax.broadcasted_iota(jnp.int32, (rows, width), 1)
        cond = jnp.concatenate(
            [cond_ref[layer].astype(FULL), jnp.zeros((rows, width - mel), FULL)], axis=1
        )
        cond = jnp.where(place == mel, biases[:, layer : layer + 1], cond)
        cond = jnp.where(place == mel + 1, biases[:, layers + layer : layers + layer + 1], cond)
        to_ref[:, :early] = out_ref[layer]
        to_ref[:, early:extra] = conv_ref[layer]
        to_ref[:, extra:] = cond.astype(LOW)


def unpack_layers(layers, mel, *refs):
    conv_ref, cond_ref, conv_b_ref, out_ref, out_b_ref = refs[-5:]
    count = (len(refs) - 5) // layers
    rows = conv_ref.shape[1]
    same = lax.broadcasted_iota(jnp.int32, (rows, rows), 0)
    same = (same == lax.broadcasted_iota(jnp.int32, (rows, rows), 1)).astype(FULL)
    early, extra = out_ref.shape[2], out_ref.shape[2] + conv_ref.shape[2]
    for layer in range(layers):
        total = sum(ref[...].astype(FULL) for ref in refs[layer * count : (layer + 1) * count])
        out_ref[layer] = total[:, :early]
        conv_ref[layer] = total[:, early:extra]
        cond_ref[layer] = total[:, extra : extra + mel]
        biases = dot_rows(total[:, extra:], same, precision=lax.Precision.HIGHEST)
        conv_b_ref[layer : layer + 1] = biases[mel : mel + 1]
        out_b_ref[layer : layer + 1] = biases[mel + 1 : mel + 2]


def in_vmem(value):
    return pltpu.with_memory_space_constraint(value, pltpu.VMEM)


def plain(kernel, operands, outs, at_end=False):
    shapes = outs if at_end else [pltpu.VMEM(x.shape, x.dtype) for x in outs]
    return pl.pallas_call(
        kernel,
        out_shape=shapes,
        in_specs=[KEPT] * len(operands),
        out_specs=[KEPT] * len(outs),
        compiler_params=pltpu.CompilerParams(vmem_limit_bytes=ROOM_SMALL * MIB),
    )(*map(in_vmem, operands))


def call(kernel, grid, info, operands, outs, scratch, flops, room, onto=None):
    arrays = [x if spec else in_vmem(x) for x, spec in operands]
    shapes = [x if spec else pltpu.VMEM(x.shape, x.dtype) for x, spec in outs]
    moved = sum(x.size * x.dtype.itemsize for x, spec in (*operands, *outs) if spec)
    return pl.pallas_call(
        kernel,
        grid_spec=pltpu.PrefetchScalarGridSpec(
            num_scalar_prefetch=1,
            grid=(grid,),
            in_specs=[spec or KEPT for _, spec in operands],
            out_specs=[spec or KEPT for _, spec in outs],
            scratch_shapes=scratch,
        ),
        out_shape=shapes,
        input_output_aliases=onto or {},
        compiler_params=pltpu.CompilerParams(
            vmem_limit_bytes=room * MIB, dimension_semantics=("arbitrary",)
        ),
        cost_estimate=pl.CostEstimate(flops=flops // HINT, bytes_accessed=moved // HINT, transcendentals=0),
    )(info, *arrays)


def at_home(value):
    return pltpu.with_memory_space_constraint(value, pltpu.HBM)


def shape_of(*shape, dtype=LOW):
    return jax.ShapeDtypeStruct(shape, dtype)


def tiled(width, place=lambda i: i):
    return pl.BlockSpec((TILE, width), lambda i, info: (place(i), 0))


def fixed(*shape, at=(0, 0)):
    return pl.BlockSpec(shape, lambda i, info: at)


KEPT = pl.BlockSpec(memory_space=pltpu.VMEM)


class Wires:
    def __init__(self, dp, cores, channels):
        self.rest = dp // 4
        assert dp == self.rest * 4 and self.rest & (self.rest - 1) == 0 and cores == 2
        self.devices = dp * 2
        self.rows = channels // self.devices
        self.direct = self.rows % 16 == 0
        self.dp = lax.axis_index(AXES[0])
        self.core = lax.axis_index(AXES[1])
        every = range(self.devices)
        self.sibling = [(i, i ^ 1) for i in every]
        self.first = [(i, i ^ (4 if i % 2 else 2)) for i in every]
        self.second = [(i, i ^ (2 if i % 2 else 4)) for i in every]

    def along_rest(self, distance):
        return [(i, i ^ (8 * distance)) for i in range(self.devices)]

    def hop(self, value, pairs):
        return lax.ppermute(value, AXES, pairs)

    def spread(self, blocks):
        return [blocks[0]] + [
            self.hop(blocks[k], self.along_rest(k)) for k in range(1, self.rest)
        ]

    def passed(self, *pieces):
        pieces = [*pieces, *(self.hop(piece, self.sibling) for piece in pieces)]
        return pieces if self.direct else [self.put_in_order(pieces)]

    def put_in_order(self, pieces):
        whole = jnp.zeros((self.rest, 2, 2, 2) + pieces[0].shape[1:], LOW)
        order = jnp.arange(self.rest) ^ (self.dp >> 2)
        for index, piece in enumerate(pieces):
            source = self.core ^ (index // 4)
            at_a, at_b = turned(self.dp, source, index % 2, (index // 2) % 2)
            whole = lax.dynamic_update_slice(
                whole, piece[order][:, None, None, None], (0, at_b, at_a, source, 0, 0)
            )
        return whole.reshape(-1, pieces[0].shape[2])

    def put_together(self, info_ref, pieces, w_ref):
        if not self.direct:
            w_ref[...] = pieces[0][...]
            return
        dp, core = info_ref[2], info_ref[3]
        for index, piece in enumerate(pieces):
            source = core ^ (index // 4)
            at_a, at_b = turned(dp, source, index % 2, (index // 2) % 2)
            for distance in range(self.rest):
                place = ((((dp >> 2) ^ distance) * 2 + at_b) * 2 + at_a) * 2 + source
                w_ref[rows_of(place, self.rows)] = piece[distance]

    def put_apart(self, info_ref, step, grads, here_ref, away_ref):
        start = 0
        for value in (grad.astype(LOW) for grad in grads):
            columns = slice(start, start + value.shape[1])
            start += value.shape[1]
            if not self.direct:
                here_ref[rows_of(step, value.shape[0]), columns] = value
                continue
            dp, core = info_ref[2], info_ref[3]
            blocks = value.shape[0] // self.rows
            for block in range(0, blocks, 2):
                at_b, at_a = (block // 4) % 2, (block // 2) % 2
                distance = (step * (blocks // 8) + block // 8) ^ (dp >> 2)
                on_a, on_b = at_a ^ (dp & 1), at_b ^ ((dp >> 1) & 1)
                even = value[block * self.rows : (block + 1) * self.rows]
                odd = value[(block + 1) * self.rows : (block + 2) * self.rows]
                first, second = jnp.where(core == 0, on_a, on_b), jnp.where(core == 0, on_b, on_a)
                here_ref[first, second, distance, :, columns] = jnp.where(core == 0, even, odd)
                away_ref[second, first, distance, :, columns] = jnp.where(core == 0, odd, even)

    def apart(self, depth):
        if not self.direct:
            return [(shape_of(self.devices * self.rows, depth), None), (shape_of(16, LANES), None)]
        return [(shape_of(2, 2, self.rest, self.rows, depth), None)] * 2

    def by_distance(self, full):
        rows = full.shape[0] // self.devices
        blocks = full.reshape(self.rest, 2, 2, 2, rows, full.shape[1])
        blocks = blocks[jnp.arange(self.rest) ^ (self.dp >> 2)]
        parts = []
        for away in range(2):
            source = self.core ^ away
            for first in range(2):
                for second in range(2):
                    at_a, at_b = turned(self.dp, source, first, second)
                    parts.append(
                        lax.dynamic_slice(
                            blocks,
                            (0, at_b, at_a, source, 0, 0),
                            (self.rest, 1, 1, 1, rows, full.shape[1]),
                        )[:, 0, 0, 0]
                    )
        return jnp.stack(parts).reshape(2, 2, 2, self.rest, rows, full.shape[1])


def turned(dp, owner, first, second):
    along_a = jnp.where(owner == 0, first, second)
    along_b = jnp.where(owner == 0, second, first)
    return (dp & 1) ^ along_a, ((dp >> 1) & 1) ^ along_b


def add_low(left, right):
    return (left.astype(FULL) + right.astype(FULL)).astype(LOW)


def per_device(
    dp,
    cores,
    samples,
    mel,
    lengths,
    hops,
    conv_weight,
    cond_weight,
    conv_bias,
    out_weight,
    out_bias,
    grad_out,
    grad_skip,
):
    sample_count, channels = samples.shape[1:]
    frame_count, mel_count = mel.shape[1:]
    layers = conv_weight.shape[0]
    size = Sizes(channels, mel_count)
    gate = size.gate
    wires = Wires(dp, cores, gate)
    assert layers == 2 and sample_count % TILE == 0 and TILE == FIRST_DILATION
    steps, wide_steps = sample_count // TILE, sample_count // WIDE
    where = jnp.stack([wires.dp, wires.core]).astype(jnp.int32)
    info = jnp.concatenate([lengths, hops, where])
    x, go, gs = samples[0], grad_out[0], grad_skip[0]
    conv_t, cond_t, out_t = (
        w.swapaxes(1, 2) for w in (conv_weight, cond_weight, out_weight)
    )
    rows = conv_t.shape[1]
    sources = (conv_t, cond_t, conv_bias, out_t, out_bias, mel[0])
    own0, own1, mel_table = pl.pallas_call(
        functools.partial(pack_layers, layers),
        in_specs=[pl.BlockSpec(memory_space=pl.ANY)] * len(sources),
        out_shape=[shape_of(rows, size.pack)] * layers + [shape_of(LANES, size.extra_width)],
        scratch_shapes=[pltpu.VMEM(source.shape, LOW) for source in sources]
        + [pltpu.VMEM((LANES, size.extra_width), FULL), pltpu.SemaphoreType.DMA((len(sources),))],
        compiler_params=pltpu.CompilerParams(vmem_limit_bytes=ROOM_SMALL * MIB),
    )(*map(at_home, sources))
    last_shape = shape_of(wires.rest, rows, size.pack)
    half_shape = shape_of(2, wires.rest, rows, size.pack)
    blocks_shape = [shape_of(rows, size.pack)] * wires.rest
    side_by_side = lambda blocks: plain(put_side_by_side, blocks, [last_shape])[0]
    table = fixed(LANES, size.extra_width)
    macs = sample_count * channels * channels
    assert gate % PART == 0 and gate % PART_0 == 0 and sample_count % WIDE == 0
    kept = lambda *columns: [(shape_of(sample_count, c), None) for c in columns]
    whole_w = (shape_of(gate, size.pack), None)
    parts = gate // PART
    mel_sums = (shape_of(LANES, size.extra_width, dtype=FULL), table)
    frame_sums = (shape_of(gate, LANES, dtype=FULL), None)
    scratch = lambda *shape: pltpu.VMEM(shape, LOW)

    blocked = (shape_of(sample_count, channels), tiled(channels))
    keep = lambda *values: [(value, None) for value in values]

    near0 = wires.spread([own0] * wires.rest)
    taps0, proj1 = call(
        functools.partial(prepare, size),
        steps,
        info,
        [*((at_home(value), tiled(channels)) for value in (x, go, gs)), (mel_table, table)],
        kept(gate + size.extra_width + LANES, gate),
        [],
        macs,
        ROOM_0,
    )
    near0 = near0[::-1]
    *near0, taps0, proj1 = lax.optimization_barrier((*near0, taps0, proj1))
    near0 = near0[::-1]
    mine0 = side_by_side(near0)
    one0, two0 = wires.hop(mine0, wires.first), wires.hop(mine0, wires.second)
    own1, _ = lax.optimization_barrier((own1, mine0))
    (own1,) = plain(hand_on, (own1,), [shape_of(rows, size.pack)])
    near1 = wires.spread([own1] * wires.rest)
    near1 = lax.optimization_barrier(near1[::-1])[::-1]
    mine1 = side_by_side(near1)
    mine1, two0, one0 = lax.optimization_barrier((mine1, two0, one0))
    far0 = wires.hop(one0, wires.second)
    one1, two1 = wires.hop(mine1, wires.first), wires.hop(mine1, wires.second)
    two1, one1, far0 = lax.optimization_barrier((two1, one1, far0))
    pieces0 = wires.passed(mine0, one0, two0, far0)
    taps1, gated0, slope0, w0 = call(
        functools.partial(forward_0, size, wires),
        sample_count // WIDE,
        info,
        keep(taps0, *pieces0),
        [*kept(gate + size.extra_width + LANES, channels, gate), whole_w],
        [pltpu.VMEM((1, channels), FULL), pltpu.VMEM((8, channels), FULL)],
        10 * macs,
        ROOM_0,
    )
    far1 = wires.hop(one1, wires.second)
    taps1, far1 = lax.optimization_barrier((taps1, far1))
    gated1, pre1, w1, sums1, here1, away1 = call(
        functools.partial(layer_1, size, wires, steps),
        steps + parts,
        info,
        keep(taps1, proj1, *wires.passed(mine1, one1, two1, far1)),
        [*kept(channels, gate), whole_w, frame_sums, *wires.apart(size.pack)],
        [],
        24 * macs,
        ROOM_1,
    )
    if not wires.direct:
        here1, away1 = wires.by_distance(here1)
    came1 = wires.hop(away1, wires.sibling)

    carry = (shape_of(8, channels, dtype=FULL), None)
    begun = call(
        functools.partial(backward_0, size, wide_steps - 1),
        wide_steps - wide_steps // 2,
        info,
        keep(pre1, w1, w0, proj1, slope0),
        [*kept(gate, gate), carry],
        [],
        6 * macs,
        ROOM_2,
    )
    stay1, leave1 = plain(add_and_part, (here1, came1), [half_shape] * 2)
    begun, stay1, leave1 = lax.optimization_barrier((begun, stay1, leave1))
    came1 = wires.hop(leave1, wires.first)
    proj0, pre0, _ = call(
        functools.partial(backward_0, size, wide_steps // 2 - 1),
        wide_steps // 2,
        info,
        keep(pre1, w1, w0, proj1, slope0, *begun),
        [*kept(gate, gate), carry],
        [],
        6 * macs,
        ROOM_2,
        {6: 0, 7: 1},
    )

    cut = lambda depth, *lead: shape_of(*lead, wires.rest, rows, depth)
    depths = (size.now, size.pack - size.now)
    here_a, away_a = call(
        functools.partial(weights_0_early, size, wires),
        gate // PART_0,
        info,
        keep(pre0, proj0, taps0, gated0),
        wires.apart(depths[0]),
        [],
        7 * macs,
        ROOM_3,
    )
    sums0, here_b, away_b = call(
        functools.partial(weights_0_now, size, wires),
        gate // PART_0,
        info,
        keep(pre0, proj0, taps0),
        [frame_sums, *wires.apart(depths[1])],
        [],
        5 * macs,
        ROOM_3,
    )
    if not wires.direct:
        here_a, away_a = wires.by_distance(here_a)
        here_b, away_b = wires.by_distance(here_b)
    came_a = wires.hop(away_a, wires.sibling)
    came_a, here_b = lax.optimization_barrier((came_a, here_b))
    away_b, came1 = lax.optimization_barrier((away_b, came1))
    came_b = wires.hop(away_b, wires.sibling)
    stay_a, leave_a = plain(add_and_part, (here_a, came_a), [cut(depths[0], 2)] * 2)
    came_a = wires.hop(leave_a, wires.first)
    stay1, leave_a = lax.optimization_barrier((stay1, leave_a))
    stay1, leave1 = plain(add_and_part, (stay1, came1), [last_shape] * 2)
    came1 = wires.hop(leave1, wires.second)
    came_b, leave1 = lax.optimization_barrier((came_b, leave1))
    stay_b, leave_b = plain(add_and_part, (here_b, came_b), [cut(depths[1], 2)] * 2)
    came_b = wires.hop(leave_b, wires.first)
    pre0, taps1, leave_b = lax.optimization_barrier((pre0, taps1, leave_b))

    (samples_grad,) = call(
        functools.partial(samples_gradient, size),
        steps,
        info,
        keep(proj0, pre0, w0),
        [(shape_of(sample_count, channels, dtype=FULL), tiled(channels))],
        [],
        8 * macs,
        ROOM_4,
    )
    residual_out, skip_output_sum, mel_grad = call(
        functools.partial(forward_outputs, size),
        steps,
        info,
        keep(taps1, gated0, gated1, w0, w1, sums0, sums1),
        [blocked, blocked, mel_sums],
        [pltpu.VMEM((1, gate), FULL)],
        8 * macs,
        ROOM_5,
    )
    came_a, came_b, came1, samples_grad, residual_out = lax.optimization_barrier(
        (came_a, came_b, came1, samples_grad, residual_out)
    )
    parts1 = lax.optimization_barrier(wires.spread(plain(add_and_part, (stay1, came1), blocks_shape))[::-1])[::-1]
    stay0, leave0 = plain(add_both, (stay_a, came_a, stay_b, came_b), [last_shape] * 2)
    came0 = wires.hop(leave0, wires.second)
    parts0 = wires.spread(plain(add_and_part, (stay0, came0), blocks_shape))
    grads = plain(
        functools.partial(unpack_layers, layers, mel_count),
        (*parts0, *parts1),
        [
            shape_of(layers, rows, 2 * channels, dtype=FULL),
            shape_of(layers, rows, mel_count, dtype=FULL),
            shape_of(layers, rows, dtype=FULL),
            shape_of(layers, rows, channels, dtype=FULL),
            shape_of(layers, rows, dtype=FULL),
        ],
        at_end=True,
    )
    conv_grad, cond_grad, conv_b_grad, out_grad, out_b_grad = grads
    return (
        residual_out[None],
        skip_output_sum[None],
        samples_grad[None],
        mel_grad[:frame_count, :mel_count][None],
        conv_grad.swapaxes(1, 2),
        cond_grad.swapaxes(1, 2),
        conv_b_grad,
        out_grad.swapaxes(1, 2),
        out_b_grad,
    )


def solution(mesh):
    dp, cores = mesh.shape["dp"], mesh.shape["group"]

    def everything(*arrays):
        return per_device(dp, cores, *arrays)

    clips = P(AXES, None, None)
    columns = P(None, None, AXES)
    biases = P(None, AXES)
    return jax.shard_map(
        everything,
        mesh=mesh,
        in_specs=(
            clips, clips, P(AXES), P(AXES), columns, columns, biases, columns, biases, clips, clips,
        ),
        out_specs=(clips, clips, clips, clips, columns, columns, biases, columns, biases),
        check_vma=False,
    )
```
